32 devices in a mesh: dp: 4 (over y, x), ctx: 8 (over z, core).
Axes of the slice: x: 2, y: 2, z: 4, core: 2. Of those that a mesh axis runs over, the one named last changes fastest.
Arguments:
- tokens: bfloat16 [1024, 8, 2048], P('ctx', 'dp'), may hold values from -6 to 6
- positions: int32 [1024, 8], P('ctx', 'dp'), may hold values from 0 to 1023, as said below
- attn_norm: bfloat16 [2048], P(('dp', 'ctx')), may hold values from 0.5 to 1.5
- query_proj: bfloat16 [2048, 2048], P(('dp', 'ctx')), may hold values from -0.125 to 0.125
- key_projected: bfloat16 [2048, 1024], P(('dp', 'ctx')), may hold values from -0.125 to 0.125
- value_projected: bfloat16 [2048, 1024], P(('dp', 'ctx')), may hold values from -0.125 to 0.125
- head_norms: bfloat16 [2, 128], replicated, may hold values from 0.5 to 1.5
- out_proj: bfloat16 [2048, 2048], P(('dp', 'ctx')), may hold values from -0.5 to 0.5
- mlp_norm: bfloat16 [2048], P(('dp', 'ctx')), may hold values from 0.5 to 1.5
- gate_proj: bfloat16 [2048, 6144], P(('dp', 'ctx')), may hold values from -0.125 to 0.125
- up_proj: bfloat16 [2048, 6144], P(('dp', 'ctx')), may hold values from -0.125 to 0.125
- down_proj: bfloat16 [2048, 6144], P(('dp', 'ctx')), may hold values from -0.078125 to 0.078125
- out_grad: bfloat16 [1024, 8, 2048], P('ctx', 'dp'), may hold values from -6 to 6
Outputs:
- layer_out: bfloat16 [1024, 8, 2048], P('ctx', 'dp')
- input_grad: float32 [1024, 8, 2048], P('ctx', 'dp')
- attn_norm_grad: float32 [2048], P(('dp', 'ctx'))
- query_grad: float32 [2048, 2048], P(('dp', 'ctx'))
- key_grad: float32 [2048, 1024], P(('dp', 'ctx'))
- value_grad: float32 [2048, 1024], P(('dp', 'ctx'))
- head_norm_grad: float32 [2, 128], replicated
- out_proj_grad: float32 [2048, 2048], P(('dp', 'ctx'))
- mlp_norm_grad: float32 [2048], P(('dp', 'ctx'))
- gate_grad: float32 [2048, 6144], P(('dp', 'ctx'))
- up_grad: float32 [2048, 6144], P(('dp', 'ctx'))
- down_grad: float32 [2048, 6144], P(('dp', 'ctx'))
The draws below stay inside these ranges and needn't reach their ends.
Inputs may be any that keep to these rules, and one draw needn't show every extreme that they name: Each of the 8 sequences is a pack of documents: positions count from 0 at a document's first token and rise by one a token; every sequence begins at position 0; among the 2 sequences of each index of dp one is a single document.
All inputs are finite; a program needn't handle non-finite values.
Results may differ from the reference program's by a relative error of at most 0.017.
Values may be sent and summed in bfloat16 or wider, within the bound.
No kernel may reach another device: no remote copies, remote signals or barrier semaphores. Data moves between devices by JAX's collectives and lax.ppermute only.
A program may use at most 576 MiB of HBM per device.

```python
import jax
import jax.numpy as jnp
from jax import lax

MODEL_DIMENSION = 2048
QUERY_HEADS = 16
KEY_VALUE_HEADS = 8
HEAD_DIMENSION = 128
FF = 6144
SEQS = 2
LEN = 1024
BATCH = 8


def draw_positions(key, part):
    key = jax.random.fold_in(key, 11)
    start_key, pick_key = jax.random.split(key)
    token_index = jnp.arange(LEN, dtype=jnp.int32)
    start_flags = jax.random.randint(start_key, (BATCH, LEN), 0, LEN) < 4
    chosen = jax.random.randint(pick_key, (BATCH // SEQS,), 0, SEQS)
    row_number = jnp.arange(BATCH, dtype=jnp.int32)
    single = row_number % SEQS == jnp.repeat(chosen, SEQS)
    doc_starts = jnp.where(single[:, None], False, start_flags) | (token_index[None, :] == 0)
    doc_begin = lax.cummax(jnp.where(doc_starts, token_index[None, :], 0), axis=1)
    return (token_index[None, :] - doc_begin).T.astype(jnp.int32)


def level_of(rng, shape, cuts, smallest, largest):
    def one(dim, blocks):
        draws = jax.random.uniform(jax.random.fold_in(jax.random.fold_in(rng, 6), dim), (blocks,), jnp.float32, smallest / len(cuts), largest / len(cuts))
        return jnp.repeat(jnp.exp(draws), shape[dim] // blocks).reshape((-1,) + (1,) * (len(shape) - dim - 1))

    gain = one(*cuts[0])
    for cut in cuts[1:]:
        gain = gain * one(*cut)
    return gain


def gaussian(rng, extent, width, reach, shards=(), held_as=jnp.bfloat16):
    values = jax.random.normal(rng, extent, jnp.float32) * width
    if len(shards) > 0:
        values = level_of(rng, extent, shards, -0.22, 0.18) * values
    return jnp.clip(values, min=-reach, max=reach).astype(held_as)


def setup_inputs(seed: int = 0) -> dict:
    splits = jax.random.split(jax.random.key(seed), 14)
    tokens = gaussian(splits[0], (LEN, BATCH, MODEL_DIMENSION), 1.0, 6.0, ((0, 8), (1, 4)))
    positions = draw_positions(jax.random.fold_in(splits[13], 71), 0)
    attn_norm = jnp.clip(1.0 + 0.1 * jax.random.normal(splits[2], (MODEL_DIMENSION,), jnp.float32), 0.5, 1.5).astype(jnp.bfloat16)
    query_proj = gaussian(splits[3], (MODEL_DIMENSION, QUERY_HEADS * HEAD_DIMENSION), MODEL_DIMENSION ** -0.5, 0.125, ((0, 32),))
    key_projected = gaussian(splits[4], (MODEL_DIMENSION, KEY_VALUE_HEADS * HEAD_DIMENSION), MODEL_DIMENSION ** -0.5, 0.125, ((0, 32),))
    value_projected = gaussian(splits[5], (MODEL_DIMENSION, KEY_VALUE_HEADS * HEAD_DIMENSION), MODEL_DIMENSION ** -0.5, 0.125, ((0, 32),))
    head_norms = jnp.clip(1.0 + 0.1 * jax.random.normal(splits[6], (2, HEAD_DIMENSION), jnp.float32), 0.5, 1.5).astype(jnp.bfloat16)
    out_proj = gaussian(splits[7], (MODEL_DIMENSION, QUERY_HEADS * HEAD_DIMENSION), (QUERY_HEADS * HEAD_DIMENSION // 16) ** -0.5, 0.5, ((0, 32),))
    mlp_norm = jnp.clip(1.0 + 0.1 * jax.random.normal(splits[8], (MODEL_DIMENSION,), jnp.float32), 0.5, 1.5).astype(jnp.bfloat16)
    gate_proj = gaussian(splits[9], (MODEL_DIMENSION, FF), MODEL_DIMENSION ** -0.5, 0.125, ((0, 32),))
    up_proj = gaussian(splits[10], (MODEL_DIMENSION, FF), MODEL_DIMENSION ** -0.5, 0.125, ((0, 32),))
    down_proj = gaussian(splits[11], (MODEL_DIMENSION, FF), FF ** -0.5, 0.078125, ((0, 32),))
    out_grad = gaussian(splits[12], (LEN, BATCH, MODEL_DIMENSION), 1.0, 6.0, ((0, 8), (1, 4)))
    return {"tokens": tokens, "positions": positions, "attn_norm": attn_norm, "query_proj": query_proj, "key_projected": key_projected, "value_projected": value_projected, "head_norms": head_norms, "out_proj": out_proj, "mlp_norm": mlp_norm, "gate_proj": gate_proj, "up_proj": up_proj, "down_proj": down_proj, "out_grad": out_grad}


epsilon = 1e-06
theta_base = 1000000.0
top_precision = lax.Precision.HIGHEST

@jax.custom_vjp
def reduced_precision(v):
    return lax.optimization_barrier(v.astype(jnp.bfloat16)).astype(jnp.float32)

@jax.custom_vjp
def reduced_backward(v):
    return v

def low_keep(v):
    return (reduced_precision(v), None)

def low_pass(kept, grad):
    return (grad,)

def back_keep(v):
    return (v, None)

def back_low(kept, grad):
    return (reduced_precision(grad),)
reduced_precision.defvjp(low_keep, low_pass)
reduced_backward.defvjp(back_keep, back_low)

def normalized_rows(matrix):
    return matrix * lax.rsqrt(lax.optimization_barrier(jnp.mean(matrix * matrix, axis=-1, keepdims=True)) + epsilon)

def rotary_tables(places, head_size):
    half_width = head_size // 2
    frequency = theta_base ** (-(jnp.arange(half_width, dtype=jnp.float32) * 2.0 / head_size))
    angles = places.astype(jnp.float32)[..., None] * frequency
    return (jnp.cos(angles), jnp.sin(angles))

def apply_rotary(matrix, cosine_lookup, sine_lookup):
    half_width = matrix.shape[-1] // 2
    first_half = matrix[..., :half_width]
    second_half = matrix[..., half_width:]
    return jnp.concatenate([first_half * cosine_lookup - second_half * sine_lookup, second_half * cosine_lookup + first_half * sine_lookup], axis=-1)

def dot_transposed(operand, matrix):
    return lax.dot_general(operand, matrix, (((1,), (1,)), ((), ())), precision=top_precision)

def layer(inputs, places, attn_gain, query_weight, key_matrix, value_matrix, head_norm_scale, out_weight, mlp_gain, gate_weight, up_weight, down_weight):
    sequence_length, sequence_count, model_width = inputs.shape
    groups_per_head = QUERY_HEADS // KEY_VALUE_HEADS
    flat_rows = inputs.reshape(sequence_length * sequence_count, model_width)
    first_hidden_state = reduced_precision(normalized_rows(flat_rows) * attn_gain)
    query_row_matrix = reduced_backward(jnp.dot(first_hidden_state, query_weight, precision=top_precision)).reshape(sequence_length, sequence_count, QUERY_HEADS, HEAD_DIMENSION)
    key_row_matrix = reduced_backward(jnp.dot(first_hidden_state, key_matrix, precision=top_precision)).reshape(sequence_length, sequence_count, KEY_VALUE_HEADS, HEAD_DIMENSION)
    value_rows = reduced_precision(reduced_backward(jnp.dot(first_hidden_state, value_matrix, precision=top_precision))).reshape(sequence_length, sequence_count, KEY_VALUE_HEADS, HEAD_DIMENSION)
    cosine_lookup, sine_lookup = rotary_tables(places, HEAD_DIMENSION)
    cosine_lookup = cosine_lookup[:, :, None]
    sine_lookup = sine_lookup[:, :, None]
    query_row_matrix = reduced_precision(apply_rotary(normalized_rows(query_row_matrix) * head_norm_scale[0], cosine_lookup, sine_lookup)).reshape(sequence_length, sequence_count, KEY_VALUE_HEADS, groups_per_head, HEAD_DIMENSION)
    key_row_matrix = reduced_precision(apply_rotary(normalized_rows(key_row_matrix) * head_norm_scale[1], cosine_lookup, sine_lookup))
    scores = reduced_backward(jnp.einsum('tsgre,usge->sgrtu', query_row_matrix, key_row_matrix, precision=top_precision) * HEAD_DIMENSION ** (-0.5))
    token_index = jnp.arange(sequence_length)
    earliest = (token_index[:, None] - places).T
    allowed = (token_index[None, None, :] >= earliest[:, :, None]) & (token_index[None, None, :] <= token_index[None, :, None])
    masked = jnp.where(allowed[:, None, None], scores, -1e+30)
    shifted = jnp.exp(masked - lax.optimization_barrier(jnp.max(masked, axis=-1, keepdims=True)))
    prob_low = reduced_precision(shifted / lax.optimization_barrier(jnp.sum(shifted, axis=-1, keepdims=True)))
    attn_mix = jnp.einsum('sgrtu,usge->tsgre', prob_low, value_rows, precision=top_precision)
    attn_mix = reduced_precision(reduced_backward(attn_mix.reshape(sequence_length * sequence_count, QUERY_HEADS * HEAD_DIMENSION)))
    middle = flat_rows + reduced_backward(dot_transposed(attn_mix, out_weight))
    hidden_two = reduced_precision(normalized_rows(middle) * mlp_gain)
    gate_pre = reduced_backward(jnp.dot(hidden_two, gate_weight, precision=top_precision))
    up_pre = reduced_backward(jnp.dot(hidden_two, up_weight, precision=top_precision))
    hidden_low = reduced_precision(gate_pre * jax.nn.sigmoid(gate_pre) * up_pre)
    result = middle + reduced_backward(dot_transposed(hidden_low, down_weight))
    return result.reshape(sequence_length, sequence_count, model_width)

def reference(tokens, positions, attn_norm, query_proj, key_projected, value_projected, head_norms, out_proj, mlp_norm, gate_proj, up_proj, down_proj, out_grad):
    weights = tuple((weight_arg.astype(jnp.float32) for weight_arg in (attn_norm, query_proj, key_projected, value_projected, head_norms, out_proj, mlp_norm, gate_proj, up_proj, down_proj)))
    group_count = BATCH // SEQS

    def split_groups(stacked):
        return jnp.moveaxis(stacked.reshape((LEN, group_count, SEQS) + stacked.shape[2:]), 1, 0)

    def join_groups(stacked):
        return jnp.moveaxis(stacked, 0, 1).reshape((LEN, BATCH) + stacked.shape[3:])
    inputs = split_groups(tokens.astype(jnp.float32))
    places = split_groups(positions)
    cotangent = split_groups(out_grad.astype(jnp.float32))

    def group_step(totals, pieces):
        group_in, group_places, group_cot = pieces

        def forward(*operands):
            return layer(operands[0], group_places, *operands[1:])
        outputs, pullback = jax.vjp(forward, group_in, *weights)
        gradients = pullback(group_cot)
        totals = tuple((running + gradient for running, gradient in zip(totals, gradients[1:])))
        return (totals, (outputs, gradients[0]))
    zero_sums = tuple((jnp.zeros_like(weight_arg) for weight_arg in weights))
    totals, (outputs, input_grads) = lax.scan(group_step, zero_sums, (inputs, places, cotangent))
    return (join_groups(outputs).astype(jnp.bfloat16), join_groups(input_grads), totals[0], totals[1], totals[2], totals[3], totals[4], totals[5], totals[6], totals[7], totals[8], totals[9])
```

```python
import functools

import jax
import jax.numpy as jnp
from jax import lax
from jax.experimental import pallas as pl
from jax.experimental.pallas import tpu as pltpu
from jax.sharding import Mesh
from jax.sharding import PartitionSpec as P

QUERY_HEADS = 16
KEY_VALUE_HEADS = 8
HEAD_DIMENSION = 128
GROUP = QUERY_HEADS // KEY_VALUE_HEADS
HEAD_SET = (GROUP + 2) * HEAD_DIMENSION

epsilon = 1e-06
theta_base = 1000000.0
score_scaling = HEAD_DIMENSION ** (-0.5)
F32 = jnp.float32
BF16 = jnp.bfloat16


def norm_factor(matrix):
    return lax.rsqrt(jnp.mean(matrix * matrix, axis=-1, keepdims=True) + epsilon)


def norm_back(matrix, factor, upstream):
    return factor * upstream - matrix * (factor * factor * factor) * jnp.mean(
        upstream * matrix, axis=-1, keepdims=True
    )


def dot(a, b, ca=1, cb=0):
    return lax.dot_general(a, b, (((ca,), (cb,)), ((), ())), preferred_element_type=F32)


def rotate(x, cos, sin):
    return x * cos + pltpu.roll(x, HEAD_DIMENSION // 2, 1) * sin


def head_slice(i):
    return slice(i * HEAD_DIMENSION, (i + 1) * HEAD_DIMENSION)


def normed_rotated(raw, gain, cos, sin):
    return rotate(raw * norm_factor(raw) * gain, cos, sin).astype(BF16)


def probabilities(keys, queries, first_query, earliest):
    scores = dot(keys, queries, 1, 1) * score_scaling
    key_index = lax.broadcasted_iota(jnp.int32, scores.shape, 0)
    query_index = lax.broadcasted_iota(jnp.int32, scores.shape, 1) + first_query
    allowed = (key_index <= query_index) & (key_index >= earliest)
    masked = jnp.where(allowed, scores, -1e30)
    shifted = jnp.exp(masked - jnp.max(masked, axis=0, keepdims=True))
    return shifted * (1.0 / jnp.sum(shifted, axis=0, keepdims=True))


def forward_kernel(block, qkv_ref, gain_ref, cos_ref, sin_ref, early_ref, out_ref):
    length = qkv_ref.shape[0]
    gains = gain_ref[...]
    cos, sin = cos_ref[...], sin_ref[...]
    keys = normed_rotated(qkv_ref[:, head_slice(GROUP)], gains[1:2], cos, sin)
    values_t = qkv_ref[:, head_slice(GROUP + 1)].T.astype(BF16)
    for i in range(length // block):
        rows = slice(i * block, (i + 1) * block)
        seen = (i + 1) * block
        for g in range(GROUP):
            queries = normed_rotated(qkv_ref[rows, head_slice(g)], gains[0:1], cos[rows], sin[rows])
            probs = probabilities(keys[:seen], queries, i * block, early_ref[0:1, rows]).astype(BF16)
            mixed = dot(values_t[:, :seen], probs)
            out_ref[rows, head_slice(g)] = mixed.T.astype(BF16)


def backward_kernel(
    block, qkv_ref, dout_ref, gain_ref, cos_ref, sin_ref, early_ref, dqkv_ref, dgain_ref, dkey_ref, dvalue_ref
):
    length = qkv_ref.shape[0]
    gains = gain_ref[...]
    cos, sin = cos_ref[...], sin_ref[...]
    key_raw = qkv_ref[:, head_slice(GROUP)]
    keys = normed_rotated(key_raw, gains[1:2], cos, sin)
    keys_t = keys.astype(F32).T.astype(BF16)
    values = qkv_ref[:, head_slice(GROUP + 1)].astype(BF16)
    dkey_ref[...] = jnp.zeros_like(dkey_ref)
    dvalue_ref[...] = jnp.zeros_like(dvalue_ref)
    query_gain_sum = jnp.zeros((1, HEAD_DIMENSION), F32)
    for i in range(length // block):
        rows = slice(i * block, (i + 1) * block)
        seen = (i + 1) * block
        for g in range(GROUP):
            query_raw = qkv_ref[rows, head_slice(g)]
            queries = normed_rotated(query_raw, gains[0:1], cos[rows], sin[rows])
            dout = dout_ref[rows, head_slice(g)]
            probs = probabilities(keys[:seen], queries, i * block, early_ref[0:1, rows])
            dprobs = dot(values[:seen], dout, 1, 1)
            delta = jnp.sum(probs * dprobs, axis=0, keepdims=True)
            dscores = (probs * (dprobs - delta)).astype(BF16)
            dkey_ref[:seen] += dot(dscores, queries)
            dvalue_ref[:seen] += dot(probs.astype(BF16), dout)
            dquery = dot(keys_t[:, :seen], dscores).T * score_scaling
            dquery = rotate(dquery, cos[rows], -sin[rows])
            factor = norm_factor(query_raw)
            query_gain_sum += jnp.sum(query_raw * factor * dquery, axis=0, keepdims=True)
            dqkv_ref[rows, head_slice(g)] = norm_back(query_raw, factor, dquery * gains[0:1]).astype(BF16)
    dkey = rotate(dkey_ref[...] * score_scaling, cos, -sin)
    factor = norm_factor(key_raw)
    dgain_ref[0, 0:1, :] = query_gain_sum
    dgain_ref[0, 1:2, :] = jnp.sum(key_raw * factor * dkey, axis=0, keepdims=True)
    dgain_ref[0, 2:, :] = jnp.zeros((6, HEAD_DIMENSION), F32)
    dqkv_ref[:, head_slice(GROUP)] = norm_back(key_raw, factor, dkey * gains[1:2]).astype(BF16)
    dqkv_ref[:, head_slice(GROUP + 1)] = dvalue_ref[...].astype(BF16)


def per_head_specs(length):
    whole = lambda shape: pl.BlockSpec(shape, lambda n: (0,) * len(shape))
    return [
        whole((2, HEAD_DIMENSION)),
        whole((length, HEAD_DIMENSION)),
        whole((length, HEAD_DIMENSION)),
        whole((8, length)),
    ]


def columns_spec(length, width):
    return pl.BlockSpec((length, width), lambda n: (0, n))


def attention_forward(qkv, gains, cos, sin, earliest):
    length, width = qkv.shape
    heads = width // HEAD_SET
    return pl.pallas_call(
        functools.partial(forward_kernel, 256),
        grid=(heads,),
        in_specs=[columns_spec(length, HEAD_SET)] + per_head_specs(length),
        out_specs=columns_spec(length, GROUP * HEAD_DIMENSION),
        out_shape=jax.ShapeDtypeStruct((length, heads * GROUP * HEAD_DIMENSION), BF16),
        compiler_params=pltpu.CompilerParams(vmem_limit_bytes=48 << 20),
        cost_estimate=pl.CostEstimate(
            flops=heads * GROUP * 2 * length * length * HEAD_DIMENSION * 2,
            bytes_accessed=length * width * 6,
            transcendentals=heads * GROUP * length * length // 2,
        ),
    )(qkv, gains, cos, sin, earliest)


def attention_backward(qkv, dout, gains, cos, sin, earliest):
    length, width = qkv.shape
    heads = width // HEAD_SET
    return pl.pallas_call(
        functools.partial(backward_kernel, 256),
        grid=(heads,),
        in_specs=[columns_spec(length, HEAD_SET), columns_spec(length, GROUP * HEAD_DIMENSION)]
        + per_head_specs(length),
        out_specs=[
            columns_spec(length, HEAD_SET),
            pl.BlockSpec((1, 8, HEAD_DIMENSION), lambda n: (n, 0, 0)),
        ],
        out_shape=[
            jax.ShapeDtypeStruct((length, width), BF16),
            jax.ShapeDtypeStruct((heads, 8, HEAD_DIMENSION), F32),
        ],
        scratch_shapes=[pltpu.VMEM((length, HEAD_DIMENSION), F32)] * 2,
        compiler_params=pltpu.CompilerParams(vmem_limit_bytes=48 << 20),
        cost_estimate=pl.CostEstimate(
            flops=heads * GROUP * 2 * length * length * HEAD_DIMENSION * 5,
            bytes_accessed=length * width * 8,
            transcendentals=heads * GROUP * length * length // 2,
        ),
    )(qkv, dout, gains, cos, sin, earliest)


def per_device(
    tokens,
    positions,
    attn_norm,
    query_proj,
    key_projected,
    value_projected,
    head_norms,
    out_proj,
    mlp_norm,
    gate_proj,
    up_proj,
    down_proj,
    out_grad,
):
    block, seqs, width = tokens.shape
    rows = block * seqs
    dp = lax.axis_size("dp")
    parts = lax.axis_size("t")
    ctx = 2 * parts
    length = block * ctx
    depth = query_proj.shape[0]
    half = lax.axis_index("h")
    part = lax.axis_index("t")
    everywhere = ("dp", "h", "t")

    def to_sequence(blocks):
        keep = lax.dynamic_index_in_dim(blocks, half, 1, keepdims=False)
        give = lax.dynamic_index_in_dim(blocks, 1 - half, 1, keepdims=False)
        got = lax.ppermute(give, "h", [(0, 1), (1, 0)])
        pair = jnp.where(half == 0, jnp.stack([keep, got]), jnp.stack([got, keep]))
        return lax.all_gather(pair, "t", axis=1, tiled=True).reshape(length, width)

    def to_blocks(partial):
        pair = lax.psum_scatter(
            partial.astype(BF16).reshape(2, length // 2, width), "t", scatter_dimension=1, tiled=True
        )
        keep = lax.dynamic_index_in_dim(pair, half, 0, keepdims=False)
        give = lax.dynamic_index_in_dim(pair, 1 - half, 0, keepdims=False)
        got = lax.ppermute(give, "h", [(0, 1), (1, 0)])
        return jnp.where(half == 0, jnp.stack([keep, got], 1), jnp.stack([got, keep], 1)).reshape(rows, width)

    def gather_dp(x):
        return lax.all_gather(x, "dp", axis=0, tiled=True)

    def scatter_dp(x):
        return lax.psum_scatter(x.astype(BF16), "dp", scatter_dimension=0, tiled=True)

    small = jnp.concatenate(
        [
            attn_norm.astype(F32),
            mlp_norm.astype(F32),
            positions.T.reshape(-1).astype(F32),
        ]
    )
    small_all = lax.all_gather(small, everywhere, axis=0, tiled=False)
    attn_gain = small_all[:, :depth].reshape(1, width)
    mlp_gain = small_all[:, depth : 2 * depth].reshape(1, width)
    own_places = lax.dynamic_slice_in_dim(
        small_all[:, 2 * depth :].reshape(dp, ctx, seqs, block), lax.axis_index("dp"), 1, 0
    )[0]
    places = lax.dynamic_index_in_dim(own_places, half, 1, keepdims=False).reshape(length)

    heads = KEY_VALUE_HEADS // parts
    qkv_set = jnp.concatenate(
        [
            query_proj.reshape(depth, KEY_VALUE_HEADS, GROUP * HEAD_DIMENSION),
            key_projected.reshape(depth, KEY_VALUE_HEADS, HEAD_DIMENSION),
            value_projected.reshape(depth, KEY_VALUE_HEADS, HEAD_DIMENSION),
        ],
        axis=2,
    ).reshape(depth, parts, heads * HEAD_SET)
    mix_width = heads * GROUP * HEAD_DIMENSION
    attn_set = jnp.concatenate([qkv_set, out_proj.reshape(depth, parts, mix_width)], axis=2)
    attn_set = lax.all_to_all(jnp.transpose(attn_set, (1, 0, 2)), "t", 0, 0, tiled=True)
    attn_set = attn_set.reshape(parts * depth, heads * HEAD_SET + mix_width)
    qkv_weight = lax.all_gather(attn_set[:, : heads * HEAD_SET], ("dp", "h"), axis=0, tiled=True)
    out_weight = lax.all_gather(attn_set[:, heads * HEAD_SET :], ("dp", "h"), axis=0, tiled=True)

    hidden = gate_proj.shape[1] // dp

    def ffn_columns(w):
        w = jnp.transpose(w.reshape(depth, dp, hidden), (1, 0, 2))
        w = lax.all_to_all(w, "dp", 0, 0, tiled=True)
        return lax.all_gather(w, ("h", "t"), axis=1, tiled=True).reshape(width, hidden)

    def ffn_owner(g):
        g = lax.psum_scatter(
            g.astype(BF16).reshape(dp, ctx * depth, hidden), ("h", "t"), scatter_dimension=1, tiled=True
        )
        g = lax.all_to_all(g, "dp", 0, 0, tiled=True)
        return jnp.transpose(g, (1, 0, 2)).reshape(depth, dp * hidden).astype(F32)

    sequence = to_sequence(tokens).astype(F32)
    gate_weight, up_weight, down_weight = ffn_columns(gate_proj), ffn_columns(up_proj), ffn_columns(down_proj)
    grad_own = out_grad.reshape(rows, width)
    grad_rows = gather_dp(grad_own)

    gains = head_norms.astype(F32)
    half_width = HEAD_DIMENSION // 2
    frequency = theta_base ** (-(jnp.arange(half_width, dtype=F32) * 2.0 / HEAD_DIMENSION))
    angles = places[:, None] * frequency
    cos, sin = jnp.cos(angles), jnp.sin(angles)
    cos = jnp.concatenate([cos, cos], axis=1)
    sin = jnp.concatenate([-sin, sin], axis=1)
    earliest = jnp.broadcast_to(
        (jnp.arange(length, dtype=jnp.int32) - places.astype(jnp.int32))[None, :], (8, length)
    )
    seq_factor = norm_factor(sequence)
    hidden_one = (sequence * seq_factor * attn_gain).astype(BF16)
    qkv = dot(hidden_one, qkv_weight)
    mixed = attention_forward(qkv, gains, cos, sin, earliest)
    inputs = tokens.astype(F32).reshape(rows, width)
    middle = inputs + to_blocks(dot(mixed, out_weight, 1, 1)).astype(F32)

    factor_two = norm_factor(middle)
    hidden_two = gather_dp((middle * factor_two * mlp_gain).astype(BF16))
    gate_pre = dot(hidden_two, gate_weight)
    up_pre = dot(hidden_two, up_weight)
    gate_sig = jax.nn.sigmoid(gate_pre)
    gate_act = gate_pre * gate_sig
    hidden_low = (gate_act * up_pre).astype(BF16)
    grad_hidden = dot(grad_rows, down_weight)
    grad_gate = (grad_hidden * up_pre * gate_sig * (1.0 + gate_pre * (1.0 - gate_sig))).astype(BF16)
    grad_up = (grad_hidden * gate_act).astype(BF16)
    grad_two = scatter_dp(dot(grad_gate, gate_weight, 1, 1) + dot(grad_up, up_weight, 1, 1)).astype(F32)
    branch = scatter_dp(dot(hidden_low, down_weight, 1, 1)).astype(F32)
    layer_out = (middle + branch).astype(BF16).reshape(block, seqs, width)
    down_grad = ffn_owner(dot(grad_rows, hidden_low, 0, 0))
    gate_grad = ffn_owner(dot(hidden_two, grad_gate, 0, 0))
    up_grad = ffn_owner(dot(hidden_two, grad_up, 0, 0))

    mlp_norm_sum = jnp.sum(middle * factor_two * grad_two, axis=0, keepdims=True)
    grad_middle = grad_own.astype(F32) + norm_back(middle, factor_two, grad_two * mlp_gain)

    grad_mid = to_sequence(grad_middle.astype(BF16).reshape(block, seqs, width))
    grad_mixed = dot(grad_mid, out_weight).astype(BF16)
    out_term = dot(grad_mid, mixed, 0, 0)
    grad_qkv, gain_terms = attention_backward(qkv, grad_mixed, gains, cos, sin, earliest)
    qkv_term = dot(hidden_one, grad_qkv, 0, 0)
    grad_one_part = dot(grad_qkv, qkv_weight, 1, 1)
    attn_norm_sum = jnp.sum(sequence * seq_factor * grad_one_part, axis=0, keepdims=True)
    grad_one = to_blocks(grad_one_part).astype(F32)

    sums = jnp.concatenate(
        [attn_norm_sum, mlp_norm_sum, jnp.sum(gain_terms, axis=0)[:2].reshape(1, -1)], axis=1
    )
    sums = lax.psum(sums, everywhere)[0]
    owner = (lax.axis_index("dp") * ctx + half * parts + part) * depth
    attn_norm_grad = lax.dynamic_slice_in_dim(sums, owner, depth)
    mlp_norm_grad = lax.dynamic_slice_in_dim(sums, width + owner, depth)
    head_norm_grad = sums[2 * width :].reshape(2, HEAD_DIMENSION)

    attn_terms = jnp.concatenate([qkv_term.astype(BF16), out_term.astype(BF16)], axis=1)
    attn_terms = lax.psum_scatter(attn_terms, ("dp", "h"), scatter_dimension=0, tiled=True)
    attn_terms = lax.all_to_all(attn_terms.reshape(parts, depth, -1), "t", 0, 0, tiled=True)
    attn_terms = jnp.transpose(attn_terms, (1, 0, 2)).astype(F32)
    qkv_grad = attn_terms[:, :, : heads * HEAD_SET].reshape(depth, KEY_VALUE_HEADS, HEAD_SET)
    split = GROUP * HEAD_DIMENSION
    query_grad = qkv_grad[:, :, :split].reshape(depth, -1)
    key_grad = qkv_grad[:, :, split : split + HEAD_DIMENSION].reshape(depth, -1)
    value_grad = qkv_grad[:, :, split + HEAD_DIMENSION :].reshape(depth, -1)
    out_proj_grad = attn_terms[:, :, heads * HEAD_SET :].reshape(depth, -1)

    input_grad = (grad_middle + norm_back(inputs, norm_factor(inputs), grad_one * attn_gain)).reshape(
        block, seqs, width
    )
    return (
        layer_out,
        input_grad,
        attn_norm_grad,
        query_grad,
        key_grad,
        value_grad,
        head_norm_grad,
        out_proj_grad,
        mlp_norm_grad,
        gate_grad,
        up_grad,
        down_grad,
    )


def solution(mesh):
    dp, ctx = mesh.shape["dp"], mesh.shape["ctx"]
    fine = Mesh(mesh.devices.reshape(dp, 2, ctx // 2), ("dp", "h", "t"))
    acts = P(("h", "t"), "dp", None)
    rows = P(("dp", "h", "t"), None)
    gain = P(("dp", "h", "t"))
    in_specs = (
        acts,
        P(("h", "t"), "dp"),
        gain,
        rows,
        rows,
        rows,
        P(),
        rows,
        gain,
        rows,
        rows,
        rows,
        acts,
    )
    out_specs = (acts, acts, gain, rows, rows, rows, P(), rows, gain, rows, rows, rows)
    return jax.shard_map(per_device, mesh=fine, in_specs=in_specs, out_specs=out_specs, check_vma=False)
```

```python
import functools

import jax
import jax.numpy as jnp
from jax import lax
from jax.experimental import pallas as pl
from jax.experimental.pallas import tpu as pltpu
from jax.sharding import Mesh
from jax.sharding import PartitionSpec as P

QUERY_HEADS = 16
KEY_VALUE_HEADS = 8
HEAD_DIMENSION = 128
GROUP = QUERY_HEADS // KEY_VALUE_HEADS
HEAD_SET = (GROUP + 2) * HEAD_DIMENSION

epsilon = 1e-06
theta_base = 1000000.0
score_scaling = HEAD_DIMENSION ** (-0.5)
F32 = jnp.float32
BF16 = jnp.bfloat16


def norm_factor(matrix):
    return lax.rsqrt(jnp.mean(matrix * matrix, axis=-1, keepdims=True) + epsilon)


def norm_back(matrix, factor, upstream):
    return factor * upstream - matrix * (factor * factor * factor) * jnp.mean(
        upstream * matrix, axis=-1, keepdims=True
    )


def dot(a, b, ca=1, cb=0):
    return lax.dot_general(a, b, (((ca,), (cb,)), ((), ())), preferred_element_type=F32)


F_AFTER_W = True
PRE_LATE = True
CHEAP = pl.CostEstimate(flops=1 << 20, bytes_accessed=1 << 16, transcendentals=0)


def rows_kernel(contract, a_ref, b_ref, *out_refs):
    out = dot(a_ref[...], b_ref[...], 1, contract).astype(out_refs[0].dtype)
    step = out_refs[0].shape[0]
    for k, out_ref in enumerate(out_refs):
        out_ref[...] = out[k * step : (k + 1) * step]


def rows_product(a, b, contract, tile, dtype, pieces=1):
    rows, depth = a.shape
    columns = b.shape[1 - contract]
    tile = min(tile, columns)
    out = pl.pallas_call(
        functools.partial(rows_kernel, contract),
        grid=(columns // tile,),
        in_specs=[
            pl.BlockSpec((rows, depth), lambda j: (0, 0)),
            pl.BlockSpec((depth, tile), lambda j: (0, j))
            if contract == 0
            else pl.BlockSpec((tile, depth), lambda j: (j, 0)),
        ],
        out_specs=[pl.BlockSpec((rows // pieces, tile), lambda j: (0, j))] * pieces,
        out_shape=[jax.ShapeDtypeStruct((rows // pieces, columns), dtype)] * pieces,
        compiler_params=pltpu.CompilerParams(vmem_limit_bytes=48 << 20),
        cost_estimate=CHEAP,
    )(a, b)
    return out if pieces > 1 else out[0]


def term_kernel(a_ref, b_ref, out_ref):
    out_ref[...] = dot(a_ref[...], b_ref[...], 0, 0).astype(BF16).reshape(out_ref.shape)


def term_product(a, b, groups, blocks):
    rows, width = a.shape
    columns = b.shape[1]
    depth = width // (groups * blocks)
    return pl.pallas_call(
        term_kernel,
        grid=(groups,),
        in_specs=[
            pl.BlockSpec((rows, blocks * depth), lambda i: (0, i)),
            pl.BlockSpec((rows, columns), lambda i: (0, 0)),
        ],
        out_specs=pl.BlockSpec((blocks, 1, depth, columns), lambda i: (0, i, 0, 0)),
        out_shape=jax.ShapeDtypeStruct((blocks, groups, depth, columns), BF16),
        compiler_params=pltpu.CompilerParams(vmem_limit_bytes=56 << 20),
        cost_estimate=CHEAP,
    )(a, b).reshape(width, columns)


def pieces_kernel(me_ref, a_ref, b_ref, *refs):
    norm_ref, out_refs = (refs[0], refs[1:]) if refs[0].shape[0] == 8 else (None, refs)
    wide = b_ref.shape[1]
    part = dot(a_ref[...], b_ref[...], 0, 0).astype(BF16)
    for s, out_ref in enumerate(out_refs):

        @pl.when(pl.program_id(0) == s)
        def _():
            out_ref[:, :wide] = part
            if norm_ref is not None:
                sums = norm_ref[...].T
                rest = jnp.zeros((sums.shape[0], HEAD_DIMENSION - 8), F32)
                out_ref[:, wide:] = jnp.concatenate([sums, rest], axis=1).astype(BF16)


def term_pieces(a, b, me, count, norms=None):
    rows, width = a.shape
    columns = b.shape[1]
    step = width // count
    extra = 0 if norms is None else HEAD_DIMENSION
    in_specs = [
        pl.BlockSpec((rows, step), lambda i, me: (0, me[0] ^ i)),
        pl.BlockSpec((rows, columns), lambda i, me: (0, 0)),
    ]
    if norms is not None:
        in_specs.append(pl.BlockSpec((8, step), lambda i, me: (0, me[0] ^ i)))
    return pl.pallas_call(
        pieces_kernel,
        grid_spec=pltpu.PrefetchScalarGridSpec(
            num_scalar_prefetch=1,
            grid=(count,),
            in_specs=in_specs,
            out_specs=[pl.BlockSpec((step, columns + extra), lambda i, me: (0, 0))] * count,
        ),
        out_shape=[jax.ShapeDtypeStruct((step, columns + extra), BF16)] * count,
        compiler_params=pltpu.CompilerParams(vmem_limit_bytes=56 << 20),
        cost_estimate=CHEAP,
    )(me.reshape(1).astype(jnp.int32), a, b, *([] if norms is None else [norms]))


def input_kernel(grad_ref, weight_ref, normed_ref, other_ref, out_ref, sum_ref):
    part = dot(grad_ref[...], weight_ref[...], 1, 1)
    out_ref[...] = part.astype(BF16)
    sum_ref[...] = jnp.zeros_like(sum_ref)
    sum_ref[0:1] = jnp.sum(normed_ref[...].astype(F32) * part, axis=0, keepdims=True)
    sum_ref[1:2] = other_ref[...]


def input_product(grad, weight, normed, other, tile):
    rows, depth = grad.shape
    columns = weight.shape[0]
    return pl.pallas_call(
        input_kernel,
        grid=(columns // tile,),
        in_specs=[
            pl.BlockSpec((rows, depth), lambda j: (0, 0)),
            pl.BlockSpec((tile, depth), lambda j: (j, 0)),
            pl.BlockSpec((rows, tile), lambda j: (0, j)),
            pl.BlockSpec((1, tile), lambda j: (0, j)),
        ],
        out_specs=[pl.BlockSpec((rows, tile), lambda j: (0, j)), pl.BlockSpec((8, tile), lambda j: (0, j))],
        out_shape=[jax.ShapeDtypeStruct((rows, columns), BF16), jax.ShapeDtypeStruct((8, columns), F32)],
        compiler_params=pltpu.CompilerParams(vmem_limit_bytes=48 << 20),
        cost_estimate=CHEAP,
    )(grad, weight, normed, other)


def whole(kernel, shapes, me, *arrays):
    vmem = pl.BlockSpec(memory_space=pltpu.VMEM)
    return pl.pallas_call(
        kernel,
        in_specs=[pl.BlockSpec(memory_space=pltpu.SMEM)] + [vmem] * len(arrays),
        out_specs=[vmem] * len(shapes),
        out_shape=shapes,
        compiler_params=pltpu.CompilerParams(vmem_limit_bytes=48 << 20),
        cost_estimate=CHEAP,
    )(me.reshape(1).astype(jnp.int32), *arrays)


def lanes(index, size):
    return pl.ds(pl.multiple_of(index * size, HEAD_DIMENSION), size)


def attn_split_kernel(heads, me_ref, gain_ref, q_ref, k_ref, v_ref, o_ref, *out_refs):
    pair = GROUP * HEAD_DIMENSION
    gain = gain_ref[...]

    def scaled(ref, index, size):
        return (ref[:, lanes(index, size)].astype(F32) * gain).astype(BF16)

    for s, out_ref in enumerate(out_refs):
        part = me_ref[0] ^ s
        for n in range(heads):
            head, at = part * heads + n, n * HEAD_SET
            out_ref[:, at : at + pair] = scaled(q_ref, head, pair)
            out_ref[:, at + pair : at + pair + HEAD_DIMENSION] = scaled(k_ref, head, HEAD_DIMENSION)
            out_ref[:, at + pair + HEAD_DIMENSION : at + HEAD_SET] = scaled(v_ref, head, HEAD_DIMENSION)
        out_ref[:, heads * HEAD_SET :] = o_ref[:, lanes(part, heads * pair)]


def attn_join_kernel(heads, me_ref, gain_ref, *refs):
    count = len(refs) - 5
    q_ref, k_ref, v_ref, o_ref, norm_ref = refs[count:]
    pair = GROUP * HEAD_DIMENSION
    gain = gain_ref[...]
    norms = jnp.zeros(norm_ref.shape, F32)
    for s, got_ref in enumerate(refs[:count]):
        part = me_ref[0] ^ s
        for n in range(heads):
            head, at = part * heads + n, n * HEAD_SET
            q_ref[:, lanes(head, pair)] = got_ref[:, at : at + pair].astype(F32) * gain
            k_ref[:, lanes(head, HEAD_DIMENSION)] = (
                got_ref[:, at + pair : at + pair + HEAD_DIMENSION].astype(F32) * gain
            )
            v_ref[:, lanes(head, HEAD_DIMENSION)] = (
                got_ref[:, at + pair + HEAD_DIMENSION : at + HEAD_SET].astype(F32) * gain
            )
        norms += got_ref[:, heads * HEAD_SET : heads * HEAD_SET + HEAD_DIMENSION].astype(F32)
        o_ref[:, lanes(part, heads * pair)] = got_ref[:, heads * HEAD_SET + HEAD_DIMENSION :].astype(F32)
    norm_ref[...] = norms


def ffn_split_kernel(tiles, me_ref, gain_ref, gate_ref, up_ref, down_ref, *out_refs):
    gain = gain_ref[...]
    hidden = out_refs[0].shape[1] // 3
    tile = hidden // tiles
    for s, out_ref in enumerate(out_refs):
        part = me_ref[0] ^ s
        for n in range(tiles):
            for k, ref in enumerate((gate_ref, up_ref)):
                at = (2 * n + k) * tile
                out_ref[:, at : at + tile] = (ref[:, lanes(part * tiles + n, tile)].astype(F32) * gain).astype(
                    BF16
                )
        out_ref[:, 2 * hidden :] = down_ref[:, lanes(part, hidden)]


def ffn_join_kernel(tiles, me_ref, gain_ref, *refs):
    count = len(refs) - 3
    gate_ref, up_ref, down_ref = refs[count:]
    gain = gain_ref[...]
    hidden = refs[0].shape[1] // 3
    tile = hidden // tiles
    for s, got_ref in enumerate(refs[:count]):
        part = me_ref[0] ^ s
        for n in range(tiles):
            for k, ref in enumerate((gate_ref, up_ref)):
                at = (2 * n + k) * tile
                ref[:, lanes(part * tiles + n, tile)] = got_ref[:, at : at + tile].astype(F32) * gain
        down_ref[:, lanes(part, hidden)] = got_ref[:, 2 * hidden :].astype(F32)


def rows_join_kernel(me_ref, *refs):
    first_ref, second_ref = refs[-2:]
    depth = refs[0].shape[0]
    wide = first_ref.shape[1]
    for s, got_ref in enumerate(refs[:-2]):
        rows = pl.ds(pl.multiple_of((me_ref[0] ^ s) * depth, depth), depth)
        first_ref[rows] = got_ref[:, :wide]
        second_ref[rows] = got_ref[:, wide:]


def rows_join(got, wide, me):
    depth, width = got[0].shape
    return whole(
        rows_join_kernel,
        [jax.ShapeDtypeStruct((len(got) * depth, n), BF16) for n in (wide, width - wide)],
        me,
        *got,
    )


def rotate(x, cos, sin):
    return x * cos + pltpu.roll(x, HEAD_DIMENSION // 2, 1) * sin


def head_slice(i):
    return slice(i * HEAD_DIMENSION, (i + 1) * HEAD_DIMENSION)


def normed_rotated(raw, gain, cos, sin):
    return rotate(raw * norm_factor(raw) * gain, cos, sin).astype(BF16)


def probabilities(keys, queries, first_query, earliest):
    scores = dot(keys, queries, 1, 1) * score_scaling
    key_index = lax.broadcasted_iota(jnp.int32, scores.shape, 0)
    query_index = lax.broadcasted_iota(jnp.int32, scores.shape, 1) + first_query
    allowed = (key_index <= query_index) & (key_index >= earliest)
    masked = jnp.where(allowed, scores, -1e30)
    shifted = jnp.exp(masked - jnp.max(masked, axis=0, keepdims=True))
    return shifted * (1.0 / jnp.sum(shifted, axis=0, keepdims=True))


def forward_kernel(block, qkv_ref, gain_ref, cos_ref, sin_ref, early_ref, out_ref):
    length = qkv_ref.shape[0]
    gains = gain_ref[...]
    cos, sin = cos_ref[...], sin_ref[...]
    keys = normed_rotated(qkv_ref[:, head_slice(GROUP)], gains[1:2], cos, sin)
    values_t = qkv_ref[:, head_slice(GROUP + 1)].T.astype(BF16)
    for i in range(length // block):
        rows = slice(i * block, (i + 1) * block)
        seen = (i + 1) * block
        for g in range(GROUP):
            queries = normed_rotated(qkv_ref[rows, head_slice(g)], gains[0:1], cos[rows], sin[rows])
            probs = probabilities(keys[:seen], queries, i * block, early_ref[0:1, rows]).astype(BF16)
            mixed = dot(values_t[:, :seen], probs)
            out_ref[rows, head_slice(g)] = mixed.T.astype(BF16)


def backward_kernel(
    block, qkv_ref, dout_ref, gain_ref, cos_ref, sin_ref, early_ref, dqkv_ref, dgain_ref, dkey_ref, dvalue_ref
):
    length = qkv_ref.shape[0]
    gains = gain_ref[...]
    cos, sin = cos_ref[...], sin_ref[...]
    key_raw = qkv_ref[:, head_slice(GROUP)]
    keys = normed_rotated(key_raw, gains[1:2], cos, sin)
    keys_t = keys.astype(F32).T.astype(BF16)
    values = qkv_ref[:, head_slice(GROUP + 1)].astype(BF16)
    dkey_ref[...] = jnp.zeros_like(dkey_ref)
    dvalue_ref[...] = jnp.zeros_like(dvalue_ref)
    query_gain_sum = jnp.zeros((1, HEAD_DIMENSION), F32)
    for i in range(length // block):
        rows = slice(i * block, (i + 1) * block)
        seen = (i + 1) * block
        for g in range(GROUP):
            query_raw = qkv_ref[rows, head_slice(g)]
            queries = normed_rotated(query_raw, gains[0:1], cos[rows], sin[rows])
            dout = dout_ref[rows, head_slice(g)]
            probs = probabilities(keys[:seen], queries, i * block, early_ref[0:1, rows])
            dprobs = dot(values[:seen], dout, 1, 1)
            delta = jnp.sum(probs * dprobs, axis=0, keepdims=True)
            dscores = (probs * (dprobs - delta)).astype(BF16)
            dkey_ref[:seen] += dot(dscores, queries)
            dvalue_ref[:seen] += dot(probs.astype(BF16), dout)
            dquery = dot(keys_t[:, :seen], dscores).T * score_scaling
            dquery = rotate(dquery, cos[rows], -sin[rows])
            factor = norm_factor(query_raw)
            query_gain_sum += jnp.sum(query_raw * factor * dquery, axis=0, keepdims=True)
            dqkv_ref[rows, head_slice(g)] = norm_back(query_raw, factor, dquery * gains[0:1]).astype(BF16)
    dkey = rotate(dkey_ref[...] * score_scaling, cos, -sin)
    factor = norm_factor(key_raw)
    dgain_ref[0, 0:1, :] = query_gain_sum
    dgain_ref[0, 1:2, :] = jnp.sum(key_raw * factor * dkey, axis=0, keepdims=True)
    dgain_ref[0, 2:, :] = jnp.zeros((6, HEAD_DIMENSION), F32)
    dqkv_ref[:, head_slice(GROUP)] = norm_back(key_raw, factor, dkey * gains[1:2]).astype(BF16)
    dqkv_ref[:, head_slice(GROUP + 1)] = dvalue_ref[...].astype(BF16)


def per_head_specs(length):
    whole = lambda shape: pl.BlockSpec(shape, lambda n: (0,) * len(shape))
    return [
        whole((2, HEAD_DIMENSION)),
        whole((length, HEAD_DIMENSION)),
        whole((length, HEAD_DIMENSION)),
        whole((8, length)),
    ]


def columns_spec(length, width):
    return pl.BlockSpec((length, width), lambda n: (0, n))


def attention_forward(qkv, gains, cos, sin, earliest):
    length, width = qkv.shape
    heads = width // HEAD_SET
    return pl.pallas_call(
        functools.partial(forward_kernel, 256),
        grid=(heads,),
        in_specs=[columns_spec(length, HEAD_SET)] + per_head_specs(length),
        out_specs=columns_spec(length, GROUP * HEAD_DIMENSION),
        out_shape=jax.ShapeDtypeStruct((length, heads * GROUP * HEAD_DIMENSION), BF16),
        compiler_params=pltpu.CompilerParams(vmem_limit_bytes=48 << 20),
        cost_estimate=CHEAP,
    )(qkv, gains, cos, sin, earliest)


def attention_backward(qkv, dout, gains, cos, sin, earliest):
    length, width = qkv.shape
    heads = width // HEAD_SET
    return pl.pallas_call(
        functools.partial(backward_kernel, 256),
        grid=(heads,),
        in_specs=[columns_spec(length, HEAD_SET), columns_spec(length, GROUP * HEAD_DIMENSION)]
        + per_head_specs(length),
        out_specs=[
            columns_spec(length, HEAD_SET),
            pl.BlockSpec((1, 8, HEAD_DIMENSION), lambda n: (n, 0, 0)),
        ],
        out_shape=[
            jax.ShapeDtypeStruct((length, width), BF16),
            jax.ShapeDtypeStruct((heads, 8, HEAD_DIMENSION), F32),
        ],
        scratch_shapes=[pltpu.VMEM((length, HEAD_DIMENSION), F32)] * 2,
        compiler_params=pltpu.CompilerParams(vmem_limit_bytes=48 << 20),
        cost_estimate=CHEAP,
    )(qkv, dout, gains, cos, sin, earliest)


def hidden_kernel(pre_ref, grad_ref, down_ref, hidden_ref, dpre_ref):
    tile = hidden_ref.shape[1]
    grad_hidden = dot(grad_ref[...], down_ref[...])
    step = 128
    for start in range(0, hidden_ref.shape[0], step):
        rows = slice(start, start + step)
        gate, up, grad = pre_ref[rows, :tile], pre_ref[rows, tile:], grad_hidden[rows]
        sig = 1.0 / (1.0 + jnp.exp(-gate))
        act = gate * sig
        hidden_ref[rows] = (act * up).astype(BF16)
        dpre_ref[rows, :tile] = (grad * up * sig * (1.0 + gate * (1.0 - sig))).astype(BF16)
        dpre_ref[rows, tile:] = (grad * act).astype(BF16)


def hidden_layer(pre, grad, down, tiles):
    rows, width = grad.shape
    tile = down.shape[1] // tiles
    step = min(rows, 1024)
    return pl.pallas_call(
        hidden_kernel,
        grid=(tiles, rows // step),
        in_specs=[
            pl.BlockSpec((step, 2 * tile), lambda j, i: (i, j)),
            pl.BlockSpec((step, width), lambda j, i: (i, 0)),
            pl.BlockSpec((width, tile), lambda j, i: (0, j)),
        ],
        out_specs=[
            pl.BlockSpec((step, tile), lambda j, i: (i, j)),
            pl.BlockSpec((step, 2 * tile), lambda j, i: (i, j)),
        ],
        out_shape=[
            jax.ShapeDtypeStruct((rows, tile * tiles), BF16),
            jax.ShapeDtypeStruct((rows, 2 * tile * tiles), BF16),
        ],
        compiler_params=pltpu.CompilerParams(vmem_limit_bytes=56 << 20),
        cost_estimate=CHEAP,
    )(pre, grad, down)


def tie(*items):
    return lax.optimization_barrier(items)


def swap(x, axis, bit):
    return lax.ppermute(x, axis, [(i, i ^ bit) for i in range(lax.axis_size(axis))])


def to_sequence(blocks):
    half, part, parts = lax.axis_index("h"), lax.axis_index("t"), lax.axis_size("t")
    block = blocks.shape[1]
    own = lax.dynamic_index_in_dim(blocks, half, 0, keepdims=False)
    got = swap(lax.dynamic_index_in_dim(blocks, 1 - half, 0, keepdims=False), "h", 1)
    placed = []
    for first, start in ((own, 0), (got, parts)):
        held, keys = [first[None]], [start]
        bit = parts // 2
        while bit:
            held.append(swap(jnp.concatenate(held, axis=0), "t", bit))
            keys += [k | bit for k in keys]
            bit //= 2
        flat = [piece[i] for piece in held for i in range(piece.shape[0])]
        placed += [(b, ((half * parts + part) ^ k) * block) for b, k in zip(flat, keys)]
    return placed


def assemble(placed, columns=slice(None), out=None):
    rows = sum(part.shape[0] for part, _ in placed)
    if out is None:
        out = jnp.zeros((rows, placed[0][0][:, columns].shape[1]), placed[0][0].dtype)
    for part, start in placed:
        out = lax.dynamic_update_slice_in_dim(out, part[:, columns], start, 0)
    return out


def to_blocks(partial):
    half, part, parts = lax.axis_index("h"), lax.axis_index("t"), lax.axis_size("t")
    both = partial.reshape(2, parts, -1, partial.shape[1])
    held = [lax.dynamic_index_in_dim(both, part ^ key, 1, keepdims=False) for key in range(parts)]

    def pick(x, h):
        return lax.dynamic_index_in_dim(x, h, 0, keepdims=False)

    bit = 1
    while 2 * bit < parts:
        got = {key: swap(held[key].astype(BF16), "t", bit) for key in reversed(range(parts)) if held[key] is not None and key & bit}
        for key, value in got.items():
            held[key ^ bit] = held[key ^ bit].astype(F32) + value.astype(F32)
            held[key] = None
        bit *= 2
    far = pick(held[0], 1 - half).astype(F32) + swap(pick(held[bit], 1 - half).astype(BF16), "t", bit).astype(F32)
    got = swap(far.astype(BF16), "h", 1).astype(F32)
    own = pick(held[0], half).astype(F32) + swap(pick(held[bit], half).astype(BF16), "t", bit).astype(F32)
    return jnp.where(half == 0, jnp.stack([own, got]), jnp.stack([got, own]))


def swaps(pieces, axis="dp"):
    return [pieces[0]] + list(reversed([swap(pieces[s], axis, s) for s in reversed(range(1, len(pieces)))]))


def gather_h(x):
    return [x, swap(x, "h", 1)]


def place_rows(blocks):
    dp, half = lax.axis_index("dp"), lax.axis_index("h")
    count, (rows, width) = lax.axis_size("dp"), blocks[0][0].shape
    out = jnp.zeros((count * 2 * rows, width), blocks[0][0].dtype)
    for k, parts in enumerate(blocks):
        for s, part in enumerate(parts):
            out = lax.dynamic_update_slice_in_dim(out, part, ((dp ^ s) * 2 + (half ^ k)) * rows, 0)
    return out


def sum_h(got):
    half = lax.axis_index("h")
    total = sum(g.astype(F32) for g in got)
    total = total.reshape(2, total.shape[0] // 2, -1)
    give = lax.dynamic_index_in_dim(total, 1 - half, 0, keepdims=False).astype(BF16)
    return lax.dynamic_index_in_dim(total, half, 0, keepdims=False), give


def total_over(x, axis):
    bit = 1
    while bit < lax.axis_size(axis):
        x = x + swap(x, axis, bit)
        bit *= 2
    return x


def per_device(
    tokens,
    positions,
    attn_norm,
    query_proj,
    key_projected,
    value_projected,
    head_norms,
    out_proj,
    mlp_norm,
    gate_proj,
    up_proj,
    down_proj,
    out_grad,
):
    block, seqs, width = tokens.shape
    rows = block * seqs
    dp = lax.axis_size("dp")
    parts = lax.axis_size("t")
    ctx = 2 * parts
    length = block * ctx
    depth = query_proj.shape[0]
    part = lax.axis_index("t")
    attn_gain = attn_norm.astype(F32)[:, None]
    mlp_gain = mlp_norm.astype(F32)[:, None]

    inputs = jnp.transpose(tokens, (1, 0, 2)).astype(F32)
    factor_one = norm_factor(inputs)
    digits = jnp.stack([positions.T // 16, positions.T % 16], axis=2).astype(BF16)
    digits = jnp.pad(digits, ((0, 0), (0, 0), (0, HEAD_DIMENSION - 2)))
    placed = to_sequence(jnp.concatenate([(inputs * factor_one).astype(BF16), digits], axis=2))
    normed_one = assemble(placed, slice(0, width))
    places = assemble(placed, slice(width, width + HEAD_DIMENSION))[:, :2].astype(jnp.int32)
    places = places[:, 0] * 16 + places[:, 1]

    heads = KEY_VALUE_HEADS // parts
    pair = GROUP * HEAD_DIMENSION
    qkv_width, mix_width = heads * HEAD_SET, heads * pair
    attn_width = qkv_width + mix_width

    dp_index = lax.axis_index("dp")
    attn_set = whole(
        functools.partial(attn_split_kernel, heads),
        [jax.ShapeDtypeStruct((depth, attn_width), BF16)] * parts,
        part,
        attn_gain,
        query_proj,
        key_projected,
        value_projected,
        out_proj,
    )
    attn_set, gate_proj = tie(attn_set, gate_proj)
    qkv_rows, out_rows = rows_join(swaps(attn_set, "t"), qkv_width, part)

    hidden = gate_proj.shape[1] // dp
    tiles = 3
    ffn_set = whole(
        functools.partial(ffn_split_kernel, tiles),
        [jax.ShapeDtypeStruct((depth, 3 * hidden), BF16)] * dp,
        dp_index,
        mlp_gain,
        gate_proj,
        up_proj,
        down_proj,
    )

    qkv_blocks = gather_h(qkv_rows)
    qkv_own = swaps([qkv_blocks[0]] * dp)
    if F_AFTER_W:
        qkv_own, ffn_set = tie(qkv_own, ffn_set)
    ffn_got = swaps(ffn_set)
    qkv_weight = place_rows([qkv_own, swaps([qkv_blocks[1]] * dp)])
    pre_rows, down_rows = rows_join(ffn_got, 2 * hidden, dp_index)
    pre_rows, normed_one = tie(pre_rows, normed_one)

    def ffn_gather(x):
        return lax.all_gather(x, ("h", "t"), axis=0, tiled=False)

    def ordered(w):
        return jnp.transpose(w.reshape(ctx, dp, depth, -1), (1, 0, 2, 3)).reshape(width, -1)

    pre_all = ffn_gather(pre_rows)

    def ffn_scatter(term):
        return lax.psum_scatter(term, ("h", "t"), scatter_dimension=0, tiled=True).reshape(dp, depth, -1)

    gains = head_norms.astype(F32)
    half_width = HEAD_DIMENSION // 2
    frequency = theta_base ** (-(jnp.arange(half_width, dtype=F32) * 2.0 / HEAD_DIMENSION))
    angles = places.astype(F32)[:, None] * frequency
    cos, sin = jnp.cos(angles), jnp.sin(angles)
    cos = jnp.concatenate([cos, cos], axis=1)
    sin = jnp.concatenate([-sin, sin], axis=1)
    earliest = jnp.broadcast_to((jnp.arange(length, dtype=jnp.int32) - places)[None, :], (8, length))
    out_rows, normed_one = tie(out_rows, normed_one)
    out_blocks = gather_h(out_rows)
    qkv = rows_product(normed_one, qkv_weight, 0, 256, F32)
    out_blocks, qkv = tie(out_blocks, qkv)
    out_weight = place_rows([swaps([b] * dp) for b in out_blocks])
    mixed = attention_forward(qkv, gains, cos, sin, earliest)
    grad_own = jnp.transpose(out_grad, (1, 0, 2)).reshape(rows, width)
    out_weight, mixed, grad_own = tie(out_weight, mixed, grad_own)
    grad_rows = swaps([grad_own] * dp)
    mixed_sum = to_blocks(rows_product(mixed, out_weight, 1, 512, BF16))
    middle = (inputs + mixed_sum).reshape(rows, width)
    pre_all, down_rows, middle = tie(pre_all, down_rows, middle)
    pre_weight, down_weight = ordered(pre_all), ordered(ffn_gather(down_rows))

    factor_two = norm_factor(middle)
    own_two = (middle * factor_two).astype(BF16)
    grad_rows, own_two = tie(grad_rows, own_two)
    grad_rows = jnp.concatenate(grad_rows, axis=0)
    normed_two = jnp.concatenate(swaps([own_two] * dp), axis=0)
    pre = rows_product(normed_two, pre_weight, 0, hidden // 2, F32)
    hidden_low, grad_pre = hidden_layer(pre, grad_rows, down_weight, tiles)
    down_term = term_product(grad_rows, hidden_low, dp, ctx)
    down_term, grad_pre = tie(down_term, grad_pre)
    down_sum = ffn_scatter(down_term)
    two_part = rows_product(grad_pre, pre_weight, 1, 512, BF16, dp)
    grad_pre, two_part = tie(grad_pre, two_part)
    two_got = swaps(two_part)
    pre_term = term_product(normed_two, grad_pre, dp, ctx)
    pre_term, two_got = tie(pre_term, two_got)
    grad_two = sum(g.astype(F32) for g in two_got)
    mlp_norm_sum = jnp.sum(middle * factor_two * grad_two, axis=0)
    grad_middle = grad_own.astype(F32) + norm_back(middle, factor_two, grad_two)
    grad_mid_own = grad_middle.astype(BF16).reshape(seqs, block, width)
    grad_mid_own, hidden_low = tie(grad_mid_own, hidden_low)
    branch_got = swaps(rows_product(hidden_low, down_weight, 1, 512, BF16, dp))

    grad_mid = assemble(to_sequence(grad_mid_own), slice(None), normed_two)
    if PRE_LATE:
        grad_mid, pre_term = tie(grad_mid, pre_term)
    pre_sum = ffn_scatter(pre_term)
    grad_mixed = rows_product(grad_mid, out_weight, 0, 256, BF16)
    out_pieces = term_pieces(grad_mid, mixed, dp_index, dp)
    grad_mixed, out_pieces = tie(grad_mixed, out_pieces)
    out_got = swaps(out_pieces)
    grad_qkv, gain_terms = attention_backward(qkv, grad_mixed, gains, cos, sin, earliest)
    grad_one_part, norm_sums = input_product(grad_qkv, qkv_weight, normed_one, mlp_norm_sum[None], 512)

    qkv_pieces = term_pieces(normed_one, grad_qkv, dp_index, dp, norm_sums)
    qkv_pieces, grad_one_part, branch_got, out_got = tie(qkv_pieces, grad_one_part, branch_got, out_got)
    qkv_got = swaps(qkv_pieces)
    branch = sum(g.astype(F32) for g in branch_got)
    layer_out = (middle + branch).astype(BF16)
    out_keep, out_give = sum_h(out_got)
    out_sum = out_keep + swap(out_give, "h", 1).astype(F32)
    grad_one = to_blocks(grad_one_part)
    qkv_keep, qkv_give = sum_h(qkv_got)
    head_norm_grad = total_over(total_over(jnp.sum(gain_terms, axis=0)[:2], "t"), "h")
    qkv_give, out_sum, pre_sum, down_sum = tie(qkv_give, out_sum, pre_sum, down_sum)
    qkv_sum = qkv_keep + swap(qkv_give, "h", 1).astype(F32)
    ffn_sum = jnp.concatenate([pre_sum, down_sum], axis=2)
    ffn_grad = swaps(
        [lax.dynamic_index_in_dim(ffn_sum, dp_index ^ k, 0, keepdims=False) for k in range(dp)]
    )
    gate_grad, up_grad, down_grad = whole(
        functools.partial(ffn_join_kernel, tiles),
        [jax.ShapeDtypeStruct(gate_proj.shape, F32)] * 3,
        dp_index,
        mlp_gain,
        *ffn_grad,
    )
    input_grad = grad_middle.reshape(seqs, block, width) + norm_back(inputs, factor_one, grad_one)

    attn_sum = jnp.concatenate([qkv_sum, out_sum], axis=1).astype(BF16)
    attn_sum, head_norm_grad = tie(attn_sum, head_norm_grad)
    head_norm_grad = total_over(head_norm_grad, "dp")
    attn_grad = swaps(
        [lax.dynamic_slice_in_dim(attn_sum, (part ^ k) * depth, depth, 0) for k in range(parts)], "t"
    )
    query_grad, key_grad, value_grad, out_proj_grad, norm_grads = whole(
        functools.partial(attn_join_kernel, heads),
        [
            jax.ShapeDtypeStruct(x.shape, F32)
            for x in (query_proj, key_projected, value_projected, out_proj, jnp.zeros((depth, HEAD_DIMENSION)))
        ],
        part,
        attn_gain,
        *attn_grad,
    )
    attn_norm_grad = norm_grads[:, 0] / attn_gain[:, 0]
    mlp_norm_grad = norm_grads[:, 1] / mlp_gain[:, 0]

    layer_out = jnp.transpose(layer_out.reshape(seqs, block, width), (1, 0, 2))
    input_grad = jnp.transpose(input_grad, (1, 0, 2))
    return (
        layer_out,
        input_grad,
        attn_norm_grad,
        query_grad,
        key_grad,
        value_grad,
        head_norm_grad,
        out_proj_grad,
        mlp_norm_grad,
        gate_grad,
        up_grad,
        down_grad,
    )


def solution(mesh):
    dp, ctx = mesh.shape["dp"], mesh.shape["ctx"]
    fine = Mesh(mesh.devices.reshape(dp, 2, ctx // 2), ("dp", "h", "t"))
    acts = P(("h", "t"), "dp", None)
    rows = P(("dp", "h", "t"), None)
    gain = P(("dp", "h", "t"))
    in_specs = (
        acts,
        P(("h", "t"), "dp"),
        gain,
        rows,
        rows,
        rows,
        P(),
        rows,
        gain,
        rows,
        rows,
        rows,
        acts,
    )
    out_specs = (acts, acts, gain, rows, rows, rows, P(), rows, gain, rows, rows, rows)
    return jax.shard_map(per_device, mesh=fine, in_specs=in_specs, out_specs=out_specs, check_vma=False)
```

```python
import functools

import jax
import jax.numpy as jnp
from jax import lax
from jax.experimental import pallas as pl
from jax.experimental.pallas import tpu as pltpu
from jax.sharding import Mesh
from jax.sharding import PartitionSpec as P

QUERY_HEADS = 16
KEY_VALUE_HEADS = 8
HEAD_DIMENSION = 128
GROUP = QUERY_HEADS // KEY_VALUE_HEADS
HEAD_SET = (GROUP + 2) * HEAD_DIMENSION

epsilon = 1e-06
theta_base = 1000000.0
score_scaling = HEAD_DIMENSION ** (-0.5)
F32 = jnp.float32
BF16 = jnp.bfloat16


def norm_factor(matrix):
    return lax.rsqrt(jnp.mean(matrix * matrix, axis=-1, keepdims=True) + epsilon)


def norm_back(matrix, factor, upstream):
    return factor * upstream - matrix * (factor * factor * factor) * jnp.mean(
        upstream * matrix, axis=-1, keepdims=True
    )


def dot(a, b, ca=1, cb=0):
    return lax.dot_general(a, b, (((ca,), (cb,)), ((), ())), preferred_element_type=F32)


PRE_LATE = True
CHEAP = pl.CostEstimate(flops=1 << 20, bytes_accessed=1 << 16, transcendentals=0)


def rows_kernel(contract, a_ref, b_ref, *out_refs):
    out = dot(a_ref[...], b_ref[...], 1, contract).astype(out_refs[0].dtype)
    step = out_refs[0].shape[0]
    for k, out_ref in enumerate(out_refs):
        out_ref[...] = out[k * step : (k + 1) * step]


def rows_product(a, b, contract, tile, dtype, pieces=1):
    rows, depth = a.shape
    columns = b.shape[1 - contract]
    tile = min(tile, columns)
    out = pl.pallas_call(
        functools.partial(rows_kernel, contract),
        grid=(columns // tile,),
        in_specs=[
            pl.BlockSpec((rows, depth), lambda j: (0, 0)),
            pl.BlockSpec((depth, tile), lambda j: (0, j))
            if contract == 0
            else pl.BlockSpec((tile, depth), lambda j: (j, 0)),
        ],
        out_specs=[pl.BlockSpec((rows // pieces, tile), lambda j: (0, j))] * pieces,
        out_shape=[jax.ShapeDtypeStruct((rows // pieces, columns), dtype)] * pieces,
        compiler_params=pltpu.CompilerParams(vmem_limit_bytes=48 << 20),
        cost_estimate=CHEAP,
    )(a, b)
    return out if pieces > 1 else out[0]


def blocks_kernel(where_ref, a_ref, *refs):
    w_refs, out_ref = refs[:-1], refs[-1]
    depth = w_refs[0].shape[0]
    total = None
    for k, w_ref in enumerate(w_refs):
        start = pl.multiple_of(where_ref[k] * depth, HEAD_DIMENSION)
        part = dot(a_ref[:, pl.ds(start, depth)], w_ref[...])
        total = part if total is None else total + part
    out_ref[...] = total


def blocks_product(a, w_blocks, where, tile):
    rows, depth = a.shape
    columns = w_blocks[0].shape[1]
    return pl.pallas_call(
        blocks_kernel,
        grid_spec=pltpu.PrefetchScalarGridSpec(
            num_scalar_prefetch=1,
            grid=(columns // tile,),
            in_specs=[pl.BlockSpec((rows, depth), lambda j, where: (0, 0))]
            + [pl.BlockSpec((w.shape[0], tile), lambda j, where: (0, j)) for w in w_blocks],
            out_specs=pl.BlockSpec((rows, tile), lambda j, where: (0, j)),
        ),
        out_shape=jax.ShapeDtypeStruct((rows, columns), F32),
        compiler_params=pltpu.CompilerParams(vmem_limit_bytes=48 << 20),
        cost_estimate=CHEAP,
    )(where, a, *w_blocks)


def blocks_back_kernel(where_ref, a_ref, *refs):
    w_refs, out_ref = refs[:-1], refs[-1]
    depth = w_refs[0].shape[0]
    for k, w_ref in enumerate(w_refs):
        start = pl.multiple_of(where_ref[k] * depth, HEAD_DIMENSION)
        out_ref[:, pl.ds(start, depth)] = dot(a_ref[...], w_ref[...], 1, 1).astype(BF16)


def blocks_back(a, w_blocks, where, pieces):
    rows, depth = a.shape
    columns = sum(w.shape[0] for w in w_blocks)
    return pl.pallas_call(
        blocks_back_kernel,
        grid_spec=pltpu.PrefetchScalarGridSpec(
            num_scalar_prefetch=1,
            grid=(pieces,),
            in_specs=[pl.BlockSpec((rows // pieces, depth), lambda j, where: (j, 0))]
            + [pl.BlockSpec(w.shape, lambda j, where: (0, 0)) for w in w_blocks],
            out_specs=pl.BlockSpec((rows // pieces, columns), lambda j, where: (j, 0)),
        ),
        out_shape=jax.ShapeDtypeStruct((rows, columns), BF16),
        compiler_params=pltpu.CompilerParams(vmem_limit_bytes=48 << 20),
        cost_estimate=CHEAP,
    )(where, a, *w_blocks)


def stacked_kernel(a_ref, w_ref, out_ref):
    out_ref[...] = stacked_dot(a_ref, w_ref).astype(out_ref.dtype)


def stacked_dot(a_ref, w_ref):
    blocks, groups, depth, columns = w_ref.shape
    step = blocks * depth
    total = None
    for d in range(groups):
        part = dot(a_ref[:, d * step : (d + 1) * step], w_ref[:, d].reshape(step, columns))
        total = part if total is None else total + part
    return total


def stacked_product(a, w, tile):
    rows, depth = a.shape
    columns = w.shape[3]
    return pl.pallas_call(
        stacked_kernel,
        grid=(columns // tile,),
        in_specs=[
            pl.BlockSpec((rows, depth), lambda j: (0, 0)),
            pl.BlockSpec(w.shape[:3] + (tile,), lambda j: (0, 0, 0, j)),
        ],
        out_specs=pl.BlockSpec((rows, tile), lambda j: (0, j)),
        out_shape=jax.ShapeDtypeStruct((rows, columns), F32),
        compiler_params=pltpu.CompilerParams(vmem_limit_bytes=56 << 20),
        cost_estimate=CHEAP,
    )(a, w)


def stacked_back_kernel(a_ref, w_ref, *out_refs):
    blocks, _, depth, columns = w_ref.shape
    out = dot(a_ref[...], w_ref[:, 0].reshape(blocks * depth, columns), 1, 1).astype(BF16)
    step = out_refs[0].shape[0]
    for k, out_ref in enumerate(out_refs):
        out_ref[...] = out[k * step : (k + 1) * step]


def stacked_back(a, w, pieces):
    rows, depth = a.shape
    blocks, groups, n, columns = w.shape
    step = blocks * n
    return pl.pallas_call(
        stacked_back_kernel,
        grid=(groups,),
        in_specs=[
            pl.BlockSpec((rows, depth), lambda j: (0, 0)),
            pl.BlockSpec((blocks, 1, n, columns), lambda j: (0, j, 0, 0)),
        ],
        out_specs=[pl.BlockSpec((rows // pieces, step), lambda j: (0, j))] * pieces,
        out_shape=[jax.ShapeDtypeStruct((rows // pieces, groups * step), BF16)] * pieces,
        compiler_params=pltpu.CompilerParams(vmem_limit_bytes=56 << 20),
        cost_estimate=CHEAP,
    )(a, w)


def term_kernel(a_ref, b_ref, out_ref):
    out_ref[...] = dot(a_ref[...], b_ref[...], 0, 0).astype(BF16).reshape(out_ref.shape)


def term_product(a, b, groups, blocks):
    rows, width = a.shape
    columns = b.shape[1]
    depth = width // (groups * blocks)
    return pl.pallas_call(
        term_kernel,
        grid=(groups,),
        in_specs=[
            pl.BlockSpec((rows, blocks * depth), lambda i: (0, i)),
            pl.BlockSpec((rows, columns), lambda i: (0, 0)),
        ],
        out_specs=pl.BlockSpec((blocks, 1, depth, columns), lambda i: (0, i, 0, 0)),
        out_shape=jax.ShapeDtypeStruct((blocks, groups, depth, columns), BF16),
        compiler_params=pltpu.CompilerParams(vmem_limit_bytes=56 << 20),
        cost_estimate=CHEAP,
    )(a, b).reshape(width, columns)


def pieces_kernel(me_ref, a_ref, b_ref, *refs):
    norm_ref, out_refs = (refs[0], refs[1:]) if refs[0].shape[0] == 8 else (None, refs)
    wide = b_ref.shape[1]
    part = dot(a_ref[...], b_ref[...], 0, 0).astype(BF16)
    for s, out_ref in enumerate(out_refs):

        @pl.when(pl.program_id(0) == s)
        def _():
            out_ref[:, :wide] = part
            if norm_ref is not None:
                sums = norm_ref[...].T
                rest = jnp.zeros((sums.shape[0], HEAD_DIMENSION - 8), F32)
                out_ref[:, wide:] = jnp.concatenate([sums, rest], axis=1).astype(BF16)


def term_pieces(a, b, me, count, norms=None):
    rows, width = a.shape
    columns = b.shape[1]
    step = width // count
    extra = 0 if norms is None else HEAD_DIMENSION
    in_specs = [
        pl.BlockSpec((rows, step), lambda i, me: (0, me[0] ^ i)),
        pl.BlockSpec((rows, columns), lambda i, me: (0, 0)),
    ]
    if norms is not None:
        in_specs.append(pl.BlockSpec((8, step), lambda i, me: (0, me[0] ^ i)))
    return pl.pallas_call(
        pieces_kernel,
        grid_spec=pltpu.PrefetchScalarGridSpec(
            num_scalar_prefetch=1,
            grid=(count,),
            in_specs=in_specs,
            out_specs=[pl.BlockSpec((step, columns + extra), lambda i, me: (0, 0))] * count,
        ),
        out_shape=[jax.ShapeDtypeStruct((step, columns + extra), BF16)] * count,
        compiler_params=pltpu.CompilerParams(vmem_limit_bytes=56 << 20),
        cost_estimate=CHEAP,
    )(me.reshape(1).astype(jnp.int32), a, b, *([] if norms is None else [norms]))


def input_kernel(grad_ref, weight_ref, normed_ref, other_ref, out_ref, sum_ref):
    part = dot(grad_ref[...], weight_ref[...], 1, 1)
    out_ref[...] = part.astype(BF16)
    sum_ref[...] = jnp.zeros_like(sum_ref)
    sum_ref[0:1] = jnp.sum(normed_ref[...].astype(F32) * part, axis=0, keepdims=True)
    sum_ref[1:2] = other_ref[...]


def input_product(grad, weight, normed, other, tile):
    rows, depth = grad.shape
    columns = weight.shape[0]
    return pl.pallas_call(
        input_kernel,
        grid=(columns // tile,),
        in_specs=[
            pl.BlockSpec((rows, depth), lambda j: (0, 0)),
            pl.BlockSpec((tile, depth), lambda j: (j, 0)),
            pl.BlockSpec((rows, tile), lambda j: (0, j)),
            pl.BlockSpec((1, tile), lambda j: (0, j)),
        ],
        out_specs=[pl.BlockSpec((rows, tile), lambda j: (0, j)), pl.BlockSpec((8, tile), lambda j: (0, j))],
        out_shape=[jax.ShapeDtypeStruct((rows, columns), BF16), jax.ShapeDtypeStruct((8, columns), F32)],
        compiler_params=pltpu.CompilerParams(vmem_limit_bytes=48 << 20),
        cost_estimate=CHEAP,
    )(grad, weight, normed, other)


def whole(kernel, shapes, me, *arrays):
    vmem = pl.BlockSpec(memory_space=pltpu.VMEM)
    return pl.pallas_call(
        kernel,
        in_specs=[pl.BlockSpec(memory_space=pltpu.SMEM)] + [vmem] * len(arrays),
        out_specs=[vmem] * len(shapes),
        out_shape=shapes,
        compiler_params=pltpu.CompilerParams(vmem_limit_bytes=48 << 20),
        cost_estimate=CHEAP,
    )(me.reshape(1).astype(jnp.int32), *arrays)


def lanes(index, size):
    return pl.ds(pl.multiple_of(index * size, HEAD_DIMENSION), size)


def attn_split_kernel(heads, me_ref, gain_ref, q_ref, k_ref, v_ref, o_ref, *out_refs):
    pair = GROUP * HEAD_DIMENSION
    gain = gain_ref[...]

    def scaled(ref, index, size):
        return (ref[:, lanes(index, size)].astype(F32) * gain).astype(BF16)

    for s, out_ref in enumerate(out_refs):
        part = me_ref[0] ^ s
        for n in range(heads):
            head, at = part * heads + n, n * HEAD_SET
            out_ref[:, at : at + pair] = scaled(q_ref, head, pair)
            out_ref[:, at + pair : at + pair + HEAD_DIMENSION] = scaled(k_ref, head, HEAD_DIMENSION)
            out_ref[:, at + pair + HEAD_DIMENSION : at + HEAD_SET] = scaled(v_ref, head, HEAD_DIMENSION)
        out_ref[:, heads * HEAD_SET :] = o_ref[:, lanes(part, heads * pair)]


def attn_join_kernel(heads, me_ref, gain_ref, *refs):
    count = len(refs) - 5
    q_ref, k_ref, v_ref, o_ref, norm_ref = refs[count:]
    pair = GROUP * HEAD_DIMENSION
    gain = gain_ref[...]
    norms = jnp.zeros(norm_ref.shape, F32)
    for s, got_ref in enumerate(refs[:count]):
        part = me_ref[0] ^ s
        for n in range(heads):
            head, at = part * heads + n, n * HEAD_SET
            q_ref[:, lanes(head, pair)] = got_ref[:, at : at + pair].astype(F32) * gain
            k_ref[:, lanes(head, HEAD_DIMENSION)] = (
                got_ref[:, at + pair : at + pair + HEAD_DIMENSION].astype(F32) * gain
            )
            v_ref[:, lanes(head, HEAD_DIMENSION)] = (
                got_ref[:, at + pair + HEAD_DIMENSION : at + HEAD_SET].astype(F32) * gain
            )
        norms += got_ref[:, heads * HEAD_SET : heads * HEAD_SET + HEAD_DIMENSION].astype(F32)
        o_ref[:, lanes(part, heads * pair)] = got_ref[:, heads * HEAD_SET + HEAD_DIMENSION :].astype(F32)
    norm_ref[...] = norms


def ffn_split_kernel(tiles, me_ref, gain_ref, gate_ref, up_ref, down_ref, *out_refs):
    gain = gain_ref[...]
    hidden = out_refs[0].shape[1] // 3
    tile = hidden // tiles
    for s, out_ref in enumerate(out_refs):
        part = me_ref[0] ^ s
        for n in range(tiles):
            for k, ref in enumerate((gate_ref, up_ref)):
                at = (2 * n + k) * tile
                out_ref[:, at : at + tile] = (ref[:, lanes(part * tiles + n, tile)].astype(F32) * gain).astype(
                    BF16
                )
        out_ref[:, 2 * hidden :] = down_ref[:, lanes(part, hidden)]


def ffn_join_kernel(tiles, me_ref, gain_ref, *refs):
    count = (len(refs) - 3) // 2
    gate_ref, up_ref, down_ref = refs[2 * count :]
    gain = gain_ref[...]
    hidden = refs[0].shape[1] // 2
    tile = hidden // tiles
    for s, (got_ref, down_got_ref) in enumerate(zip(refs[:count], refs[count:])):
        part = me_ref[0] ^ s
        for n in range(tiles):
            for k, ref in enumerate((gate_ref, up_ref)):
                at = (2 * n + k) * tile
                ref[:, lanes(part * tiles + n, tile)] = got_ref[:, at : at + tile].astype(F32) * gain
        down_ref[:, lanes(part, hidden)] = down_got_ref[...].astype(F32)


def rows_join_kernel(me_ref, *refs):
    first_ref, second_ref = refs[-2:]
    depth = refs[0].shape[0]
    wide = first_ref.shape[1]
    for s, got_ref in enumerate(refs[:-2]):
        rows = pl.ds(pl.multiple_of((me_ref[0] ^ s) * depth, depth), depth)
        first_ref[rows] = got_ref[:, :wide]
        second_ref[rows] = got_ref[:, wide:]


def rows_join(got, wide, me):
    depth, width = got[0].shape
    return whole(
        rows_join_kernel,
        [jax.ShapeDtypeStruct((len(got) * depth, n), BF16) for n in (wide, width - wide)],
        me,
        *got,
    )


def rotate(x, cos, sin):
    return x * cos + pltpu.roll(x, HEAD_DIMENSION // 2, 1) * sin


def head_slice(i):
    return slice(i * HEAD_DIMENSION, (i + 1) * HEAD_DIMENSION)


def normed_rotated(raw, gain, cos, sin):
    return rotate(raw * norm_factor(raw) * gain, cos, sin).astype(BF16)


def probabilities(keys, queries, first_query, earliest):
    scores = dot(keys, queries, 1, 1) * score_scaling
    key_index = lax.broadcasted_iota(jnp.int32, scores.shape, 0)
    query_index = lax.broadcasted_iota(jnp.int32, scores.shape, 1) + first_query
    allowed = (key_index <= query_index) & (key_index >= earliest)
    masked = jnp.where(allowed, scores, -1e30)
    shifted = jnp.exp(masked - jnp.max(masked, axis=0, keepdims=True))
    return shifted * (1.0 / jnp.sum(shifted, axis=0, keepdims=True))


def forward_kernel(block, qkv_ref, gain_ref, cos_ref, sin_ref, early_ref, out_ref):
    length = qkv_ref.shape[0]
    gains = gain_ref[...]
    cos, sin = cos_ref[...], sin_ref[...]
    keys = normed_rotated(qkv_ref[:, head_slice(GROUP)], gains[1:2], cos, sin)
    values_t = qkv_ref[:, head_slice(GROUP + 1)].T.astype(BF16)
    for i in range(length // block):
        rows = slice(i * block, (i + 1) * block)
        seen = (i + 1) * block
        for g in range(GROUP):
            queries = normed_rotated(qkv_ref[rows, head_slice(g)], gains[0:1], cos[rows], sin[rows])
            probs = probabilities(keys[:seen], queries, i * block, early_ref[0:1, rows]).astype(BF16)
            mixed = dot(values_t[:, :seen], probs)
            out_ref[rows, head_slice(g)] = mixed.T.astype(BF16)


def backward_kernel(
    block, qkv_ref, dout_ref, gain_ref, cos_ref, sin_ref, early_ref, dqkv_ref, dgain_ref, dkey_ref, dvalue_ref
):
    length = qkv_ref.shape[0]
    gains = gain_ref[...]
    cos, sin = cos_ref[...], sin_ref[...]
    key_raw = qkv_ref[:, head_slice(GROUP)]
    keys = normed_rotated(key_raw, gains[1:2], cos, sin)
    keys_t = keys.astype(F32).T.astype(BF16)
    values = qkv_ref[:, head_slice(GROUP + 1)].astype(BF16)
    dkey_ref[...] = jnp.zeros_like(dkey_ref)
    dvalue_ref[...] = jnp.zeros_like(dvalue_ref)
    query_gain_sum = jnp.zeros((1, HEAD_DIMENSION), F32)
    for i in range(length // block):
        rows = slice(i * block, (i + 1) * block)
        seen = (i + 1) * block
        for g in range(GROUP):
            query_raw = qkv_ref[rows, head_slice(g)]
            queries = normed_rotated(query_raw, gains[0:1], cos[rows], sin[rows])
            dout = dout_ref[rows, head_slice(g)]
            probs = probabilities(keys[:seen], queries, i * block, early_ref[0:1, rows])
            dprobs = dot(values[:seen], dout, 1, 1)
            delta = jnp.sum(probs * dprobs, axis=0, keepdims=True)
            dscores = (probs * (dprobs - delta)).astype(BF16)
            dkey_ref[:seen] += dot(dscores, queries)
            dvalue_ref[:seen] += dot(probs.astype(BF16), dout)
            dquery = dot(keys_t[:, :seen], dscores).T * score_scaling
            dquery = rotate(dquery, cos[rows], -sin[rows])
            factor = norm_factor(query_raw)
            query_gain_sum += jnp.sum(query_raw * factor * dquery, axis=0, keepdims=True)
            dqkv_ref[rows, head_slice(g)] = norm_back(query_raw, factor, dquery * gains[0:1]).astype(BF16)
    dkey = rotate(dkey_ref[...] * score_scaling, cos, -sin)
    factor = norm_factor(key_raw)
    dgain_ref[0, 0:1, :] = query_gain_sum
    dgain_ref[0, 1:2, :] = jnp.sum(key_raw * factor * dkey, axis=0, keepdims=True)
    dgain_ref[0, 2:, :] = jnp.zeros((6, HEAD_DIMENSION), F32)
    dqkv_ref[:, head_slice(GROUP)] = norm_back(key_raw, factor, dkey * gains[1:2]).astype(BF16)
    dqkv_ref[:, head_slice(GROUP + 1)] = dvalue_ref[...].astype(BF16)


def per_head_specs(length):
    whole = lambda shape: pl.BlockSpec(shape, lambda n: (0,) * len(shape))
    return [
        whole((2, HEAD_DIMENSION)),
        whole((length, HEAD_DIMENSION)),
        whole((length, HEAD_DIMENSION)),
        whole((8, length)),
    ]


def columns_spec(length, width):
    return pl.BlockSpec((length, width), lambda n: (0, n))


def attention_forward(qkv, gains, cos, sin, earliest):
    length, width = qkv.shape
    heads = width // HEAD_SET
    return pl.pallas_call(
        functools.partial(forward_kernel, 256),
        grid=(heads,),
        in_specs=[columns_spec(length, HEAD_SET)] + per_head_specs(length),
        out_specs=columns_spec(length, GROUP * HEAD_DIMENSION),
        out_shape=jax.ShapeDtypeStruct((length, heads * GROUP * HEAD_DIMENSION), BF16),
        compiler_params=pltpu.CompilerParams(vmem_limit_bytes=48 << 20),
        cost_estimate=CHEAP,
    )(qkv, gains, cos, sin, earliest)


def attention_backward(qkv, dout, gains, cos, sin, earliest):
    length, width = qkv.shape
    heads = width // HEAD_SET
    return pl.pallas_call(
        functools.partial(backward_kernel, 256),
        grid=(heads,),
        in_specs=[columns_spec(length, HEAD_SET), columns_spec(length, GROUP * HEAD_DIMENSION)]
        + per_head_specs(length),
        out_specs=[
            columns_spec(length, HEAD_SET),
            pl.BlockSpec((1, 8, HEAD_DIMENSION), lambda n: (n, 0, 0)),
        ],
        out_shape=[
            jax.ShapeDtypeStruct((length, width), BF16),
            jax.ShapeDtypeStruct((heads, 8, HEAD_DIMENSION), F32),
        ],
        scratch_shapes=[pltpu.VMEM((length, HEAD_DIMENSION), F32)] * 2,
        compiler_params=pltpu.CompilerParams(vmem_limit_bytes=48 << 20),
        cost_estimate=CHEAP,
    )(qkv, dout, gains, cos, sin, earliest)


def hidden_kernel(pre_ref, grad_ref, down_ref, hidden_ref, dpre_ref):
    tile = hidden_ref.shape[1]
    grad_hidden = stacked_dot(grad_ref, down_ref)
    step = 128
    for start in range(0, hidden_ref.shape[0], step):
        rows = slice(start, start + step)
        gate, up, grad = pre_ref[rows, :tile], pre_ref[rows, tile:], grad_hidden[rows]
        sig = 1.0 / (1.0 + jnp.exp(-gate))
        act = gate * sig
        hidden_ref[rows] = (act * up).astype(BF16)
        dpre_ref[rows, :tile] = (grad * up * sig * (1.0 + gate * (1.0 - sig))).astype(BF16)
        dpre_ref[rows, tile:] = (grad * act).astype(BF16)


def hidden_layer(pre, grad, down, tiles):
    rows, width = grad.shape
    tile = down.shape[3] // tiles
    step = min(rows, 1024)
    return pl.pallas_call(
        hidden_kernel,
        grid=(tiles, rows // step),
        in_specs=[
            pl.BlockSpec((step, 2 * tile), lambda j, i: (i, j)),
            pl.BlockSpec((step, width), lambda j, i: (i, 0)),
            pl.BlockSpec(down.shape[:3] + (tile,), lambda j, i: (0, 0, 0, j)),
        ],
        out_specs=[
            pl.BlockSpec((step, tile), lambda j, i: (i, j)),
            pl.BlockSpec((step, 2 * tile), lambda j, i: (i, j)),
        ],
        out_shape=[
            jax.ShapeDtypeStruct((rows, tile * tiles), BF16),
            jax.ShapeDtypeStruct((rows, 2 * tile * tiles), BF16),
        ],
        compiler_params=pltpu.CompilerParams(vmem_limit_bytes=56 << 20),
        cost_estimate=CHEAP,
    )(pre, grad, down)


def tie(*items):
    return lax.optimization_barrier(items)


def swap(x, axis, bit):
    return lax.ppermute(x, axis, [(i, i ^ bit) for i in range(lax.axis_size(axis))])


def sequence_steps(blocks, together):
    half, part, parts = lax.axis_index("h"), lax.axis_index("t"), lax.axis_size("t")
    block = blocks.shape[1]
    own = lax.dynamic_index_in_dim(blocks, half, 0, keepdims=True)
    got = swap(lax.dynamic_index_in_dim(blocks, 1 - half, 0, keepdims=True), "h", 1)
    if not together:
        own_first, got = tie(swap(own, "t", parts // 2), got)
    got = yield got
    if together:
        starts = [(jnp.concatenate([own, got], axis=0), [0, parts])]
    else:
        starts = [(own, [0]), (got, [parts])]
    placed = []
    for first, keys in starts:
        held = [first]
        bit = parts // 2
        while bit:
            if together:
                for piece in list(held):
                    got = yield swap(piece, "t", bit)
                    held.append(got)
            else:
                if first is own and len(held) == 1:
                    got = yield own_first
                else:
                    got = yield swap(jnp.concatenate(held, axis=0) if len(held) > 1 else first, "t", bit)
                held.append(got)
            keys = keys + [k | bit for k in keys]
            bit //= 2
        flat = [piece[i] for piece in held for i in range(piece.shape[0])]
        placed += [(b, ((half * parts + part) ^ k) * block) for b, k in zip(flat, keys)]
    return placed


def run_steps(steps, ties):
    number, arrived = 0, next(steps)
    while True:
        try:
            arrived = steps.send(ties[number](arrived) if number in ties else arrived)
        except StopIteration as end:
            return end.value
        number += 1


def assemble(placed, columns=slice(None), out=None):
    rows = sum(part.shape[0] for part, _ in placed)
    if out is None:
        out = blank((rows, placed[0][0][:, columns].shape[1]), placed[0][0].dtype)
    for part, start in placed:
        out = lax.dynamic_update_slice_in_dim(out, part[:, columns], start, 0)
    return out


def to_blocks(partial, early=(), late=()):
    half, part, parts = lax.axis_index("h"), lax.axis_index("t"), lax.axis_size("t")
    both = partial.reshape(2, parts, -1, partial.shape[1])
    held = [lax.dynamic_index_in_dim(both, part ^ key, 1, keepdims=False) for key in range(parts)]

    def pick(x, h):
        return lax.dynamic_index_in_dim(x, h, 0, keepdims=False)

    bit = 1
    while 2 * bit < parts:
        keys = [key for key in range(parts) if held[key] is not None and key & bit]
        got = swap(jnp.stack([held[key].astype(BF16) for key in keys]), "t", bit)
        for n, key in enumerate(keys):
            held[key ^ bit] = held[key ^ bit].astype(F32) + got[n].astype(F32)
            held[key] = None
        bit *= 2
    far = pick(held[0], 1 - half).astype(F32) + swap(pick(held[bit], 1 - half).astype(BF16), "t", bit).astype(F32)
    far, near = tie(far.astype(BF16), pick(held[bit], half).astype(BF16))
    got = swap(far, "h", 1).astype(F32)
    own = pick(held[0], half).astype(F32) + swap(near, "t", bit).astype(F32)
    own, early = tie(own, list(early))
    got, own, late = tie(got, own, list(late(early) if callable(late) else late))
    return jnp.where(half == 0, jnp.stack([own, got]), jnp.stack([got, own])), early, late


def swaps(pieces, axis="dp"):
    return [pieces[0]] + list(reversed([swap(pieces[s], axis, s) for s in reversed(range(1, len(pieces)))]))


def gather_h(x):
    return [x, swap(x, "h", 1)]


def block_places():
    dp, half, count = lax.axis_index("dp"), lax.axis_index("h"), lax.axis_size("dp")
    return jnp.stack([(dp ^ s) * 2 + (half ^ k) for k in (0, 1) for s in range(count)]).astype(jnp.int32)


def blank(shape, dtype):
    return pl.pallas_call(
        lambda out_ref: None,
        out_specs=pl.BlockSpec(memory_space=pl.ANY),
        out_shape=jax.ShapeDtypeStruct(shape, dtype),
    )()


def place_rows(blocks, places):
    rows, width = blocks[0].shape
    out = blank((len(blocks) * rows, width), blocks[0].dtype)
    for k, part in enumerate(blocks):
        out = lax.dynamic_update_slice_in_dim(out, part, places[k] * rows, 0)
    return out


def sum_h(got):
    half = lax.axis_index("h")
    total = sum(g.astype(F32) for g in got)
    total = total.reshape(2, total.shape[0] // 2, -1)
    give = lax.dynamic_index_in_dim(total, 1 - half, 0, keepdims=False).astype(BF16)
    return lax.dynamic_index_in_dim(total, half, 0, keepdims=False), give


def total_over(x, axis):
    bit = 1
    while bit < lax.axis_size(axis):
        x = x + swap(x, axis, bit)
        bit *= 2
    return x


def per_device(
    tokens,
    positions,
    attn_norm,
    query_proj,
    key_projected,
    value_projected,
    head_norms,
    out_proj,
    mlp_norm,
    gate_proj,
    up_proj,
    down_proj,
    out_grad,
):
    block, seqs, width = tokens.shape
    rows = block * seqs
    dp = lax.axis_size("dp")
    parts = lax.axis_size("t")
    ctx = 2 * parts
    length = block * ctx
    depth = query_proj.shape[0]
    part = lax.axis_index("t")
    attn_gain = attn_norm.astype(F32)[:, None]
    mlp_gain = mlp_norm.astype(F32)[:, None]

    inputs = jnp.transpose(tokens, (1, 0, 2)).astype(F32)
    factor_one = norm_factor(inputs)
    digits = jnp.stack([positions.T // 16, positions.T % 16], axis=2).astype(BF16)
    digits = jnp.pad(digits, ((0, 0), (0, 0), (0, HEAD_DIMENSION - 2)))
    own_one = jnp.concatenate([(inputs * factor_one).astype(BF16), digits], axis=2)
    own_one, query_proj, gate_proj = tie(own_one, query_proj, gate_proj)

    heads = KEY_VALUE_HEADS // parts
    pair = GROUP * HEAD_DIMENSION
    qkv_width, mix_width = heads * HEAD_SET, heads * pair
    attn_width = qkv_width + mix_width

    dp_index = lax.axis_index("dp")
    attn_set = whole(
        functools.partial(attn_split_kernel, heads),
        [jax.ShapeDtypeStruct((depth, attn_width), BF16)] * parts,
        part,
        attn_gain,
        query_proj,
        key_projected,
        value_projected,
        out_proj,
    )
    attn_set, gate_proj = tie(attn_set, gate_proj)

    hidden = gate_proj.shape[1] // dp
    tiles = 3
    ffn_set = whole(
        functools.partial(ffn_split_kernel, tiles),
        [jax.ShapeDtypeStruct((depth, 3 * hidden), BF16)] * dp,
        dp_index,
        mlp_gain,
        gate_proj,
        up_proj,
        down_proj,
    )

    def swap_h(x):
        return swap(x, "h", 1)

    def swap_dp(x, keys):
        return [swap(x[k] if isinstance(x, (list, tuple)) else x, "dp", k) for k in keys]

    near, far = range(1, dp - 1), range(dp - 1, dp)
    bits = parts.bit_length() - 1
    hold = {}

    def first_step(x):
        x, got, ffn_near = tie(x, swaps(attn_set, "t"), swap_dp(ffn_set, near))
        qkv_rows, out_rows = rows_join(got, qkv_width, part)
        hold.update(qkv=qkv_rows, out=out_rows, ffn_near=ffn_near)
        return x

    def second_step(x):
        x, qkv_h, ffn_far, qkv_near, out_h = tie(
            x,
            swap_h(hold["qkv"]),
            swap_dp(ffn_set, far),
            swap_dp(hold["qkv"], near),
            swap_h(hold["out"]),
        )
        hold.update(qkv_h=qkv_h, ffn_far=ffn_far, qkv_near=qkv_near, out_h=out_h)
        return x

    def third_step(x):
        x, qkv_far, qkv_h_got = tie(
            x, swap_dp(hold["qkv"], far), swap_dp(hold["qkv_h"], range(1, dp))
        )
        hold.update(qkv_far=qkv_far, qkv_h_got=qkv_h_got)
        return x

    placed = run_steps(sequence_steps(own_one, True), {0: first_step, 1: second_step, parts - 1: third_step})
    normed_one = assemble(placed, slice(0, width))
    places = assemble(placed, slice(width, width + HEAD_DIMENSION))[:, :2].astype(jnp.int32)
    places = places[:, 0] * 16 + places[:, 1]
    normed_one, out_rows = tie(normed_one, hold["out"])
    qkv_blocks = [hold["qkv"], *hold["qkv_near"], *hold["qkv_far"], hold["qkv_h"], *hold["qkv_h_got"]]
    block_at = block_places()
    ffn_got = [ffn_set[0], *hold["ffn_near"], *hold["ffn_far"]]
    pre_rows, down_rows = rows_join(ffn_got, 2 * hidden, dp_index)

    def ffn_gather(x):
        return lax.all_gather(x, ("h", "t"), axis=0, tiled=False).reshape(ctx, dp, depth, -1)

    pre_weight = ffn_gather(pre_rows)

    def ffn_scatter(term):
        return lax.psum_scatter(term, ("h", "t"), scatter_dimension=0, tiled=True).reshape(dp, depth, -1)

    gains = head_norms.astype(F32)
    half_width = HEAD_DIMENSION // 2
    frequency = theta_base ** (-(jnp.arange(half_width, dtype=F32) * 2.0 / HEAD_DIMENSION))
    angles = places.astype(F32)[:, None] * frequency
    cos, sin = jnp.cos(angles), jnp.sin(angles)
    cos = jnp.concatenate([cos, cos], axis=1)
    sin = jnp.concatenate([-sin, sin], axis=1)
    earliest = jnp.broadcast_to((jnp.arange(length, dtype=jnp.int32) - places)[None, :], (8, length))
    out_pair = jnp.concatenate([out_rows, hold["out_h"]], axis=0)
    qkv = blocks_product(normed_one, qkv_blocks, block_at, 256)
    grad_own = jnp.transpose(out_grad, (1, 0, 2)).reshape(rows, width)
    qkv, qkv_blocks, out_near, grad_own = tie(qkv, qkv_blocks, swap_dp(out_pair, near), grad_own)
    mixed = attention_forward(qkv, gains, cos, sin, earliest)
    mixed, out_far = tie(mixed, swap_dp(out_pair, far))
    out_pairs = [out_pair, *out_near, *out_far]
    out_blocks = [p[: parts * depth] for p in out_pairs] + [p[parts * depth :] for p in out_pairs]
    mixed_part = blocks_back(mixed, out_blocks, block_at, 2)
    mixed_part, out_blocks, qkv_blocks, early = tie(
        mixed_part, out_blocks, qkv_blocks, swap_dp(grad_own, range(1, 2))
    )
    qkv_weight, out_weight = place_rows(qkv_blocks, block_at), place_rows(out_blocks, block_at)
    mixed_sum, _, (late, pre_weight, down_rows, qkv_weight, out_weight) = to_blocks(
        mixed_part, [], [swap_dp(grad_own, range(2, dp)), pre_weight, down_rows, qkv_weight, out_weight]
    )
    middle = (inputs + mixed_sum).reshape(rows, width)
    down_weight = ffn_gather(down_rows)

    factor_two = norm_factor(middle)
    own_two = (middle * factor_two).astype(BF16)
    normed_two = swaps([own_two] * dp)
    grad_rows = jnp.concatenate([grad_own, *early, *late], axis=0)
    normed_two = jnp.concatenate(normed_two, axis=0)
    pre = stacked_product(normed_two, pre_weight, hidden // 2)
    hidden_low, grad_pre = hidden_layer(pre, grad_rows, down_weight, tiles)
    down_term = term_product(grad_rows, hidden_low, dp, ctx)
    down_term, grad_pre = tie(down_term, grad_pre)
    down_sum = ffn_scatter(down_term)
    two_part = stacked_back(grad_pre, pre_weight, dp)
    grad_pre, two_part = tie(grad_pre, two_part)
    two_got = swaps(two_part)
    pre_term = term_product(normed_two, grad_pre, dp, ctx)
    branch_part = stacked_back(hidden_low, down_weight, dp)
    pre_term, branch_part, two_got = tie(pre_term, branch_part, two_got)
    grad_two = sum(g.astype(F32) for g in two_got)
    grad_middle = grad_own.astype(F32) + norm_back(middle, factor_two, grad_two)
    grad_mid_own = grad_middle.astype(BF16).reshape(seqs, block, width)
    grad_mid_own, grad_two = tie(grad_mid_own, grad_two)
    mlp_norm_sum = jnp.sum(middle * factor_two * grad_two, axis=0)

    def to_dp(x):
        return [lax.dynamic_index_in_dim(x, dp_index ^ k, 0, keepdims=False) for k in range(dp)]

    def near_step(x):
        x, hold["branch_near"] = tie(x, swap_dp(branch_part, near))
        return x

    def far_step(x):
        x, hold["branch_far"], hold["mlp_sum"] = tie(x, swap_dp(branch_part, far), mlp_norm_sum)
        return x

    placed = run_steps(sequence_steps(grad_mid_own, False), {bits + 1: near_step, 2 * bits: far_step})
    mlp_norm_sum = hold["mlp_sum"]
    grad_mid = assemble(placed, slice(None), normed_two)
    if PRE_LATE:
        grad_mid, pre_term = tie(grad_mid, pre_term)
    pre_sum = ffn_scatter(pre_term)
    grad_mixed = rows_product(grad_mid, out_weight, 0, 256, BF16)
    out_pieces = term_pieces(grad_mid, mixed, dp_index, dp)
    grad_mixed, out_pieces = tie(grad_mixed, out_pieces)
    grad_qkv, gain_terms = attention_backward(qkv, grad_mixed, gains, cos, sin, earliest)
    grad_qkv, out_got = tie(grad_qkv, swap_dp(out_pieces, range(1, dp)))
    out_keep, out_give = sum_h([out_pieces[0], *out_got])
    grad_qkv, out_give, down_give = tie(grad_qkv, out_give, to_dp(down_sum))
    grad_one_part, norm_sums = input_product(grad_qkv, qkv_weight, normed_one, mlp_norm_sum[None], 512)
    grad_qkv, grad_one_part = tie(grad_qkv, grad_one_part)

    qkv_pieces = term_pieces(normed_one, grad_qkv, dp_index, dp, norm_sums)
    head_sum = total_over(jnp.sum(gain_terms, axis=0)[:2], "dp")
    qkv_pieces, grad_one_part, out_h_got, head_sum, down_got = tie(
        qkv_pieces, grad_one_part, swap_h(out_give), head_sum, swaps(down_give)
    )
    out_sum = out_keep + out_h_got.astype(F32)
    qkv_got = swaps(qkv_pieces)

    def late_step(early):
        keep, hold["give"] = sum_h(early[0])
        return [keep]

    branch_got = [branch_part[0], *hold["branch_near"], *hold["branch_far"]]
    grad_one, (_, branch_got), (qkv_keep,) = to_blocks(grad_one_part, [qkv_got, branch_got], late_step)
    qkv_give = hold["give"]
    layer_out = (middle + sum(g.astype(F32) for g in branch_got)).astype(BF16)
    qkv_h_got = swap_h(qkv_give)
    qkv_h_got, head_sum = tie(qkv_h_got, head_sum)
    head_norm_grad = total_over(total_over(head_sum, "t"), "h")
    grad_one, pre_give = tie(grad_one, to_dp(pre_sum))
    pre_grad = swaps(pre_give)
    qkv_sum = qkv_keep + qkv_h_got.astype(F32)
    attn_sum = jnp.concatenate([qkv_sum, out_sum], axis=1).astype(BF16)
    attn_grad = swaps(
        [lax.dynamic_slice_in_dim(attn_sum, (part ^ k) * depth, depth, 0) for k in range(parts)], "t"
    )
    gate_grad, up_grad, down_grad = whole(
        functools.partial(ffn_join_kernel, tiles),
        [jax.ShapeDtypeStruct(gate_proj.shape, F32)] * 3,
        dp_index,
        mlp_gain,
        *pre_grad,
        *down_got,
    )
    input_grad = grad_middle.reshape(seqs, block, width) + norm_back(inputs, factor_one, grad_one)
    query_grad, key_grad, value_grad, out_proj_grad, norm_grads = whole(
        functools.partial(attn_join_kernel, heads),
        [
            jax.ShapeDtypeStruct(x.shape, F32)
            for x in (query_proj, key_projected, value_projected, out_proj, jnp.zeros((depth, HEAD_DIMENSION)))
        ],
        part,
        attn_gain,
        *attn_grad,
    )
    attn_norm_grad = norm_grads[:, 0] / attn_gain[:, 0]
    mlp_norm_grad = norm_grads[:, 1] / mlp_gain[:, 0]

    layer_out = jnp.transpose(layer_out.reshape(seqs, block, width), (1, 0, 2))
    input_grad = jnp.transpose(input_grad, (1, 0, 2))
    return (
        layer_out,
        input_grad,
        attn_norm_grad,
        query_grad,
        key_grad,
        value_grad,
        head_norm_grad,
        out_proj_grad,
        mlp_norm_grad,
        gate_grad,
        up_grad,
        down_grad,
    )


def solution(mesh):
    dp, ctx = mesh.shape["dp"], mesh.shape["ctx"]
    fine = Mesh(mesh.devices.reshape(dp, 2, ctx // 2), ("dp", "h", "t"))
    acts = P(("h", "t"), "dp", None)
    rows = P(("dp", "h", "t"), None)
    gain = P(("dp", "h", "t"))
    in_specs = (
        acts,
        P(("h", "t"), "dp"),
        gain,
        rows,
        rows,
        rows,
        P(),
        rows,
        gain,
        rows,
        rows,
        rows,
        acts,
    )
    out_specs = (acts, acts, gain, rows, rows, rows, P(), rows, gain, rows, rows, rows)
    return jax.shard_map(per_device, mesh=fine, in_specs=in_specs, out_specs=out_specs, check_vma=False)
```

```python
import functools

import jax
import jax.numpy as jnp
from jax import lax
from jax.experimental import pallas as pl
from jax.experimental.pallas import tpu as pltpu
from jax.sharding import Mesh
from jax.sharding import PartitionSpec as P

QUERY_HEADS = 16
KEY_VALUE_HEADS = 8
HEAD_DIMENSION = 128
GROUP = QUERY_HEADS // KEY_VALUE_HEADS
HEAD_SET = (GROUP + 2) * HEAD_DIMENSION

epsilon = 1e-06
theta_base = 1000000.0
score_scaling = HEAD_DIMENSION ** (-0.5)
F32 = jnp.float32
BF16 = jnp.bfloat16


def norm_factor(matrix):
    return lax.rsqrt(jnp.mean(matrix * matrix, axis=-1, keepdims=True) + epsilon)


def norm_back(matrix, factor, upstream):
    return factor * upstream - matrix * (factor * factor * factor) * jnp.mean(
        upstream * matrix, axis=-1, keepdims=True
    )


def dot(a, b, ca=1, cb=0):
    return lax.dot_general(a, b, (((ca,), (cb,)), ((), ())), preferred_element_type=F32)


PRE_LATE = True
CHEAP = pl.CostEstimate(flops=1 << 20, bytes_accessed=1 << 16, transcendentals=0)


def rows_kernel(contract, a_ref, b_ref, *out_refs):
    out = dot(a_ref[...], b_ref[...], 1, contract).astype(out_refs[0].dtype)
    step = out_refs[0].shape[0]
    for k, out_ref in enumerate(out_refs):
        out_ref[...] = out[k * step : (k + 1) * step]


def rows_product(a, b, contract, tile, dtype, pieces=1):
    rows, depth = a.shape
    columns = b.shape[1 - contract]
    tile = min(tile, columns)
    out = pl.pallas_call(
        functools.partial(rows_kernel, contract),
        grid=(columns // tile,),
        in_specs=[
            pl.BlockSpec((rows, depth), lambda j: (0, 0)),
            pl.BlockSpec((depth, tile), lambda j: (0, j))
            if contract == 0
            else pl.BlockSpec((tile, depth), lambda j: (j, 0)),
        ],
        out_specs=[pl.BlockSpec((rows // pieces, tile), lambda j: (0, j))] * pieces,
        out_shape=[jax.ShapeDtypeStruct((rows // pieces, columns), dtype)] * pieces,
        compiler_params=pltpu.CompilerParams(vmem_limit_bytes=48 << 20),
        cost_estimate=CHEAP,
    )(a, b)
    return out if pieces > 1 else out[0]


def blocks_kernel(where_ref, a_ref, *refs):
    w_refs, out_ref = refs[:-1], refs[-1]
    depth = w_refs[0].shape[0]
    total = None
    for k, w_ref in enumerate(w_refs):
        start = pl.multiple_of(where_ref[k] * depth, HEAD_DIMENSION)
        part = dot(a_ref[:, pl.ds(start, depth)], w_ref[...])
        total = part if total is None else total + part
    out_ref[...] = total


def blocks_product(a, w_blocks, where, tile):
    rows, depth = a.shape
    columns = w_blocks[0].shape[1]
    return pl.pallas_call(
        blocks_kernel,
        grid_spec=pltpu.PrefetchScalarGridSpec(
            num_scalar_prefetch=1,
            grid=(columns // tile,),
            in_specs=[pl.BlockSpec((rows, depth), lambda j, where: (0, 0))]
            + [pl.BlockSpec((w.shape[0], tile), lambda j, where: (0, j)) for w in w_blocks],
            out_specs=pl.BlockSpec((rows, tile), lambda j, where: (0, j)),
        ),
        out_shape=jax.ShapeDtypeStruct((rows, columns), F32),
        compiler_params=pltpu.CompilerParams(vmem_limit_bytes=48 << 20),
        cost_estimate=CHEAP,
    )(where, a, *w_blocks)


def blocks_back_kernel(where_ref, a_ref, *refs):
    w_refs, out_ref = refs[:-1], refs[-1]
    depth = w_refs[0].shape[0]
    for k, w_ref in enumerate(w_refs):
        start = pl.multiple_of(where_ref[k] * depth, HEAD_DIMENSION)
        out_ref[:, pl.ds(start, depth)] = dot(a_ref[...], w_ref[...], 1, 1).astype(BF16)


def blocks_back(a, w_blocks, where, pieces):
    rows, depth = a.shape
    columns = sum(w.shape[0] for w in w_blocks)
    return pl.pallas_call(
        blocks_back_kernel,
        grid_spec=pltpu.PrefetchScalarGridSpec(
            num_scalar_prefetch=1,
            grid=(pieces,),
            in_specs=[pl.BlockSpec((rows // pieces, depth), lambda j, where: (j, 0))]
            + [pl.BlockSpec(w.shape, lambda j, where: (0, 0)) for w in w_blocks],
            out_specs=pl.BlockSpec((rows // pieces, columns), lambda j, where: (j, 0)),
        ),
        out_shape=jax.ShapeDtypeStruct((rows, columns), BF16),
        compiler_params=pltpu.CompilerParams(vmem_limit_bytes=48 << 20),
        cost_estimate=CHEAP,
    )(where, a, *w_blocks)


def stacked_kernel(a_ref, w_ref, out_ref):
    out_ref[...] = stacked_dot(a_ref, w_ref).astype(out_ref.dtype)


def stacked_dot(a_ref, w_ref):
    blocks, groups, depth, columns = w_ref.shape
    step = blocks * depth
    total = None
    for d in range(groups):
        part = dot(a_ref[:, d * step : (d + 1) * step], w_ref[:, d].reshape(step, columns))
        total = part if total is None else total + part
    return total


def stacked_product(a, w, tile):
    rows, depth = a.shape
    columns = w.shape[3]
    return pl.pallas_call(
        stacked_kernel,
        grid=(columns // tile,),
        in_specs=[
            pl.BlockSpec((rows, depth), lambda j: (0, 0)),
            pl.BlockSpec(w.shape[:3] + (tile,), lambda j: (0, 0, 0, j)),
        ],
        out_specs=pl.BlockSpec((rows, tile), lambda j: (0, j)),
        out_shape=jax.ShapeDtypeStruct((rows, columns), F32),
        compiler_params=pltpu.CompilerParams(vmem_limit_bytes=56 << 20),
        cost_estimate=CHEAP,
    )(a, w)


def stacked_back_kernel(a_ref, w_ref, *out_refs):
    blocks, _, depth, columns = w_ref.shape
    out = dot(a_ref[...], w_ref[:, 0].reshape(blocks * depth, columns), 1, 1).astype(BF16)
    step = out_refs[0].shape[0]
    for k, out_ref in enumerate(out_refs):
        out_ref[...] = out[k * step : (k + 1) * step]


def stacked_back(a, w, pieces):
    rows, depth = a.shape
    blocks, groups, n, columns = w.shape
    step = blocks * n
    return pl.pallas_call(
        stacked_back_kernel,
        grid=(groups,),
        in_specs=[
            pl.BlockSpec((rows, depth), lambda j: (0, 0)),
            pl.BlockSpec((blocks, 1, n, columns), lambda j: (0, j, 0, 0)),
        ],
        out_specs=[pl.BlockSpec((rows // pieces, step), lambda j: (0, j))] * pieces,
        out_shape=[jax.ShapeDtypeStruct((rows // pieces, groups * step), BF16)] * pieces,
        compiler_params=pltpu.CompilerParams(vmem_limit_bytes=56 << 20),
        cost_estimate=CHEAP,
    )(a, w)


def term_kernel(a_ref, b_ref, out_ref):
    out_ref[...] = dot(a_ref[...], b_ref[...], 0, 0).astype(BF16).reshape(out_ref.shape)


def term_product(a, b, groups, blocks):
    rows, width = a.shape
    columns = b.shape[1]
    depth = width // (groups * blocks)
    return pl.pallas_call(
        term_kernel,
        grid=(groups,),
        in_specs=[
            pl.BlockSpec((rows, blocks * depth), lambda i: (0, i)),
            pl.BlockSpec((rows, columns), lambda i: (0, 0)),
        ],
        out_specs=pl.BlockSpec((blocks, 1, depth, columns), lambda i: (0, i, 0, 0)),
        out_shape=jax.ShapeDtypeStruct((blocks, groups, depth, columns), BF16),
        compiler_params=pltpu.CompilerParams(vmem_limit_bytes=56 << 20),
        cost_estimate=CHEAP,
    )(a, b).reshape(width, columns)


def pieces_kernel(me_ref, a_ref, b_ref, *refs):
    norm_ref, out_refs = (refs[0], refs[1:]) if refs[0].shape[0] == 8 else (None, refs)
    wide = b_ref.shape[1]
    part = dot(a_ref[...], b_ref[...], 0, 0).astype(BF16)
    for s, out_ref in enumerate(out_refs):

        @pl.when(pl.program_id(0) == s)
        def _():
            out_ref[:, :wide] = part
            if norm_ref is not None:
                sums = norm_ref[...].T
                rest = jnp.zeros((sums.shape[0], HEAD_DIMENSION - 8), F32)
                out_ref[:, wide:] = jnp.concatenate([sums, rest], axis=1).astype(BF16)


def term_pieces(a, b, me, count, norms=None):
    rows, width = a.shape
    columns = b.shape[1]
    step = width // count
    extra = 0 if norms is None else HEAD_DIMENSION
    in_specs = [
        pl.BlockSpec((rows, step), lambda i, me: (0, me[0] ^ i)),
        pl.BlockSpec((rows, columns), lambda i, me: (0, 0)),
    ]
    if norms is not None:
        in_specs.append(pl.BlockSpec((8, step), lambda i, me: (0, me[0] ^ i)))
    return pl.pallas_call(
        pieces_kernel,
        grid_spec=pltpu.PrefetchScalarGridSpec(
            num_scalar_prefetch=1,
            grid=(count,),
            in_specs=in_specs,
            out_specs=[pl.BlockSpec((step, columns + extra), lambda i, me: (0, 0))] * count,
        ),
        out_shape=[jax.ShapeDtypeStruct((step, columns + extra), BF16)] * count,
        compiler_params=pltpu.CompilerParams(vmem_limit_bytes=56 << 20),
        cost_estimate=CHEAP,
    )(me.reshape(1).astype(jnp.int32), a, b, *([] if norms is None else [norms]))


def input_kernel(grad_ref, weight_ref, normed_ref, other_ref, out_ref, sum_ref):
    part = dot(grad_ref[...], weight_ref[...], 1, 1)
    out_ref[...] = part.astype(BF16)
    sum_ref[...] = jnp.zeros_like(sum_ref)
    sum_ref[0:1] = jnp.sum(normed_ref[...].astype(F32) * part, axis=0, keepdims=True)
    sum_ref[1:2] = other_ref[...]


def input_product(grad, weight, normed, other, tile):
    rows, depth = grad.shape
    columns = weight.shape[0]
    return pl.pallas_call(
        input_kernel,
        grid=(columns // tile,),
        in_specs=[
            pl.BlockSpec((rows, depth), lambda j: (0, 0)),
            pl.BlockSpec((tile, depth), lambda j: (j, 0)),
            pl.BlockSpec((rows, tile), lambda j: (0, j)),
            pl.BlockSpec((1, tile), lambda j: (0, j)),
        ],
        out_specs=[pl.BlockSpec((rows, tile), lambda j: (0, j)), pl.BlockSpec((8, tile), lambda j: (0, j))],
        out_shape=[jax.ShapeDtypeStruct((rows, columns), BF16), jax.ShapeDtypeStruct((8, columns), F32)],
        compiler_params=pltpu.CompilerParams(vmem_limit_bytes=48 << 20),
        cost_estimate=CHEAP,
    )(grad, weight, normed, other)


def whole(kernel, shapes, me, *arrays, seen=()):
    vmem = pl.BlockSpec(memory_space=pltpu.VMEM)

    def body(me_ref, *refs):
        kernel(me_ref, *refs[: len(arrays)], *refs[len(arrays) + len(seen) :])

    return pl.pallas_call(
        body,
        in_specs=[pl.BlockSpec(memory_space=pltpu.SMEM)]
        + [vmem] * len(arrays)
        + [pl.BlockSpec(memory_space=pl.ANY)] * len(seen),
        out_specs=[vmem] * len(shapes),
        out_shape=shapes,
        compiler_params=pltpu.CompilerParams(vmem_limit_bytes=48 << 20),
        cost_estimate=CHEAP,
    )(me.reshape(1).astype(jnp.int32), *arrays, *seen)


def lanes(index, size):
    return pl.ds(pl.multiple_of(index * size, HEAD_DIMENSION), size)


def attn_split_kernel(heads, me_ref, gain_ref, q_ref, k_ref, v_ref, o_ref, *out_refs):
    pair = GROUP * HEAD_DIMENSION
    gain = gain_ref[...]

    def scaled(ref, index, size):
        return (ref[:, lanes(index, size)].astype(F32) * gain).astype(BF16)

    for s, out_ref in enumerate(out_refs):
        part = me_ref[0] ^ s
        for n in range(heads):
            head, at = part * heads + n, n * HEAD_SET
            out_ref[:, at : at + pair] = scaled(q_ref, head, pair)
            out_ref[:, at + pair : at + pair + HEAD_DIMENSION] = scaled(k_ref, head, HEAD_DIMENSION)
            out_ref[:, at + pair + HEAD_DIMENSION : at + HEAD_SET] = scaled(v_ref, head, HEAD_DIMENSION)
        out_ref[:, heads * HEAD_SET :] = o_ref[:, lanes(part, heads * pair)]


def attn_join_kernel(heads, me_ref, gain_ref, *refs):
    count = len(refs) - 5
    q_ref, k_ref, v_ref, o_ref, norm_ref = refs[count:]
    pair = GROUP * HEAD_DIMENSION
    gain = gain_ref[...]
    norms = jnp.zeros(norm_ref.shape, F32)
    for s, got_ref in enumerate(refs[:count]):
        part = me_ref[0] ^ s
        for n in range(heads):
            head, at = part * heads + n, n * HEAD_SET
            q_ref[:, lanes(head, pair)] = got_ref[:, at : at + pair].astype(F32) * gain
            k_ref[:, lanes(head, HEAD_DIMENSION)] = (
                got_ref[:, at + pair : at + pair + HEAD_DIMENSION].astype(F32) * gain
            )
            v_ref[:, lanes(head, HEAD_DIMENSION)] = (
                got_ref[:, at + pair + HEAD_DIMENSION : at + HEAD_SET].astype(F32) * gain
            )
        norms += got_ref[:, heads * HEAD_SET : heads * HEAD_SET + HEAD_DIMENSION].astype(F32)
        o_ref[:, lanes(part, heads * pair)] = got_ref[:, heads * HEAD_SET + HEAD_DIMENSION :].astype(F32)
    norm_ref[...] = norms


def ffn_split_kernel(tiles, me_ref, gain_ref, gate_ref, up_ref, down_ref, *out_refs):
    gain = gain_ref[...]
    hidden = out_refs[0].shape[1] // 3
    tile = hidden // tiles
    for s, out_ref in enumerate(out_refs):
        part = me_ref[0] ^ s
        for n in range(tiles):
            for k, ref in enumerate((gate_ref, up_ref)):
                at = (2 * n + k) * tile
                out_ref[:, at : at + tile] = (ref[:, lanes(part * tiles + n, tile)].astype(F32) * gain).astype(
                    BF16
                )
        out_ref[:, 2 * hidden :] = down_ref[:, lanes(part, hidden)]


def ffn_join_kernel(tiles, me_ref, gain_ref, *refs):
    count = (len(refs) - 3) // 2
    gate_ref, up_ref, down_ref = refs[2 * count :]
    gain = gain_ref[...]
    hidden = refs[0].shape[1] // 2
    tile = hidden // tiles
    for s, (got_ref, down_got_ref) in enumerate(zip(refs[:count], refs[count:])):
        part = me_ref[0] ^ s
        for n in range(tiles):
            for k, ref in enumerate((gate_ref, up_ref)):
                at = (2 * n + k) * tile
                ref[:, lanes(part * tiles + n, tile)] = got_ref[:, at : at + tile].astype(F32) * gain
        down_ref[:, lanes(part, hidden)] = down_got_ref[...].astype(F32)


def rows_join_kernel(me_ref, *refs):
    first_ref, second_ref = refs[-2:]
    depth = refs[0].shape[0]
    wide = first_ref.shape[1]
    for s, got_ref in enumerate(refs[:-2]):
        rows = pl.ds(pl.multiple_of((me_ref[0] ^ s) * depth, depth), depth)
        first_ref[rows] = got_ref[:, :wide]
        second_ref[rows] = got_ref[:, wide:]


def rows_join(got, wide, me):
    depth, width = got[0].shape
    return whole(
        rows_join_kernel,
        [jax.ShapeDtypeStruct((len(got) * depth, n), BF16) for n in (wide, width - wide)],
        me,
        *got,
    )


def rotate(x, cos, sin):
    return x * cos + pltpu.roll(x, HEAD_DIMENSION // 2, 1) * sin


def head_slice(i):
    return slice(i * HEAD_DIMENSION, (i + 1) * HEAD_DIMENSION)


def normed_rotated(raw, gain, cos, sin):
    return rotate(raw * norm_factor(raw) * gain, cos, sin).astype(BF16)


def probabilities(keys, queries, first_query, earliest):
    scores = dot(keys, queries, 1, 1) * score_scaling
    key_index = lax.broadcasted_iota(jnp.int32, scores.shape, 0)
    query_index = lax.broadcasted_iota(jnp.int32, scores.shape, 1) + first_query
    allowed = (key_index <= query_index) & (key_index >= earliest)
    masked = jnp.where(allowed, scores, -1e30)
    shifted = jnp.exp(masked - jnp.max(masked, axis=0, keepdims=True))
    return shifted * (1.0 / jnp.sum(shifted, axis=0, keepdims=True))


def forward_kernel(block, qkv_ref, gain_ref, cos_ref, sin_ref, early_ref, out_ref):
    length = qkv_ref.shape[0]
    gains = gain_ref[...]
    cos, sin = cos_ref[...], sin_ref[...]
    keys = normed_rotated(qkv_ref[:, head_slice(GROUP)], gains[1:2], cos, sin)
    values_t = qkv_ref[:, head_slice(GROUP + 1)].T.astype(BF16)
    for i in range(length // block):
        rows = slice(i * block, (i + 1) * block)
        seen = (i + 1) * block
        for g in range(GROUP):
            queries = normed_rotated(qkv_ref[rows, head_slice(g)], gains[0:1], cos[rows], sin[rows])
            probs = probabilities(keys[:seen], queries, i * block, early_ref[0:1, rows]).astype(BF16)
            mixed = dot(values_t[:, :seen], probs)
            out_ref[rows, head_slice(g)] = mixed.T.astype(BF16)


def backward_kernel(
    block, qkv_ref, dout_ref, gain_ref, cos_ref, sin_ref, early_ref, dqkv_ref, dgain_ref, dkey_ref, dvalue_ref
):
    length = qkv_ref.shape[0]
    gains = gain_ref[...]
    cos, sin = cos_ref[...], sin_ref[...]
    key_raw = qkv_ref[:, head_slice(GROUP)]
    keys = normed_rotated(key_raw, gains[1:2], cos, sin)
    keys_t = keys.astype(F32).T.astype(BF16)
    values = qkv_ref[:, head_slice(GROUP + 1)].astype(BF16)
    dkey_ref[...] = jnp.zeros_like(dkey_ref)
    dvalue_ref[...] = jnp.zeros_like(dvalue_ref)
    query_gain_sum = jnp.zeros((1, HEAD_DIMENSION), F32)
    for i in range(length // block):
        rows = slice(i * block, (i + 1) * block)
        seen = (i + 1) * block
        for g in range(GROUP):
            query_raw = qkv_ref[rows, head_slice(g)]
            queries = normed_rotated(query_raw, gains[0:1], cos[rows], sin[rows])
            dout = dout_ref[rows, head_slice(g)]
            probs = probabilities(keys[:seen], queries, i * block, early_ref[0:1, rows])
            dprobs = dot(values[:seen], dout, 1, 1)
            delta = jnp.sum(probs * dprobs, axis=0, keepdims=True)
            dscores = (probs * (dprobs - delta)).astype(BF16)
            dkey_ref[:seen] += dot(dscores, queries)
            dvalue_ref[:seen] += dot(probs.astype(BF16), dout)
            dquery = dot(keys_t[:, :seen], dscores).T * score_scaling
            dquery = rotate(dquery, cos[rows], -sin[rows])
            factor = norm_factor(query_raw)
            query_gain_sum += jnp.sum(query_raw * factor * dquery, axis=0, keepdims=True)
            dqkv_ref[rows, head_slice(g)] = norm_back(query_raw, factor, dquery * gains[0:1]).astype(BF16)
    dkey = rotate(dkey_ref[...] * score_scaling, cos, -sin)
    factor = norm_factor(key_raw)
    dgain_ref[0, 0:1, :] = query_gain_sum
    dgain_ref[0, 1:2, :] = jnp.sum(key_raw * factor * dkey, axis=0, keepdims=True)
    dgain_ref[0, 2:, :] = jnp.zeros((6, HEAD_DIMENSION), F32)
    dqkv_ref[:, head_slice(GROUP)] = norm_back(key_raw, factor, dkey * gains[1:2]).astype(BF16)
    dqkv_ref[:, head_slice(GROUP + 1)] = dvalue_ref[...].astype(BF16)


def per_head_specs(length):
    whole = lambda shape: pl.BlockSpec(shape, lambda n: (0,) * len(shape))
    return [
        whole((2, HEAD_DIMENSION)),
        whole((length, HEAD_DIMENSION)),
        whole((length, HEAD_DIMENSION)),
        whole((8, length)),
    ]


def columns_spec(length, width):
    return pl.BlockSpec((length, width), lambda n: (0, n))


def attention_forward(qkv, gains, cos, sin, earliest):
    length, width = qkv.shape
    heads = width // HEAD_SET
    return pl.pallas_call(
        functools.partial(forward_kernel, 256),
        grid=(heads,),
        in_specs=[columns_spec(length, HEAD_SET)] + per_head_specs(length),
        out_specs=columns_spec(length, GROUP * HEAD_DIMENSION),
        out_shape=jax.ShapeDtypeStruct((length, heads * GROUP * HEAD_DIMENSION), BF16),
        compiler_params=pltpu.CompilerParams(vmem_limit_bytes=48 << 20),
        cost_estimate=CHEAP,
    )(qkv, gains, cos, sin, earliest)


def attention_backward(qkv, dout, gains, cos, sin, earliest):
    length, width = qkv.shape
    heads = width // HEAD_SET
    return pl.pallas_call(
        functools.partial(backward_kernel, 256),
        grid=(heads,),
        in_specs=[columns_spec(length, HEAD_SET), columns_spec(length, GROUP * HEAD_DIMENSION)]
        + per_head_specs(length),
        out_specs=[
            columns_spec(length, HEAD_SET),
            pl.BlockSpec((1, 8, HEAD_DIMENSION), lambda n: (n, 0, 0)),
        ],
        out_shape=[
            jax.ShapeDtypeStruct((length, width), BF16),
            jax.ShapeDtypeStruct((heads, 8, HEAD_DIMENSION), F32),
        ],
        scratch_shapes=[pltpu.VMEM((length, HEAD_DIMENSION), F32)] * 2,
        compiler_params=pltpu.CompilerParams(vmem_limit_bytes=48 << 20),
        cost_estimate=CHEAP,
    )(qkv, dout, gains, cos, sin, earliest)


def hidden_kernel(pre_ref, grad_ref, down_ref, hidden_ref, dpre_ref):
    tile = hidden_ref.shape[1]
    grad_hidden = stacked_dot(grad_ref, down_ref)
    step = 128
    for start in range(0, hidden_ref.shape[0], step):
        rows = slice(start, start + step)
        gate, up, grad = pre_ref[rows, :tile], pre_ref[rows, tile:], grad_hidden[rows]
        sig = 1.0 / (1.0 + jnp.exp(-gate))
        act = gate * sig
        hidden_ref[rows] = (act * up).astype(BF16)
        dpre_ref[rows, :tile] = (grad * up * sig * (1.0 + gate * (1.0 - sig))).astype(BF16)
        dpre_ref[rows, tile:] = (grad * act).astype(BF16)


def hidden_layer(pre, grad, down, tiles):
    rows, width = grad.shape
    tile = down.shape[3] // tiles
    step = min(rows, 1024)
    return pl.pallas_call(
        hidden_kernel,
        grid=(tiles, rows // step),
        in_specs=[
            pl.BlockSpec((step, 2 * tile), lambda j, i: (i, j)),
            pl.BlockSpec((step, width), lambda j, i: (i, 0)),
            pl.BlockSpec(down.shape[:3] + (tile,), lambda j, i: (0, 0, 0, j)),
        ],
        out_specs=[
            pl.BlockSpec((step, tile), lambda j, i: (i, j)),
            pl.BlockSpec((step, 2 * tile), lambda j, i: (i, j)),
        ],
        out_shape=[
            jax.ShapeDtypeStruct((rows, tile * tiles), BF16),
            jax.ShapeDtypeStruct((rows, 2 * tile * tiles), BF16),
        ],
        compiler_params=pltpu.CompilerParams(vmem_limit_bytes=56 << 20),
        cost_estimate=CHEAP,
    )(pre, grad, down)


def tie(*items):
    return lax.optimization_barrier(items)


def swap(x, axis, bit):
    return lax.ppermute(x, axis, [(i, i ^ bit) for i in range(lax.axis_size(axis))])


def own_and_other(blocks):
    half = lax.axis_index("h")
    return [lax.dynamic_index_in_dim(blocks, k, 0, keepdims=True) for k in (half, 1 - half)]


def sequence_steps(own, give, together):
    half, part, parts = lax.axis_index("h"), lax.axis_index("t"), lax.axis_size("t")
    block = own.shape[1]
    got = swap(give, "h", 1)
    if not together:
        own_first, got = tie(swap(own, "t", parts // 2), got)
    got = yield got
    if together:
        starts = [(jnp.concatenate([own, got], axis=0), [0, parts])]
    else:
        starts = [(own, [0]), (got, [parts])]
    placed = []
    for first, keys in starts:
        held = [first]
        bit = parts // 2
        while bit:
            if together:
                for piece in list(held):
                    got = yield swap(piece, "t", bit)
                    held.append(got)
            else:
                if first is own and len(held) == 1:
                    got = yield own_first
                else:
                    got = yield swap(jnp.concatenate(held, axis=0) if len(held) > 1 else first, "t", bit)
                held.append(got)
            keys = keys + [k | bit for k in keys]
            bit //= 2
        flat = [piece[i] for piece in held for i in range(piece.shape[0])]
        placed += [(b, ((half * parts + part) ^ k) * block) for b, k in zip(flat, keys)]
    return placed


def run_steps(steps, ties):
    number, arrived = 0, next(steps)
    while True:
        try:
            arrived = steps.send(ties[number](arrived) if number in ties else arrived)
        except StopIteration as end:
            return end.value
        number += 1


def assemble(placed, columns=slice(None), out=None):
    rows = sum(part.shape[0] for part, _ in placed)
    if out is None:
        out = blank((rows, placed[0][0][:, columns].shape[1]), placed[0][0].dtype)
    for part, start in placed:
        out = lax.dynamic_update_slice_in_dim(out, part[:, columns], start, 0)
    return out


def to_blocks(partial, late=(), on_first=None, on_last=None):
    half, part, parts = lax.axis_index("h"), lax.axis_index("t"), lax.axis_size("t")
    both = partial.reshape(2, parts, -1, partial.shape[1])
    held = [lax.dynamic_index_in_dim(both, part ^ key, 1, keepdims=False) for key in range(parts)]

    def pick(x, h):
        return lax.dynamic_index_in_dim(x, h, 0, keepdims=False)

    bit = 1
    while 2 * bit < parts:
        keys = [key for key in range(parts) if held[key] is not None and key & bit]
        got = swap(jnp.stack([held[key].astype(BF16) for key in keys]), "t", bit)
        for n, key in enumerate(keys):
            held[key ^ bit] = held[key ^ bit].astype(F32) + got[n].astype(F32)
            held[key] = None
        bit *= 2
    first = swap(pick(held[bit], 1 - half).astype(BF16), "t", bit)
    if on_first is not None:
        on_first(first)
    far = pick(held[0], 1 - half).astype(F32) + first.astype(F32)
    far, near = tie(far.astype(BF16), pick(held[bit], half).astype(BF16))
    got = swap(far, "h", 1)
    if on_last is not None:
        got = on_last(got)
    own = pick(held[0], half).astype(F32) + swap(near, "t", bit).astype(F32)
    got, own, late = tie(got.astype(F32), own, list(late))
    return jnp.where(half == 0, jnp.stack([own, got]), jnp.stack([got, own])), late


def swaps(pieces, axis="dp"):
    return [pieces[0]] + list(reversed([swap(pieces[s], axis, s) for s in reversed(range(1, len(pieces)))]))


def gather_h(x):
    return [x, swap(x, "h", 1)]


def block_places():
    dp, half, count = lax.axis_index("dp"), lax.axis_index("h"), lax.axis_size("dp")
    return jnp.stack([(dp ^ s) * 2 + (half ^ k) for k in (0, 1) for s in range(count)]).astype(jnp.int32)


def blank(shape, dtype):
    return pl.pallas_call(
        lambda out_ref: None,
        out_specs=pl.BlockSpec(memory_space=pl.ANY),
        out_shape=jax.ShapeDtypeStruct(shape, dtype),
    )()


def place_rows(blocks, places):
    rows, width = blocks[0].shape
    out = blank((len(blocks) * rows, width), blocks[0].dtype)
    for k, part in enumerate(blocks):
        out = lax.dynamic_update_slice_in_dim(out, part, places[k] * rows, 0)
    return out


def sum_h(got):
    half = lax.axis_index("h")
    total = sum(g.astype(F32) for g in got)
    total = total.reshape(2, total.shape[0] // 2, -1)
    give = lax.dynamic_index_in_dim(total, 1 - half, 0, keepdims=False).astype(BF16)
    return lax.dynamic_index_in_dim(total, half, 0, keepdims=False), give


def total_over(x, axis):
    bit = 1
    while bit < lax.axis_size(axis):
        x = x + swap(x, axis, bit)
        bit *= 2
    return x


def per_device(
    tokens,
    positions,
    attn_norm,
    query_proj,
    key_projected,
    value_projected,
    head_norms,
    out_proj,
    mlp_norm,
    gate_proj,
    up_proj,
    down_proj,
    out_grad,
):
    block, seqs, width = tokens.shape
    rows = block * seqs
    dp = lax.axis_size("dp")
    parts = lax.axis_size("t")
    ctx = 2 * parts
    length = block * ctx
    depth = query_proj.shape[0]
    part = lax.axis_index("t")
    attn_gain = attn_norm.astype(F32)[:, None]
    mlp_gain = mlp_norm.astype(F32)[:, None]

    inputs = jnp.transpose(tokens, (1, 0, 2)).astype(F32)
    factor_one = norm_factor(inputs)
    digits = jnp.stack([positions.T // 16, positions.T % 16], axis=2).astype(BF16)
    digits = jnp.pad(digits, ((0, 0), (0, 0), (0, HEAD_DIMENSION - 2)))
    own_one = jnp.concatenate([(inputs * factor_one).astype(BF16), digits], axis=2)
    own_one, query_proj, gate_proj = tie(own_and_other(own_one), query_proj, gate_proj)

    heads = KEY_VALUE_HEADS // parts
    pair = GROUP * HEAD_DIMENSION
    qkv_width, mix_width = heads * HEAD_SET, heads * pair
    attn_width = qkv_width + mix_width

    dp_index = lax.axis_index("dp")
    attn_set = whole(
        functools.partial(attn_split_kernel, heads),
        [jax.ShapeDtypeStruct((depth, attn_width), BF16)] * parts,
        part,
        attn_gain,
        query_proj,
        key_projected,
        value_projected,
        out_proj,
    )
    attn_set, gate_proj = tie(attn_set, gate_proj)

    hidden = gate_proj.shape[1] // dp
    tiles = 3
    ffn_set = whole(
        functools.partial(ffn_split_kernel, tiles),
        [jax.ShapeDtypeStruct((depth, 3 * hidden), BF16)] * dp,
        dp_index,
        mlp_gain,
        gate_proj,
        up_proj,
        down_proj,
    )

    def swap_h(x):
        return swap(x, "h", 1)

    def swap_dp(x, keys):
        return [swap(x[k] if isinstance(x, (list, tuple)) else x, "dp", k) for k in keys]

    near, far = range(1, dp - 1), range(dp - 1, dp)
    bits = parts.bit_length() - 1
    hold = {}

    def first_step(x):
        x, got, ffn_near = tie(x, swaps(attn_set, "t"), swap_dp(ffn_set, near))
        qkv_rows, out_rows = rows_join(got, qkv_width, part)
        hold.update(qkv=qkv_rows, out=out_rows, ffn_near=ffn_near)
        return x

    def second_step(x):
        x, qkv_h, ffn_far, qkv_got, out_h = tie(
            x,
            swap_h(hold["qkv"]),
            swap_dp(ffn_set, far),
            swap_dp(hold["qkv"], range(1, dp)),
            swap_h(hold["out"]),
        )
        hold.update(qkv_h=qkv_h, ffn_far=ffn_far, qkv_got=qkv_got, out_h=out_h)
        return x

    def third_step(x):
        x, hold["qkv_h_got"] = tie(x, swap_dp(hold["qkv_h"], range(1, dp)))
        return x

    placed = run_steps(sequence_steps(*own_one, True), {0: first_step, 1: second_step, parts - 1: third_step})
    normed_one = assemble(placed, slice(0, width))
    places = assemble(placed, slice(width, width + HEAD_DIMENSION))[:, :2].astype(jnp.int32)
    places = places[:, 0] * 16 + places[:, 1]
    normed_one, out_rows = tie(normed_one, hold["out"])
    qkv_blocks = [hold["qkv"], *hold["qkv_got"], hold["qkv_h"], *hold["qkv_h_got"]]
    block_at = block_places()
    ffn_got = [ffn_set[0], *hold["ffn_near"], *hold["ffn_far"]]
    pre_rows, down_rows = rows_join(ffn_got, 2 * hidden, dp_index)

    def ffn_gather(x):
        return lax.all_gather(x, ("h", "t"), axis=0, tiled=False).reshape(ctx, dp, depth, -1)

    pre_weight = ffn_gather(pre_rows)

    def ffn_scatter(term):
        return lax.psum_scatter(term, ("h", "t"), scatter_dimension=0, tiled=True).reshape(dp, depth, -1)

    gains = head_norms.astype(F32)
    half_width = HEAD_DIMENSION // 2
    frequency = theta_base ** (-(jnp.arange(half_width, dtype=F32) * 2.0 / HEAD_DIMENSION))
    angles = places.astype(F32)[:, None] * frequency
    cos, sin = jnp.cos(angles), jnp.sin(angles)
    cos = jnp.concatenate([cos, cos], axis=1)
    sin = jnp.concatenate([-sin, sin], axis=1)
    earliest = jnp.broadcast_to((jnp.arange(length, dtype=jnp.int32) - places)[None, :], (8, length))
    out_pair = jnp.concatenate([out_rows, hold["out_h"]], axis=0)
    qkv = blocks_product(normed_one, qkv_blocks, block_at, 256)
    grad_own = jnp.transpose(out_grad, (1, 0, 2)).reshape(rows, width)
    qkv, qkv_blocks, out_near, grad_own = tie(qkv, qkv_blocks, swap_dp(out_pair, near), grad_own)
    mixed = attention_forward(qkv, gains, cos, sin, earliest)
    mixed, out_far = tie(mixed, swap_dp(out_pair, far))
    out_pairs = [out_pair, *out_near, *out_far]
    out_blocks = [p[: parts * depth] for p in out_pairs] + [p[parts * depth :] for p in out_pairs]
    mixed_part = blocks_back(mixed, out_blocks, block_at, 2)
    mixed_part, out_blocks, qkv_blocks, early = tie(
        mixed_part, out_blocks, qkv_blocks, swap_dp(grad_own, range(1, 2))
    )
    qkv_weight, out_weight = place_rows(qkv_blocks, block_at), place_rows(out_blocks, block_at)
    mixed_sum, (late, pre_weight, down_rows, qkv_weight, out_weight) = to_blocks(
        mixed_part, [swap_dp(grad_own, range(2, dp)), pre_weight, down_rows, qkv_weight, out_weight]
    )
    middle = (inputs + mixed_sum).reshape(rows, width)
    down_weight = ffn_gather(down_rows)

    factor_two = norm_factor(middle)
    own_two = (middle * factor_two).astype(BF16)
    normed_two = swaps([own_two] * dp)
    grad_rows = jnp.concatenate([grad_own, *early, *late], axis=0)
    normed_two = jnp.concatenate(normed_two, axis=0)
    pre = stacked_product(normed_two, pre_weight, hidden // 2)
    hidden_low, grad_pre = hidden_layer(pre, grad_rows, down_weight, tiles)
    down_term = term_product(grad_rows, hidden_low, dp, ctx)
    down_term, grad_pre = tie(down_term, grad_pre)
    down_sum = ffn_scatter(down_term)
    two_part = stacked_back(grad_pre, pre_weight, dp)
    grad_pre, two_part = tie(grad_pre, two_part)
    two_got = swaps(two_part)
    pre_term = term_product(normed_two, grad_pre, dp, ctx)
    branch_part = stacked_back(hidden_low, down_weight, dp)
    pre_term, branch_part, two_got = tie(pre_term, branch_part, two_got)
    grad_two = sum(g.astype(F32) for g in two_got)
    grad_middle = grad_own.astype(F32) + norm_back(middle, factor_two, grad_two)
    grad_mid_own = grad_middle.astype(BF16).reshape(seqs, block, width)
    grad_mid_own, grad_two = tie(grad_mid_own, grad_two)
    mlp_norm_sum = jnp.sum(middle * factor_two * grad_two, axis=0)

    def to_dp(x):
        return [lax.dynamic_index_in_dim(x, dp_index ^ k, 0, keepdims=False) for k in range(dp)]

    def near_step(x):
        x, hold["branch_near"] = tie(x, swap_dp(branch_part, near))
        return x

    def last_step(x):
        x, hold["mlp_sum"] = tie(x, mlp_norm_sum)
        return x

    placed = run_steps(
        sequence_steps(*own_and_other(grad_mid_own), False), {bits + 1: near_step, 2 * bits: last_step}
    )
    mlp_norm_sum = hold["mlp_sum"]
    grad_mid = assemble(placed, slice(None), normed_two)
    if PRE_LATE:
        grad_mid, pre_term = tie(grad_mid, pre_term)
    pre_sum = ffn_scatter(pre_term)
    grad_mixed = rows_product(grad_mid, out_weight, 0, 256, BF16)
    out_pieces = term_pieces(grad_mid, mixed, dp_index, dp)
    grad_mixed, out_pieces, hold["branch_far"] = tie(grad_mixed, out_pieces, swap_dp(branch_part, far))
    grad_qkv, gain_terms = attention_backward(qkv, grad_mixed, gains, cos, sin, earliest)
    hops = [
        (axis, 1 << k) for axis in ("dp", "t", "h") for k in range(lax.axis_size(axis).bit_length() - 1)
    ]
    hold["head"] = jnp.sum(gain_terms, axis=0)[:2]

    def hop():
        axis, bit = hops.pop(0)
        return swap(hold["head"], axis, bit)

    grad_one_part, norm_sums = input_product(grad_qkv, qkv_weight, normed_one, mlp_norm_sum[None], 512)
    grad_qkv, grad_one_part, out_got, down_give, head = tie(
        grad_qkv, grad_one_part, swap_dp(out_pieces, range(1, dp)), to_dp(down_sum), hop()
    )
    hold["head"] += head
    out_keep, out_give = sum_h([out_pieces[0], *out_got])

    qkv_pieces = term_pieces(normed_one, grad_qkv, dp_index, dp, norm_sums)
    qkv_pieces, grad_one_part, down_got, head = tie(qkv_pieces, grad_one_part, swaps(down_give), hop())
    hold["head"] += head
    qkv_got = swaps(qkv_pieces)
    branch_got = [branch_part[0], *hold["branch_near"], *hold["branch_far"]]
    seen = []

    def gradients_step(first):
        got, first, out_h, head, hold["branch"] = tie(qkv_got, first, swap_h(out_give), hop(), branch_got)
        hold["head"] += head
        seen.append(first)
        hold["out_h_got"] = out_h
        hold["qkv_keep"], hold["qkv_give"] = sum_h(got)

    def last_swap_step(got):
        qkv_h_got, head = tie(swap_h(hold["qkv_give"]), hop())
        hold["head"] += head
        attn_sum = hold["qkv_keep"] + qkv_h_got.astype(F32)
        out_sum = out_keep + hold["out_h_got"].astype(F32)
        attn_sum, pre_give = tie(jnp.concatenate([attn_sum, out_sum], axis=1).astype(BF16), to_dp(pre_sum))
        attn_got = swaps(
            [lax.dynamic_slice_in_dim(attn_sum, (part ^ k) * depth, depth, 0) for k in range(parts)], "t"
        )
        while len(hops) > 1:
            hold["head"] += hop()
        hold["pre_got"] = swaps(pre_give)
        got, hold["attn_got"], head = tie(got, attn_got, hop())
        hold["head"] += head
        return got

    grad_one, _ = to_blocks(grad_one_part, [], gradients_step, last_swap_step)
    attn_grad, pre_grad = hold["attn_got"], hold["pre_got"]
    head_norm_grad = hold["head"]
    layer_out = (middle + sum(g.astype(F32) for g in hold["branch"])).astype(BF16)
    input_grad = grad_middle.reshape(seqs, block, width) + norm_back(inputs, factor_one, grad_one)
    layer_out = jnp.transpose(layer_out.reshape(seqs, block, width), (1, 0, 2))
    input_grad = jnp.transpose(input_grad, (1, 0, 2))
    pre_grad, input_grad, layer_out = tie(pre_grad, input_grad, layer_out)
    gate_grad, up_grad, down_grad = whole(
        functools.partial(ffn_join_kernel, tiles),
        [jax.ShapeDtypeStruct(gate_proj.shape, F32)] * 3,
        dp_index,
        mlp_gain,
        *pre_grad,
        *down_got,
    )
    query_grad, key_grad, value_grad, out_proj_grad, norm_grads = whole(
        functools.partial(attn_join_kernel, heads),
        [
            jax.ShapeDtypeStruct(x.shape, F32)
            for x in (query_proj, key_projected, value_projected, out_proj, jnp.zeros((depth, HEAD_DIMENSION)))
        ],
        part,
        attn_gain,
        *attn_grad,
        seen=seen,
    )
    attn_norm_grad = norm_grads[:, 0] / attn_gain[:, 0]
    mlp_norm_grad = norm_grads[:, 1] / mlp_gain[:, 0]

    return (
        layer_out,
        input_grad,
        attn_norm_grad,
        query_grad,
        key_grad,
        value_grad,
        head_norm_grad,
        out_proj_grad,
        mlp_norm_grad,
        gate_grad,
        up_grad,
        down_grad,
    )


def solution(mesh):
    dp, ctx = mesh.shape["dp"], mesh.shape["ctx"]
    fine = Mesh(mesh.devices.reshape(dp, 2, ctx // 2), ("dp", "h", "t"))
    acts = P(("h", "t"), "dp", None)
    rows = P(("dp", "h", "t"), None)
    gain = P(("dp", "h", "t"))
    in_specs = (
        acts,
        P(("h", "t"), "dp"),
        gain,
        rows,
        rows,
        rows,
        P(),
        rows,
        gain,
        rows,
        rows,
        rows,
        acts,
    )
    out_specs = (acts, acts, gain, rows, rows, rows, P(), rows, gain, rows, rows, rows)
    return jax.shard_map(per_device, mesh=fine, in_specs=in_specs, out_specs=out_specs, check_vma=False)
```

```python
import functools

import jax
import jax.numpy as jnp
from jax import lax
from jax.experimental import pallas as pl
from jax.experimental.pallas import tpu as pltpu
from jax.sharding import Mesh
from jax.sharding import PartitionSpec as P

QUERY_HEADS = 16
KEY_VALUE_HEADS = 8
HEAD_DIMENSION = 128
GROUP = QUERY_HEADS // KEY_VALUE_HEADS
HEAD_SET = (GROUP + 2) * HEAD_DIMENSION

epsilon = 1e-06
theta_base = 1000000.0
score_scaling = HEAD_DIMENSION ** (-0.5)
F32 = jnp.float32
BF16 = jnp.bfloat16


def norm_factor(matrix):
    return lax.rsqrt(jnp.mean(matrix * matrix, axis=-1, keepdims=True) + epsilon)


def norm_back(matrix, factor, upstream):
    return factor * upstream - matrix * (factor * factor * factor) * jnp.mean(
        upstream * matrix, axis=-1, keepdims=True
    )


def dot(a, b, ca=1, cb=0):
    return lax.dot_general(a, b, (((ca,), (cb,)), ((), ())), preferred_element_type=F32)


PRE_LATE = True
CHEAP = pl.CostEstimate(flops=1 << 20, bytes_accessed=1 << 16, transcendentals=0)


def rows_kernel(contract, a_ref, b_ref, *out_refs):
    out = dot(a_ref[...], b_ref[...], 1, contract).astype(out_refs[0].dtype)
    step = out_refs[0].shape[0]
    for k, out_ref in enumerate(out_refs):
        out_ref[...] = out[k * step : (k + 1) * step]


def rows_product(a, b, contract, tile, dtype, pieces=1):
    rows, depth = a.shape
    columns = b.shape[1 - contract]
    tile = min(tile, columns)
    out = pl.pallas_call(
        functools.partial(rows_kernel, contract),
        grid=(columns // tile,),
        in_specs=[
            pl.BlockSpec((rows, depth), lambda j: (0, 0)),
            pl.BlockSpec((depth, tile), lambda j: (0, j))
            if contract == 0
            else pl.BlockSpec((tile, depth), lambda j: (j, 0)),
        ],
        out_specs=[pl.BlockSpec((rows // pieces, tile), lambda j: (0, j))] * pieces,
        out_shape=[jax.ShapeDtypeStruct((rows // pieces, columns), dtype)] * pieces,
        compiler_params=pltpu.CompilerParams(vmem_limit_bytes=48 << 20),
        cost_estimate=CHEAP,
    )(a, b)
    return out if pieces > 1 else out[0]


def blocks_kernel(where_ref, a_ref, *refs):
    w_refs, out_ref = refs[:-1], refs[-1]
    depth = w_refs[0].shape[0]
    total = None
    for k, w_ref in enumerate(w_refs):
        start = pl.multiple_of(where_ref[k] * depth, HEAD_DIMENSION)
        part = dot(a_ref[:, pl.ds(start, depth)], w_ref[...])
        total = part if total is None else total + part
    out_ref[...] = total


def blocks_product(a, w_blocks, where, tile):
    rows, depth = a.shape
    columns = w_blocks[0].shape[1]
    return pl.pallas_call(
        blocks_kernel,
        grid_spec=pltpu.PrefetchScalarGridSpec(
            num_scalar_prefetch=1,
            grid=(columns // tile,),
            in_specs=[pl.BlockSpec((rows, depth), lambda j, where: (0, 0))]
            + [pl.BlockSpec((w.shape[0], tile), lambda j, where: (0, j)) for w in w_blocks],
            out_specs=pl.BlockSpec((rows, tile), lambda j, where: (0, j)),
        ),
        out_shape=jax.ShapeDtypeStruct((rows, columns), F32),
        compiler_params=pltpu.CompilerParams(vmem_limit_bytes=48 << 20),
        cost_estimate=CHEAP,
    )(where, a, *w_blocks)


def blocks_back_kernel(where_ref, a_ref, *refs):
    w_refs, out_ref = refs[:-1], refs[-1]
    depth = w_refs[0].shape[0]
    for k, w_ref in enumerate(w_refs):
        start = pl.multiple_of(where_ref[k] * depth, HEAD_DIMENSION)
        out_ref[:, pl.ds(start, depth)] = dot(a_ref[...], w_ref[...], 1, 1).astype(BF16)


def blocks_back(a, w_blocks, where, pieces):
    rows, depth = a.shape
    columns = sum(w.shape[0] for w in w_blocks)
    return pl.pallas_call(
        blocks_back_kernel,
        grid_spec=pltpu.PrefetchScalarGridSpec(
            num_scalar_prefetch=1,
            grid=(pieces,),
            in_specs=[pl.BlockSpec((rows // pieces, depth), lambda j, where: (j, 0))]
            + [pl.BlockSpec(w.shape, lambda j, where: (0, 0)) for w in w_blocks],
            out_specs=pl.BlockSpec((rows // pieces, columns), lambda j, where: (j, 0)),
        ),
        out_shape=jax.ShapeDtypeStruct((rows, columns), BF16),
        compiler_params=pltpu.CompilerParams(vmem_limit_bytes=48 << 20),
        cost_estimate=CHEAP,
    )(where, a, *w_blocks)


def stacked_kernel(a_ref, w_ref, out_ref):
    out_ref[...] = stacked_dot(a_ref, w_ref).astype(out_ref.dtype)


def stacked_dot(a_ref, w_ref):
    blocks, groups, depth, columns = w_ref.shape
    step = blocks * depth
    total = None
    for d in range(groups):
        part = dot(a_ref[:, d * step : (d + 1) * step], w_ref[:, d].reshape(step, columns))
        total = part if total is None else total + part
    return total


def stacked_product(a, w, tile):
    rows, depth = a.shape
    columns = w.shape[3]
    return pl.pallas_call(
        stacked_kernel,
        grid=(columns // tile,),
        in_specs=[
            pl.BlockSpec((rows, depth), lambda j: (0, 0)),
            pl.BlockSpec(w.shape[:3] + (tile,), lambda j: (0, 0, 0, j)),
        ],
        out_specs=pl.BlockSpec((rows, tile), lambda j: (0, j)),
        out_shape=jax.ShapeDtypeStruct((rows, columns), F32),
        compiler_params=pltpu.CompilerParams(vmem_limit_bytes=56 << 20),
        cost_estimate=CHEAP,
    )(a, w)


def stacked_back_kernel(a_ref, w_ref, *out_refs):
    blocks, _, depth, columns = w_ref.shape
    out = dot(a_ref[...], w_ref[:, 0].reshape(blocks * depth, columns), 1, 1).astype(BF16)
    step = out_refs[0].shape[0]
    for k, out_ref in enumerate(out_refs):
        out_ref[...] = out[k * step : (k + 1) * step]


def stacked_back(a, w, pieces):
    rows, depth = a.shape
    blocks, groups, n, columns = w.shape
    step = blocks * n
    return pl.pallas_call(
        stacked_back_kernel,
        grid=(groups,),
        in_specs=[
            pl.BlockSpec((rows, depth), lambda j: (0, 0)),
            pl.BlockSpec((blocks, 1, n, columns), lambda j: (0, j, 0, 0)),
        ],
        out_specs=[pl.BlockSpec((rows // pieces, step), lambda j: (0, j))] * pieces,
        out_shape=[jax.ShapeDtypeStruct((rows // pieces, groups * step), BF16)] * pieces,
        compiler_params=pltpu.CompilerParams(vmem_limit_bytes=56 << 20),
        cost_estimate=CHEAP,
    )(a, w)


def term_kernel(a_ref, b_ref, out_ref):
    out_ref[...] = dot(a_ref[...], b_ref[...], 0, 0).astype(BF16).reshape(out_ref.shape)


def term_product(a, b, groups, blocks):
    rows, width = a.shape
    columns = b.shape[1]
    depth = width // (groups * blocks)
    return pl.pallas_call(
        term_kernel,
        grid=(groups,),
        in_specs=[
            pl.BlockSpec((rows, blocks * depth), lambda i: (0, i)),
            pl.BlockSpec((rows, columns), lambda i: (0, 0)),
        ],
        out_specs=pl.BlockSpec((blocks, 1, depth, columns), lambda i: (0, i, 0, 0)),
        out_shape=jax.ShapeDtypeStruct((blocks, groups, depth, columns), BF16),
        compiler_params=pltpu.CompilerParams(vmem_limit_bytes=56 << 20),
        cost_estimate=CHEAP,
    )(a, b).reshape(width, columns)


def pieces_kernel(me_ref, a_ref, b_ref, *refs):
    norm_ref, out_refs = (refs[0], refs[1:]) if refs[0].shape[0] == 8 else (None, refs)
    wide = b_ref.shape[1]
    part = dot(a_ref[...], b_ref[...], 0, 0).astype(BF16)
    for s, out_ref in enumerate(out_refs):

        @pl.when(pl.program_id(0) == s)
        def _():
            out_ref[:, :wide] = part
            if norm_ref is not None:
                sums = norm_ref[...].T
                rest = jnp.zeros((sums.shape[0], HEAD_DIMENSION - 8), F32)
                out_ref[:, wide:] = jnp.concatenate([sums, rest], axis=1).astype(BF16)


def term_pieces(a, b, me, count, norms=None):
    rows, width = a.shape
    columns = b.shape[1]
    step = width // count
    extra = 0 if norms is None else HEAD_DIMENSION
    in_specs = [
        pl.BlockSpec((rows, step), lambda i, me: (0, me[0] ^ i)),
        pl.BlockSpec((rows, columns), lambda i, me: (0, 0)),
    ]
    if norms is not None:
        in_specs.append(pl.BlockSpec((8, step), lambda i, me: (0, me[0] ^ i)))
    return pl.pallas_call(
        pieces_kernel,
        grid_spec=pltpu.PrefetchScalarGridSpec(
            num_scalar_prefetch=1,
            grid=(count,),
            in_specs=in_specs,
            out_specs=[pl.BlockSpec((step, columns + extra), lambda i, me: (0, 0))] * count,
        ),
        out_shape=[jax.ShapeDtypeStruct((step, columns + extra), BF16)] * count,
        compiler_params=pltpu.CompilerParams(vmem_limit_bytes=56 << 20),
        cost_estimate=CHEAP,
    )(me.reshape(1).astype(jnp.int32), a, b, *([] if norms is None else [norms]))


def input_kernel(grad_ref, weight_ref, normed_ref, other_ref, out_ref, sum_ref):
    part = dot(grad_ref[...], weight_ref[...], 1, 1)
    out_ref[...] = part.astype(BF16)
    sum_ref[...] = jnp.zeros_like(sum_ref)
    sum_ref[0:1] = jnp.sum(normed_ref[...].astype(F32) * part, axis=0, keepdims=True)
    sum_ref[1:2] = other_ref[...]


def input_product(grad, weight, normed, other, tile):
    rows, depth = grad.shape
    columns = weight.shape[0]
    return pl.pallas_call(
        input_kernel,
        grid=(columns // tile,),
        in_specs=[
            pl.BlockSpec((rows, depth), lambda j: (0, 0)),
            pl.BlockSpec((tile, depth), lambda j: (j, 0)),
            pl.BlockSpec((rows, tile), lambda j: (0, j)),
            pl.BlockSpec((1, tile), lambda j: (0, j)),
        ],
        out_specs=[pl.BlockSpec((rows, tile), lambda j: (0, j)), pl.BlockSpec((8, tile), lambda j: (0, j))],
        out_shape=[jax.ShapeDtypeStruct((rows, columns), BF16), jax.ShapeDtypeStruct((8, columns), F32)],
        compiler_params=pltpu.CompilerParams(vmem_limit_bytes=48 << 20),
        cost_estimate=CHEAP,
    )(grad, weight, normed, other)


def whole(kernel, shapes, me, *arrays, seen=()):
    vmem = pl.BlockSpec(memory_space=pltpu.VMEM)

    def body(me_ref, *refs):
        kernel(me_ref, *refs[: len(arrays)], *refs[len(arrays) + len(seen) :])

    return pl.pallas_call(
        body,
        in_specs=[pl.BlockSpec(memory_space=pltpu.SMEM)]
        + [vmem] * len(arrays)
        + [pl.BlockSpec(memory_space=pl.ANY)] * len(seen),
        out_specs=[vmem] * len(shapes),
        out_shape=shapes,
        compiler_params=pltpu.CompilerParams(vmem_limit_bytes=48 << 20),
        cost_estimate=CHEAP,
    )(me.reshape(1).astype(jnp.int32), *arrays, *seen)


def lanes(index, size):
    return pl.ds(pl.multiple_of(index * size, HEAD_DIMENSION), size)


def attn_split_kernel(heads, me_ref, gain_ref, q_ref, k_ref, v_ref, o_ref, *out_refs):
    pair = GROUP * HEAD_DIMENSION
    gain = gain_ref[...]

    def scaled(ref, index, size):
        return (ref[:, lanes(index, size)].astype(F32) * gain).astype(BF16)

    for s, out_ref in enumerate(out_refs):
        part = me_ref[0] ^ s
        for n in range(heads):
            head, at = part * heads + n, n * HEAD_SET
            out_ref[:, at : at + pair] = scaled(q_ref, head, pair)
            out_ref[:, at + pair : at + pair + HEAD_DIMENSION] = scaled(k_ref, head, HEAD_DIMENSION)
            out_ref[:, at + pair + HEAD_DIMENSION : at + HEAD_SET] = scaled(v_ref, head, HEAD_DIMENSION)
        out_ref[:, heads * HEAD_SET :] = o_ref[:, lanes(part, heads * pair)]


def attn_join_kernel(heads, me_ref, gain_ref, *refs):
    count = len(refs) - 5
    q_ref, k_ref, v_ref, o_ref, norm_ref = refs[count:]
    pair = GROUP * HEAD_DIMENSION
    gain = gain_ref[...]
    norms = jnp.zeros(norm_ref.shape, F32)
    for s, got_ref in enumerate(refs[:count]):
        part = me_ref[0] ^ s
        for n in range(heads):
            head, at = part * heads + n, n * HEAD_SET
            q_ref[:, lanes(head, pair)] = got_ref[:, at : at + pair].astype(F32) * gain
            k_ref[:, lanes(head, HEAD_DIMENSION)] = (
                got_ref[:, at + pair : at + pair + HEAD_DIMENSION].astype(F32) * gain
            )
            v_ref[:, lanes(head, HEAD_DIMENSION)] = (
                got_ref[:, at + pair + HEAD_DIMENSION : at + HEAD_SET].astype(F32) * gain
            )
        norms += got_ref[:, heads * HEAD_SET : heads * HEAD_SET + HEAD_DIMENSION].astype(F32)
        o_ref[:, lanes(part, heads * pair)] = got_ref[:, heads * HEAD_SET + HEAD_DIMENSION :].astype(F32)
    norm_ref[...] = norms


def ffn_split_kernel(tiles, me_ref, gain_ref, gate_ref, up_ref, down_ref, *out_refs):
    gain = gain_ref[...]
    hidden = out_refs[0].shape[1] // 3
    tile = hidden // tiles
    for s, out_ref in enumerate(out_refs):
        part = me_ref[0] ^ s
        for n in range(tiles):
            for k, ref in enumerate((gate_ref, up_ref)):
                at = (2 * n + k) * tile
                out_ref[:, at : at + tile] = (ref[:, lanes(part * tiles + n, tile)].astype(F32) * gain).astype(
                    BF16
                )
        out_ref[:, 2 * hidden :] = down_ref[:, lanes(part, hidden)]


def ffn_join_kernel(tiles, me_ref, gain_ref, *refs):
    count = (len(refs) - 3) // 2
    gate_ref, up_ref, down_ref = refs[2 * count :]
    gain = gain_ref[...]
    hidden = refs[0].shape[1] // 2
    tile = hidden // tiles
    for s, (got_ref, down_got_ref) in enumerate(zip(refs[:count], refs[count:])):
        part = me_ref[0] ^ s
        for n in range(tiles):
            for k, ref in enumerate((gate_ref, up_ref)):
                at = (2 * n + k) * tile
                ref[:, lanes(part * tiles + n, tile)] = got_ref[:, at : at + tile].astype(F32) * gain
        down_ref[:, lanes(part, hidden)] = down_got_ref[...].astype(F32)


def rows_join_kernel(me_ref, *refs):
    first_ref, second_ref = refs[-2:]
    depth = refs[0].shape[0]
    wide = first_ref.shape[1]
    for s, got_ref in enumerate(refs[:-2]):
        rows = pl.ds(pl.multiple_of((me_ref[0] ^ s) * depth, depth), depth)
        first_ref[rows] = got_ref[:, :wide]
        second_ref[rows] = got_ref[:, wide:]


def rows_join(got, wide, me):
    depth, width = got[0].shape
    return whole(
        rows_join_kernel,
        [jax.ShapeDtypeStruct((len(got) * depth, n), BF16) for n in (wide, width - wide)],
        me,
        *got,
    )


def rotate(x, cos, sin):
    return x * cos + pltpu.roll(x, HEAD_DIMENSION // 2, 1) * sin


def head_slice(i):
    return slice(i * HEAD_DIMENSION, (i + 1) * HEAD_DIMENSION)


def normed_rotated(raw, gain, cos, sin):
    return rotate(raw * norm_factor(raw) * gain, cos, sin).astype(BF16)


def probabilities(keys, queries, first_query, earliest):
    scores = dot(keys, queries, 1, 1) * score_scaling
    key_index = lax.broadcasted_iota(jnp.int32, scores.shape, 0)
    query_index = lax.broadcasted_iota(jnp.int32, scores.shape, 1) + first_query
    allowed = (key_index <= query_index) & (key_index >= earliest)
    masked = jnp.where(allowed, scores, -1e30)
    shifted = jnp.exp(masked - jnp.max(masked, axis=0, keepdims=True))
    return shifted * (1.0 / jnp.sum(shifted, axis=0, keepdims=True))


def forward_kernel(block, qkv_ref, gain_ref, cos_ref, sin_ref, early_ref, out_ref):
    length = qkv_ref.shape[0]
    gains = gain_ref[...]
    cos, sin = cos_ref[...], sin_ref[...]
    keys = normed_rotated(qkv_ref[:, head_slice(GROUP)], gains[1:2], cos, sin)
    values_t = qkv_ref[:, head_slice(GROUP + 1)].T.astype(BF16)
    for i in range(length // block):
        rows = slice(i * block, (i + 1) * block)
        seen = (i + 1) * block
        for g in range(GROUP):
            queries = normed_rotated(qkv_ref[rows, head_slice(g)], gains[0:1], cos[rows], sin[rows])
            probs = probabilities(keys[:seen], queries, i * block, early_ref[0:1, rows]).astype(BF16)
            mixed = dot(values_t[:, :seen], probs)
            out_ref[rows, head_slice(g)] = mixed.T.astype(BF16)


def backward_kernel(
    block, qkv_ref, dout_ref, gain_ref, cos_ref, sin_ref, early_ref, dqkv_ref, dgain_ref, dkey_ref, dvalue_ref
):
    length = qkv_ref.shape[0]
    gains = gain_ref[...]
    cos, sin = cos_ref[...], sin_ref[...]
    key_raw = qkv_ref[:, head_slice(GROUP)]
    keys = normed_rotated(key_raw, gains[1:2], cos, sin)
    keys_t = keys.astype(F32).T.astype(BF16)
    values = qkv_ref[:, head_slice(GROUP + 1)].astype(BF16)
    dkey_ref[...] = jnp.zeros_like(dkey_ref)
    dvalue_ref[...] = jnp.zeros_like(dvalue_ref)
    query_gain_sum = jnp.zeros((1, HEAD_DIMENSION), F32)
    for i in range(length // block):
        rows = slice(i * block, (i + 1) * block)
        seen = (i + 1) * block
        for g in range(GROUP):
            query_raw = qkv_ref[rows, head_slice(g)]
            queries = normed_rotated(query_raw, gains[0:1], cos[rows], sin[rows])
            dout = dout_ref[rows, head_slice(g)]
            probs = probabilities(keys[:seen], queries, i * block, early_ref[0:1, rows])
            dprobs = dot(values[:seen], dout, 1, 1)
            delta = jnp.sum(probs * dprobs, axis=0, keepdims=True)
            dscores = (probs * (dprobs - delta)).astype(BF16)
            dkey_ref[:seen] += dot(dscores, queries)
            dvalue_ref[:seen] += dot(probs.astype(BF16), dout)
            dquery = dot(keys_t[:, :seen], dscores).T * score_scaling
            dquery = rotate(dquery, cos[rows], -sin[rows])
            factor = norm_factor(query_raw)
            query_gain_sum += jnp.sum(query_raw * factor * dquery, axis=0, keepdims=True)
            dqkv_ref[rows, head_slice(g)] = norm_back(query_raw, factor, dquery * gains[0:1]).astype(BF16)
    dkey = rotate(dkey_ref[...] * score_scaling, cos, -sin)
    factor = norm_factor(key_raw)
    dgain_ref[0, 0:1, :] = query_gain_sum
    dgain_ref[0, 1:2, :] = jnp.sum(key_raw * factor * dkey, axis=0, keepdims=True)
    dgain_ref[0, 2:, :] = jnp.zeros((6, HEAD_DIMENSION), F32)
    dqkv_ref[:, head_slice(GROUP)] = norm_back(key_raw, factor, dkey * gains[1:2]).astype(BF16)
    dqkv_ref[:, head_slice(GROUP + 1)] = dvalue_ref[...].astype(BF16)


def per_head_specs(length):
    whole = lambda shape: pl.BlockSpec(shape, lambda n: (0,) * len(shape))
    return [
        whole((2, HEAD_DIMENSION)),
        whole((length, HEAD_DIMENSION)),
        whole((length, HEAD_DIMENSION)),
        whole((8, length)),
    ]


def columns_spec(length, width):
    return pl.BlockSpec((length, width), lambda n: (0, n))


def attention_forward(qkv, gains, cos, sin, earliest):
    length, width = qkv.shape
    heads = width // HEAD_SET
    return pl.pallas_call(
        functools.partial(forward_kernel, 256),
        grid=(heads,),
        in_specs=[columns_spec(length, HEAD_SET)] + per_head_specs(length),
        out_specs=columns_spec(length, GROUP * HEAD_DIMENSION),
        out_shape=jax.ShapeDtypeStruct((length, heads * GROUP * HEAD_DIMENSION), BF16),
        compiler_params=pltpu.CompilerParams(vmem_limit_bytes=48 << 20),
        cost_estimate=CHEAP,
    )(qkv, gains, cos, sin, earliest)


def attention_backward(qkv, dout, gains, cos, sin, earliest):
    length, width = qkv.shape
    heads = width // HEAD_SET
    return pl.pallas_call(
        functools.partial(backward_kernel, 256),
        grid=(heads,),
        in_specs=[columns_spec(length, HEAD_SET), columns_spec(length, GROUP * HEAD_DIMENSION)]
        + per_head_specs(length),
        out_specs=[
            columns_spec(length, HEAD_SET),
            pl.BlockSpec((1, 8, HEAD_DIMENSION), lambda n: (n, 0, 0)),
        ],
        out_shape=[
            jax.ShapeDtypeStruct((length, width), BF16),
            jax.ShapeDtypeStruct((heads, 8, HEAD_DIMENSION), F32),
        ],
        scratch_shapes=[pltpu.VMEM((length, HEAD_DIMENSION), F32)] * 2,
        compiler_params=pltpu.CompilerParams(vmem_limit_bytes=48 << 20),
        cost_estimate=CHEAP,
    )(qkv, dout, gains, cos, sin, earliest)


def hidden_kernel(pre_ref, grad_ref, down_ref, hidden_ref, dpre_ref):
    tile = hidden_ref.shape[1]
    grad_hidden = stacked_dot(grad_ref, down_ref)
    step = 128
    for start in range(0, hidden_ref.shape[0], step):
        rows = slice(start, start + step)
        gate, up, grad = pre_ref[rows, :tile], pre_ref[rows, tile:], grad_hidden[rows]
        sig = 1.0 / (1.0 + jnp.exp(-gate))
        act = gate * sig
        hidden_ref[rows] = (act * up).astype(BF16)
        dpre_ref[rows, :tile] = (grad * up * sig * (1.0 + gate * (1.0 - sig))).astype(BF16)
        dpre_ref[rows, tile:] = (grad * act).astype(BF16)


def hidden_layer(pre, grad, down, tiles):
    rows, width = grad.shape
    tile = down.shape[3] // tiles
    step = min(rows, 1024)
    return pl.pallas_call(
        hidden_kernel,
        grid=(tiles, rows // step),
        in_specs=[
            pl.BlockSpec((step, 2 * tile), lambda j, i: (i, j)),
            pl.BlockSpec((step, width), lambda j, i: (i, 0)),
            pl.BlockSpec(down.shape[:3] + (tile,), lambda j, i: (0, 0, 0, j)),
        ],
        out_specs=[
            pl.BlockSpec((step, tile), lambda j, i: (i, j)),
            pl.BlockSpec((step, 2 * tile), lambda j, i: (i, j)),
        ],
        out_shape=[
            jax.ShapeDtypeStruct((rows, tile * tiles), BF16),
            jax.ShapeDtypeStruct((rows, 2 * tile * tiles), BF16),
        ],
        compiler_params=pltpu.CompilerParams(vmem_limit_bytes=56 << 20),
        cost_estimate=CHEAP,
    )(pre, grad, down)


def tie(*items):
    return lax.optimization_barrier(items)


def swap(x, axis, bit):
    return lax.ppermute(x, axis, [(i, i ^ bit) for i in range(lax.axis_size(axis))])


def own_and_other(blocks):
    half = lax.axis_index("h")
    return [lax.dynamic_index_in_dim(blocks, k, 0, keepdims=True) for k in (half, 1 - half)]


def sequence_steps(own, give, together):
    half, part, parts = lax.axis_index("h"), lax.axis_index("t"), lax.axis_size("t")
    block = own.shape[1]
    got = swap(give, "h", 1)
    if not together:
        own_first, got = tie(swap(own, "t", parts // 2), got)
    got = yield got
    if together:
        starts = [(jnp.concatenate([own, got], axis=0), [0, parts])]
    else:
        starts = [(own, [0]), (got, [parts])]
    placed = []
    for first, keys in starts:
        held = [first]
        bit = parts // 2
        while bit:
            if together:
                for piece in list(held):
                    got = yield swap(piece, "t", bit)
                    held.append(got)
            else:
                if first is own and len(held) == 1:
                    got = yield own_first
                else:
                    got = yield swap(jnp.concatenate(held, axis=0) if len(held) > 1 else first, "t", bit)
                held.append(got)
            keys = keys + [k | bit for k in keys]
            bit //= 2
        flat = [piece[i] for piece in held for i in range(piece.shape[0])]
        placed += [(b, ((half * parts + part) ^ k) * block) for b, k in zip(flat, keys)]
    return placed


def run_steps(steps, ties):
    number, arrived = 0, next(steps)
    while True:
        try:
            arrived = steps.send(ties[number](arrived) if number in ties else arrived)
        except StopIteration as end:
            return end.value
        number += 1


def assemble(placed, columns=slice(None), out=None):
    rows = sum(part.shape[0] for part, _ in placed)
    if out is None:
        out = blank((rows, placed[0][0][:, columns].shape[1]), placed[0][0].dtype)
    for part, start in placed:
        out = lax.dynamic_update_slice_in_dim(out, part[:, columns], start, 0)
    return out


def to_blocks(partial, late=(), on_first=None, on_last=None):
    half, part, parts = lax.axis_index("h"), lax.axis_index("t"), lax.axis_size("t")
    both = partial.reshape(2, parts, -1, partial.shape[1])
    held = [lax.dynamic_index_in_dim(both, part ^ key, 1, keepdims=False) for key in range(parts)]

    def pick(x, h):
        return lax.dynamic_index_in_dim(x, h, 0, keepdims=False)

    bit = 1
    while 2 * bit < parts:
        keys = [key for key in range(parts) if held[key] is not None and key & bit]
        got = swap(jnp.stack([held[key].astype(BF16) for key in keys]), "t", bit)
        for n, key in enumerate(keys):
            held[key ^ bit] = held[key ^ bit].astype(F32) + got[n].astype(F32)
            held[key] = None
        bit *= 2
    first = swap(pick(held[bit], 1 - half).astype(BF16), "t", bit)
    if on_first is not None:
        first = on_first(first)
    far = pick(held[0], 1 - half).astype(F32) + first.astype(F32)
    far, near = tie(far.astype(BF16), pick(held[bit], half).astype(BF16))
    got = swap(far, "h", 1)
    second = swap(near, "t", bit)
    if on_last is not None:
        got, second = on_last(got, second)
    own = pick(held[0], half).astype(F32) + second.astype(F32)
    got, own, late = tie(got.astype(F32), own, list(late))
    return jnp.where(half == 0, jnp.stack([own, got]), jnp.stack([got, own])), late


def swaps(pieces, axis="dp"):
    return [pieces[0]] + list(reversed([swap(pieces[s], axis, s) for s in reversed(range(1, len(pieces)))]))


def gather_h(x):
    return [x, swap(x, "h", 1)]


def block_places():
    dp, half, count = lax.axis_index("dp"), lax.axis_index("h"), lax.axis_size("dp")
    return jnp.stack([(dp ^ s) * 2 + (half ^ k) for k in (0, 1) for s in range(count)]).astype(jnp.int32)


def blank(shape, dtype):
    return pl.pallas_call(
        lambda out_ref: None,
        out_specs=pl.BlockSpec(memory_space=pl.ANY),
        out_shape=jax.ShapeDtypeStruct(shape, dtype),
    )()


def place_rows(blocks, places):
    rows, width = blocks[0].shape
    out = blank((len(blocks) * rows, width), blocks[0].dtype)
    for k, part in enumerate(blocks):
        out = lax.dynamic_update_slice_in_dim(out, part, places[k] * rows, 0)
    return out


def sum_h(got):
    half = lax.axis_index("h")
    total = sum(g.astype(F32) for g in got)
    total = total.reshape(2, total.shape[0] // 2, -1)
    give = lax.dynamic_index_in_dim(total, 1 - half, 0, keepdims=False).astype(BF16)
    return lax.dynamic_index_in_dim(total, half, 0, keepdims=False), give


def total_over(x, axis):
    bit = 1
    while bit < lax.axis_size(axis):
        x = x + swap(x, axis, bit)
        bit *= 2
    return x


def per_device(
    tokens,
    positions,
    attn_norm,
    query_proj,
    key_projected,
    value_projected,
    head_norms,
    out_proj,
    mlp_norm,
    gate_proj,
    up_proj,
    down_proj,
    out_grad,
):
    block, seqs, width = tokens.shape
    rows = block * seqs
    dp = lax.axis_size("dp")
    parts = lax.axis_size("t")
    ctx = 2 * parts
    length = block * ctx
    depth = query_proj.shape[0]
    part = lax.axis_index("t")
    attn_gain = attn_norm.astype(F32)[:, None]
    mlp_gain = mlp_norm.astype(F32)[:, None]

    inputs = jnp.transpose(tokens, (1, 0, 2)).astype(F32)
    factor_one = norm_factor(inputs)
    digits = jnp.stack([positions.T // 16, positions.T % 16], axis=2).astype(BF16)
    digits = jnp.pad(digits, ((0, 0), (0, 0), (0, HEAD_DIMENSION - 2)))
    own_one = jnp.concatenate([(inputs * factor_one).astype(BF16), digits], axis=2)
    own_one, query_proj, gate_proj = tie(own_and_other(own_one), query_proj, gate_proj)

    heads = KEY_VALUE_HEADS // parts
    pair = GROUP * HEAD_DIMENSION
    qkv_width, mix_width = heads * HEAD_SET, heads * pair
    attn_width = qkv_width + mix_width

    dp_index = lax.axis_index("dp")
    attn_set = whole(
        functools.partial(attn_split_kernel, heads),
        [jax.ShapeDtypeStruct((depth, attn_width), BF16)] * parts,
        part,
        attn_gain,
        query_proj,
        key_projected,
        value_projected,
        out_proj,
    )
    attn_set, gate_proj = tie(attn_set, gate_proj)

    hidden = gate_proj.shape[1] // dp
    tiles = 3
    ffn_set = whole(
        functools.partial(ffn_split_kernel, tiles),
        [jax.ShapeDtypeStruct((depth, 3 * hidden), BF16)] * dp,
        dp_index,
        mlp_gain,
        gate_proj,
        up_proj,
        down_proj,
    )

    def swap_h(x):
        return swap(x, "h", 1)

    def swap_dp(x, keys):
        return [swap(x[k] if isinstance(x, (list, tuple)) else x, "dp", k) for k in keys]

    near, far = range(1, dp - 1), range(dp - 1, dp)
    bits = parts.bit_length() - 1
    hold = {}

    def first_step(x):
        x, got, ffn_near = tie(x, swaps(attn_set, "t"), swap_dp(ffn_set, near))
        qkv_rows, out_rows = rows_join(got, qkv_width, part)
        hold.update(qkv=qkv_rows, out=out_rows, ffn_near=ffn_near)
        return x

    def second_step(x):
        x, qkv_h, ffn_far, qkv_got, out_h = tie(
            x,
            swap_h(hold["qkv"]),
            swap_dp(ffn_set, far),
            swap_dp(hold["qkv"], range(1, dp)),
            swap_h(hold["out"]),
        )
        hold.update(qkv_h=qkv_h, ffn_far=ffn_far, qkv_got=qkv_got, out_h=out_h)
        return x

    def third_step(x):
        x, hold["qkv_h_got"] = tie(x, swap_dp(hold["qkv_h"], range(1, dp)))
        return x

    placed = run_steps(sequence_steps(*own_one, True), {0: first_step, 1: second_step, parts - 1: third_step})
    normed_one = assemble(placed, slice(0, width))
    places = assemble(placed, slice(width, width + HEAD_DIMENSION))[:, :2].astype(jnp.int32)
    places = places[:, 0] * 16 + places[:, 1]
    normed_one, out_rows = tie(normed_one, hold["out"])
    qkv_blocks = [hold["qkv"], *hold["qkv_got"], hold["qkv_h"], *hold["qkv_h_got"]]
    block_at = block_places()
    ffn_got = [ffn_set[0], *hold["ffn_near"], *hold["ffn_far"]]
    pre_rows, down_rows = rows_join(ffn_got, 2 * hidden, dp_index)

    def ffn_gather(x):
        return lax.all_gather(x, ("h", "t"), axis=0, tiled=False).reshape(ctx, dp, depth, -1)

    pre_weight = ffn_gather(pre_rows)

    def ffn_scatter(term):
        return lax.psum_scatter(term, ("h", "t"), scatter_dimension=0, tiled=True).reshape(dp, depth, -1)

    gains = head_norms.astype(F32)
    half_width = HEAD_DIMENSION // 2
    frequency = theta_base ** (-(jnp.arange(half_width, dtype=F32) * 2.0 / HEAD_DIMENSION))
    angles = places.astype(F32)[:, None] * frequency
    cos, sin = jnp.cos(angles), jnp.sin(angles)
    cos = jnp.concatenate([cos, cos], axis=1)
    sin = jnp.concatenate([-sin, sin], axis=1)
    earliest = jnp.broadcast_to((jnp.arange(length, dtype=jnp.int32) - places)[None, :], (8, length))
    out_pair = jnp.concatenate([out_rows, hold["out_h"]], axis=0)
    qkv = blocks_product(normed_one, qkv_blocks, block_at, 256)
    qkv, qkv_blocks, out_near, out_grad = tie(qkv, qkv_blocks, swap_dp(out_pair, near), out_grad)
    grad_own = jnp.transpose(out_grad, (1, 0, 2)).reshape(rows, width)
    mixed = attention_forward(qkv, gains, cos, sin, earliest)
    mixed, out_far = tie(mixed, swap_dp(out_pair, far))
    out_pairs = [out_pair, *out_near, *out_far]
    out_blocks = [p[: parts * depth] for p in out_pairs] + [p[parts * depth :] for p in out_pairs]
    mixed_part = blocks_back(mixed, out_blocks, block_at, 2)
    mixed_part, out_blocks, qkv_blocks, early = tie(
        mixed_part, out_blocks, qkv_blocks, swap_dp(grad_own, range(1, 2))
    )
    def weights_step(first):
        first, qkv_parts, out_parts = tie(first, qkv_blocks, out_blocks)
        hold["qkv_weight"] = place_rows(qkv_parts, block_at)
        hold["out_weight"] = place_rows(out_parts, block_at)
        return first

    def weights_done(got, second):
        got, hold["qkv_weight"], hold["out_weight"] = tie(got, hold["qkv_weight"], hold["out_weight"])
        return got, second

    mixed_sum, (late, pre_weight, down_rows) = to_blocks(
        mixed_part, [swap_dp(grad_own, range(2, dp)), pre_weight, down_rows], weights_step, weights_done
    )
    qkv_weight, out_weight = hold["qkv_weight"], hold["out_weight"]
    middle = (inputs + mixed_sum).reshape(rows, width)
    down_weight = ffn_gather(down_rows)

    factor_two = norm_factor(middle)
    own_two = (middle * factor_two).astype(BF16)
    normed_two = swaps([own_two] * dp)
    grad_rows = jnp.concatenate([grad_own, *early, *late], axis=0)
    normed_two = jnp.concatenate(normed_two, axis=0)
    pre = stacked_product(normed_two, pre_weight, hidden // 2)
    hidden_low, grad_pre = hidden_layer(pre, grad_rows, down_weight, tiles)
    down_term = term_product(grad_rows, hidden_low, dp, ctx)
    down_term, grad_pre = tie(down_term, grad_pre)
    down_sum = ffn_scatter(down_term)
    two_part = stacked_back(grad_pre, pre_weight, dp)
    grad_pre, two_part = tie(grad_pre, two_part)
    two_got = swaps(two_part)
    pre_term = term_product(normed_two, grad_pre, dp, ctx)
    branch_part = stacked_back(hidden_low, down_weight, dp)
    pre_term, branch_part, two_got = tie(pre_term, branch_part, two_got)
    grad_two = sum(g.astype(F32) for g in two_got)
    grad_middle = grad_own.astype(F32) + norm_back(middle, factor_two, grad_two)
    grad_mid_own = grad_middle.astype(BF16).reshape(seqs, block, width)
    grad_mid_own, grad_two = tie(grad_mid_own, grad_two)
    mlp_norm_sum = jnp.sum(middle * factor_two * grad_two, axis=0)

    def to_dp(x):
        return [lax.dynamic_index_in_dim(x, dp_index ^ k, 0, keepdims=False) for k in range(dp)]

    def near_step(x):
        x, hold["branch_near"] = tie(x, swap_dp(branch_part, near))
        return x

    def last_step(x):
        x, hold["mlp_sum"] = tie(x, mlp_norm_sum)
        return x

    placed = run_steps(
        sequence_steps(*own_and_other(grad_mid_own), False), {bits + 1: near_step, 2 * bits: last_step}
    )
    mlp_norm_sum = hold["mlp_sum"]
    grad_mid = assemble(placed, slice(None), normed_two)
    if PRE_LATE:
        grad_mid, pre_term = tie(grad_mid, pre_term)
    pre_sum = ffn_scatter(pre_term)
    grad_mixed = rows_product(grad_mid, out_weight, 0, 256, BF16)
    out_pieces = term_pieces(grad_mid, mixed, dp_index, dp)
    grad_mixed, out_pieces = tie(grad_mixed, out_pieces)
    grad_qkv, gain_terms = attention_backward(qkv, grad_mixed, gains, cos, sin, earliest)
    grad_qkv, hold["branch_far"] = tie(grad_qkv, swap_dp(branch_part, far))
    hops = [
        (axis, 1 << k) for axis in ("dp", "t", "h") for k in range(lax.axis_size(axis).bit_length() - 1)
    ]
    hold["head"] = jnp.sum(gain_terms, axis=0)[:2]

    def hop():
        axis, bit = hops.pop(0)
        return swap(hold["head"], axis, bit)

    grad_one_part, norm_sums = input_product(grad_qkv, qkv_weight, normed_one, mlp_norm_sum[None], 512)
    grad_qkv, grad_one_part, out_got, down_give, head = tie(
        grad_qkv, grad_one_part, swap_dp(out_pieces, range(1, dp)), to_dp(down_sum), hop()
    )
    hold["head"] += head
    out_keep, out_give = sum_h([out_pieces[0], *out_got])

    qkv_pieces = term_pieces(normed_one, grad_qkv, dp_index, dp, norm_sums)
    qkv_pieces, grad_one_part, down_got, head = tie(qkv_pieces, grad_one_part, swaps(down_give), hop())
    hold["head"] += head
    qkv_got = swaps(qkv_pieces)
    branch_got = [branch_part[0], *hold["branch_near"], *hold["branch_far"]]
    seen = []

    def gradients_step(first):
        arrived = first
        got, first, out_h, head, hold["branch"] = tie(qkv_got, first, swap_h(out_give), hop(), branch_got)
        hold["head"] += head
        seen.append(first)
        hold["out_h_got"] = out_h
        hold["qkv_keep"], hold["qkv_give"] = sum_h(got)
        return arrived

    def last_swap_step(got, second):
        got, head, second, pre_give = tie(got, hop(), second, to_dp(pre_sum))
        qkv_h_got, pre_near = tie(swap_h(hold["qkv_give"]), swap_dp(pre_give, near))
        hold["head"] += head
        attn_sum = hold["qkv_keep"] + qkv_h_got.astype(F32)
        out_sum = out_keep + hold["out_h_got"].astype(F32)
        attn_sum = jnp.concatenate([attn_sum, out_sum], axis=1).astype(BF16)
        attn_got = swaps(
            [lax.dynamic_slice_in_dim(attn_sum, (part ^ k) * depth, depth, 0) for k in range(parts)], "t"
        )
        while len(hops) > 1:
            hold["head"] += hop()
        hold["pre_got"] = [pre_give[0], *pre_near, *swap_dp(pre_give, far)]
        got, hold["attn_got"], head = tie(got, attn_got, hop())
        hold["head"] += head
        return got, second

    grad_one, _ = to_blocks(grad_one_part, [], gradients_step, last_swap_step)
    attn_grad, pre_grad = hold["attn_got"], hold["pre_got"]
    head_norm_grad = hold["head"]
    layer_out = (middle + sum(g.astype(F32) for g in hold["branch"])).astype(BF16)
    input_grad = grad_middle.reshape(seqs, block, width) + norm_back(inputs, factor_one, grad_one)
    layer_out = jnp.transpose(layer_out.reshape(seqs, block, width), (1, 0, 2))
    input_grad = jnp.transpose(input_grad, (1, 0, 2))
    pre_grad, input_grad, layer_out = tie(pre_grad, input_grad, layer_out)
    gate_grad, up_grad, down_grad = whole(
        functools.partial(ffn_join_kernel, tiles),
        [jax.ShapeDtypeStruct(gate_proj.shape, F32)] * 3,
        dp_index,
        mlp_gain,
        *pre_grad,
        *down_got,
    )
    query_grad, key_grad, value_grad, out_proj_grad, norm_grads = whole(
        functools.partial(attn_join_kernel, heads),
        [
            jax.ShapeDtypeStruct(x.shape, F32)
            for x in (query_proj, key_projected, value_projected, out_proj, jnp.zeros((depth, HEAD_DIMENSION)))
        ],
        part,
        attn_gain,
        *attn_grad,
        seen=seen,
    )
    attn_norm_grad = norm_grads[:, 0] / attn_gain[:, 0]
    mlp_norm_grad = norm_grads[:, 1] / mlp_gain[:, 0]

    return (
        layer_out,
        input_grad,
        attn_norm_grad,
        query_grad,
        key_grad,
        value_grad,
        head_norm_grad,
        out_proj_grad,
        mlp_norm_grad,
        gate_grad,
        up_grad,
        down_grad,
    )


def solution(mesh):
    dp, ctx = mesh.shape["dp"], mesh.shape["ctx"]
    fine = Mesh(mesh.devices.reshape(dp, 2, ctx // 2), ("dp", "h", "t"))
    acts = P(("h", "t"), "dp", None)
    rows = P(("dp", "h", "t"), None)
    gain = P(("dp", "h", "t"))
    in_specs = (
        acts,
        P(("h", "t"), "dp"),
        gain,
        rows,
        rows,
        rows,
        P(),
        rows,
        gain,
        rows,
        rows,
        rows,
        acts,
    )
    out_specs = (acts, acts, gain, rows, rows, rows, P(), rows, gain, rows, rows, rows)
    return jax.shard_map(per_device, mesh=fine, in_specs=in_specs, out_specs=out_specs, check_vma=False)
```

```python
import functools

import jax
import jax.numpy as jnp
from jax import lax
from jax.experimental import pallas as pl
from jax.experimental.pallas import tpu as pltpu
from jax.sharding import Mesh
from jax.sharding import PartitionSpec as P

QUERY_HEADS = 16
KEY_VALUE_HEADS = 8
HEAD_DIMENSION = 128
GROUP = QUERY_HEADS // KEY_VALUE_HEADS
HEAD_SET = (GROUP + 2) * HEAD_DIMENSION

epsilon = 1e-06
theta_base = 1000000.0
score_scaling = HEAD_DIMENSION ** (-0.5)
F32 = jnp.float32
BF16 = jnp.bfloat16


def norm_factor(matrix):
    return lax.rsqrt(jnp.mean(matrix * matrix, axis=-1, keepdims=True) + epsilon)


def norm_back(matrix, factor, upstream):
    return factor * upstream - matrix * (factor * factor * factor) * jnp.mean(
        upstream * matrix, axis=-1, keepdims=True
    )


def dot(a, b, ca=1, cb=0):
    return lax.dot_general(a, b, (((ca,), (cb,)), ((), ())), preferred_element_type=F32)


PRE_LATE = True
CHEAP = pl.CostEstimate(flops=1 << 20, bytes_accessed=1 << 16, transcendentals=0)


def rows_kernel(contract, a_ref, b_ref, *out_refs):
    out = dot(a_ref[...], b_ref[...], 1, contract).astype(out_refs[0].dtype)
    step = out_refs[0].shape[0]
    for k, out_ref in enumerate(out_refs):
        out_ref[...] = out[k * step : (k + 1) * step]


def rows_product(a, b, contract, tile, dtype, pieces=1):
    rows, depth = a.shape
    columns = b.shape[1 - contract]
    tile = min(tile, columns)
    out = pl.pallas_call(
        functools.partial(rows_kernel, contract),
        grid=(columns // tile,),
        in_specs=[
            pl.BlockSpec((rows, depth), lambda j: (0, 0)),
            pl.BlockSpec((depth, tile), lambda j: (0, j))
            if contract == 0
            else pl.BlockSpec((tile, depth), lambda j: (j, 0)),
        ],
        out_specs=[pl.BlockSpec((rows // pieces, tile), lambda j: (0, j))] * pieces,
        out_shape=[jax.ShapeDtypeStruct((rows // pieces, columns), dtype)] * pieces,
        compiler_params=pltpu.CompilerParams(vmem_limit_bytes=48 << 20),
        cost_estimate=CHEAP,
    )(a, b)
    return out if pieces > 1 else out[0]


def blocks_kernel(where_ref, a_ref, *refs):
    w_refs, out_ref = refs[:-1], refs[-1]
    depth = w_refs[0].shape[0]
    total = None
    for k, w_ref in enumerate(w_refs):
        start = pl.multiple_of(where_ref[k] * depth, HEAD_DIMENSION)
        part = dot(a_ref[:, pl.ds(start, depth)], w_ref[...])
        total = part if total is None else total + part
    out_ref[...] = total


def blocks_product(a, w_blocks, where, tile):
    rows, depth = a.shape
    columns = w_blocks[0].shape[1]
    return pl.pallas_call(
        blocks_kernel,
        grid_spec=pltpu.PrefetchScalarGridSpec(
            num_scalar_prefetch=1,
            grid=(columns // tile,),
            in_specs=[pl.BlockSpec((rows, depth), lambda j, where: (0, 0))]
            + [pl.BlockSpec((w.shape[0], tile), lambda j, where: (0, j)) for w in w_blocks],
            out_specs=pl.BlockSpec((rows, tile), lambda j, where: (0, j)),
        ),
        out_shape=jax.ShapeDtypeStruct((rows, columns), F32),
        compiler_params=pltpu.CompilerParams(vmem_limit_bytes=48 << 20),
        cost_estimate=CHEAP,
    )(where, a, *w_blocks)


def blocks_back_kernel(where_ref, a_ref, *refs):
    w_refs, out_ref = refs[:-1], refs[-1]
    depth = w_refs[0].shape[0]
    for k, w_ref in enumerate(w_refs):
        start = pl.multiple_of(where_ref[k] * depth, HEAD_DIMENSION)
        out_ref[:, pl.ds(start, depth)] = dot(a_ref[...], w_ref[...], 1, 1).astype(BF16)


def blocks_back(a, w_blocks, where, pieces):
    rows, depth = a.shape
    columns = sum(w.shape[0] for w in w_blocks)
    return pl.pallas_call(
        blocks_back_kernel,
        grid_spec=pltpu.PrefetchScalarGridSpec(
            num_scalar_prefetch=1,
            grid=(pieces,),
            in_specs=[pl.BlockSpec((rows // pieces, depth), lambda j, where: (j, 0))]
            + [pl.BlockSpec(w.shape, lambda j, where: (0, 0)) for w in w_blocks],
            out_specs=pl.BlockSpec((rows // pieces, columns), lambda j, where: (j, 0)),
        ),
        out_shape=jax.ShapeDtypeStruct((rows, columns), BF16),
        compiler_params=pltpu.CompilerParams(vmem_limit_bytes=48 << 20),
        cost_estimate=CHEAP,
    )(where, a, *w_blocks)


def stacked_kernel(a_ref, w_ref, out_ref):
    out_ref[...] = stacked_dot(a_ref, w_ref).astype(out_ref.dtype)


def stacked_dot(a_ref, w_ref):
    blocks, groups, depth, columns = w_ref.shape
    step = blocks * depth
    total = None
    for d in range(groups):
        part = dot(a_ref[:, d * step : (d + 1) * step], w_ref[:, d].reshape(step, columns))
        total = part if total is None else total + part
    return total


def stacked_product(a, w, tile):
    rows, depth = a.shape
    columns = w.shape[3]
    return pl.pallas_call(
        stacked_kernel,
        grid=(columns // tile,),
        in_specs=[
            pl.BlockSpec((rows, depth), lambda j: (0, 0)),
            pl.BlockSpec(w.shape[:3] + (tile,), lambda j: (0, 0, 0, j)),
        ],
        out_specs=pl.BlockSpec((rows, tile), lambda j: (0, j)),
        out_shape=jax.ShapeDtypeStruct((rows, columns), F32),
        compiler_params=pltpu.CompilerParams(vmem_limit_bytes=56 << 20),
        cost_estimate=CHEAP,
    )(a, w)


def stacked_back_kernel(a_ref, w_ref, *out_refs):
    blocks, _, depth, columns = w_ref.shape
    out = dot(a_ref[...], w_ref[:, 0].reshape(blocks * depth, columns), 1, 1).astype(BF16)
    step = out_refs[0].shape[0]
    for k, out_ref in enumerate(out_refs):
        out_ref[...] = out[k * step : (k + 1) * step]


def stacked_back(a, w, pieces):
    rows, depth = a.shape
    blocks, groups, n, columns = w.shape
    step = blocks * n
    return pl.pallas_call(
        stacked_back_kernel,
        grid=(groups,),
        in_specs=[
            pl.BlockSpec((rows, depth), lambda j: (0, 0)),
            pl.BlockSpec((blocks, 1, n, columns), lambda j: (0, j, 0, 0)),
        ],
        out_specs=[pl.BlockSpec((rows // pieces, step), lambda j: (0, j))] * pieces,
        out_shape=[jax.ShapeDtypeStruct((rows // pieces, groups * step), BF16)] * pieces,
        compiler_params=pltpu.CompilerParams(vmem_limit_bytes=56 << 20),
        cost_estimate=CHEAP,
    )(a, w)


def term_kernel(a_ref, b_ref, out_ref):
    out_ref[...] = dot(a_ref[...], b_ref[...], 0, 0).astype(BF16).reshape(out_ref.shape)


def term_product(a, b, groups, blocks):
    rows, width = a.shape
    columns = b.shape[1]
    depth = width // (groups * blocks)
    return pl.pallas_call(
        term_kernel,
        grid=(groups,),
        in_specs=[
            pl.BlockSpec((rows, blocks * depth), lambda i: (0, i)),
            pl.BlockSpec((rows, columns), lambda i: (0, 0)),
        ],
        out_specs=pl.BlockSpec((blocks, 1, depth, columns), lambda i: (0, i, 0, 0)),
        out_shape=jax.ShapeDtypeStruct((blocks, groups, depth, columns), BF16),
        compiler_params=pltpu.CompilerParams(vmem_limit_bytes=56 << 20),
        cost_estimate=CHEAP,
    )(a, b).reshape(width, columns)


def pieces_kernel(me_ref, a_ref, b_ref, *refs):
    norm_ref, out_refs = (refs[0], refs[1:]) if refs[0].shape[0] == 8 else (None, refs)
    wide = b_ref.shape[1]
    part = dot(a_ref[...], b_ref[...], 0, 0).astype(BF16)
    for s, out_ref in enumerate(out_refs):

        @pl.when(pl.program_id(0) == s)
        def _():
            out_ref[:, :wide] = part
            if norm_ref is not None:
                sums = norm_ref[...].T
                rest = jnp.zeros((sums.shape[0], HEAD_DIMENSION - 8), F32)
                out_ref[:, wide:] = jnp.concatenate([sums, rest], axis=1).astype(BF16)


def term_pieces(a, b, me, count, norms=None):
    rows, width = a.shape
    columns = b.shape[1]
    step = width // count
    extra = 0 if norms is None else HEAD_DIMENSION
    in_specs = [
        pl.BlockSpec((rows, step), lambda i, me: (0, me[0] ^ i)),
        pl.BlockSpec((rows, columns), lambda i, me: (0, 0)),
    ]
    if norms is not None:
        in_specs.append(pl.BlockSpec((8, step), lambda i, me: (0, me[0] ^ i)))
    return pl.pallas_call(
        pieces_kernel,
        grid_spec=pltpu.PrefetchScalarGridSpec(
            num_scalar_prefetch=1,
            grid=(count,),
            in_specs=in_specs,
            out_specs=[pl.BlockSpec((step, columns + extra), lambda i, me: (0, 0))] * count,
        ),
        out_shape=[jax.ShapeDtypeStruct((step, columns + extra), BF16)] * count,
        compiler_params=pltpu.CompilerParams(vmem_limit_bytes=56 << 20),
        cost_estimate=CHEAP,
    )(me.reshape(1).astype(jnp.int32), a, b, *([] if norms is None else [norms]))


def input_kernel(grad_ref, weight_ref, normed_ref, other_ref, out_ref, sum_ref):
    part = dot(grad_ref[...], weight_ref[...], 1, 1)
    out_ref[...] = part.astype(BF16)
    sum_ref[...] = jnp.zeros_like(sum_ref)
    sum_ref[0:1] = jnp.sum(normed_ref[...].astype(F32) * part, axis=0, keepdims=True)
    sum_ref[1:2] = other_ref[...]


def input_product(grad, weight, normed, other, tile):
    rows, depth = grad.shape
    columns = weight.shape[0]
    return pl.pallas_call(
        input_kernel,
        grid=(columns // tile,),
        in_specs=[
            pl.BlockSpec((rows, depth), lambda j: (0, 0)),
            pl.BlockSpec((tile, depth), lambda j: (j, 0)),
            pl.BlockSpec((rows, tile), lambda j: (0, j)),
            pl.BlockSpec((1, tile), lambda j: (0, j)),
        ],
        out_specs=[pl.BlockSpec((rows, tile), lambda j: (0, j)), pl.BlockSpec((8, tile), lambda j: (0, j))],
        out_shape=[jax.ShapeDtypeStruct((rows, columns), BF16), jax.ShapeDtypeStruct((8, columns), F32)],
        compiler_params=pltpu.CompilerParams(vmem_limit_bytes=48 << 20),
        cost_estimate=CHEAP,
    )(grad, weight, normed, other)


def whole(kernel, shapes, me, *arrays, seen=()):
    vmem = pl.BlockSpec(memory_space=pltpu.VMEM)

    def body(me_ref, *refs):
        kernel(me_ref, *refs[: len(arrays)], *refs[len(arrays) + len(seen) :])

    return pl.pallas_call(
        body,
        in_specs=[pl.BlockSpec(memory_space=pltpu.SMEM)]
        + [vmem] * len(arrays)
        + [pl.BlockSpec(memory_space=pl.ANY)] * len(seen),
        out_specs=[vmem] * len(shapes),
        out_shape=shapes,
        compiler_params=pltpu.CompilerParams(vmem_limit_bytes=48 << 20),
        cost_estimate=CHEAP,
    )(me.reshape(1).astype(jnp.int32), *arrays, *seen)


def lanes(index, size):
    return pl.ds(pl.multiple_of(index * size, HEAD_DIMENSION), size)


def attn_split_kernel(heads, me_ref, gain_ref, q_ref, k_ref, v_ref, o_ref, *out_refs):
    pair = GROUP * HEAD_DIMENSION
    gain = gain_ref[...]

    def scaled(ref, index, size):
        return (ref[:, lanes(index, size)].astype(F32) * gain).astype(BF16)

    for s, out_ref in enumerate(out_refs):
        part = me_ref[0] ^ s
        for n in range(heads):
            head, at = part * heads + n, n * HEAD_SET
            out_ref[:, at : at + pair] = scaled(q_ref, head, pair)
            out_ref[:, at + pair : at + pair + HEAD_DIMENSION] = scaled(k_ref, head, HEAD_DIMENSION)
            out_ref[:, at + pair + HEAD_DIMENSION : at + HEAD_SET] = scaled(v_ref, head, HEAD_DIMENSION)
        out_ref[:, heads * HEAD_SET :] = o_ref[:, lanes(part, heads * pair)]


def attn_join_kernel(heads, me_ref, gain_ref, *refs):
    count = len(refs) - 5
    q_ref, k_ref, v_ref, o_ref, norm_ref = refs[count:]
    pair = GROUP * HEAD_DIMENSION
    gain = gain_ref[...]
    norms = jnp.zeros(norm_ref.shape, F32)
    for s, got_ref in enumerate(refs[:count]):
        part = me_ref[0] ^ s
        for n in range(heads):
            head, at = part * heads + n, n * HEAD_SET
            q_ref[:, lanes(head, pair)] = got_ref[:, at : at + pair].astype(F32) * gain
            k_ref[:, lanes(head, HEAD_DIMENSION)] = (
                got_ref[:, at + pair : at + pair + HEAD_DIMENSION].astype(F32) * gain
            )
            v_ref[:, lanes(head, HEAD_DIMENSION)] = (
                got_ref[:, at + pair + HEAD_DIMENSION : at + HEAD_SET].astype(F32) * gain
            )
        norms += got_ref[:, heads * HEAD_SET : heads * HEAD_SET + HEAD_DIMENSION].astype(F32)
        o_ref[:, lanes(part, heads * pair)] = got_ref[:, heads * HEAD_SET + HEAD_DIMENSION :].astype(F32)
    norm_ref[...] = norms


def ffn_split_kernel(tiles, me_ref, gain_ref, gate_ref, up_ref, down_ref, *out_refs):
    gain = gain_ref[...]
    hidden = out_refs[0].shape[1] // 3
    tile = hidden // tiles
    for s, out_ref in enumerate(out_refs):
        part = me_ref[0] ^ s
        for n in range(tiles):
            for k, ref in enumerate((gate_ref, up_ref)):
                at = (2 * n + k) * tile
                out_ref[:, at : at + tile] = (ref[:, lanes(part * tiles + n, tile)].astype(F32) * gain).astype(
                    BF16
                )
        out_ref[:, 2 * hidden :] = down_ref[:, lanes(part, hidden)]


def ffn_join_kernel(tiles, me_ref, gain_ref, *refs):
    count = (len(refs) - 3) // 2
    gate_ref, up_ref, down_ref = refs[2 * count :]
    gain = gain_ref[...]
    hidden = refs[0].shape[1] // 2
    tile = hidden // tiles
    for s, (got_ref, down_got_ref) in enumerate(zip(refs[:count], refs[count:])):
        part = me_ref[0] ^ s
        for n in range(tiles):
            for k, ref in enumerate((gate_ref, up_ref)):
                at = (2 * n + k) * tile
                ref[:, lanes(part * tiles + n, tile)] = got_ref[:, at : at + tile].astype(F32) * gain
        down_ref[:, lanes(part, hidden)] = down_got_ref[...].astype(F32)


def rows_join_kernel(me_ref, *refs):
    first_ref, second_ref = refs[-2:]
    depth = refs[0].shape[0]
    wide = first_ref.shape[1]
    for s, got_ref in enumerate(refs[:-2]):
        rows = pl.ds(pl.multiple_of((me_ref[0] ^ s) * depth, depth), depth)
        first_ref[rows] = got_ref[:, :wide]
        second_ref[rows] = got_ref[:, wide:]


def rows_join(got, wide, me):
    depth, width = got[0].shape
    return whole(
        rows_join_kernel,
        [jax.ShapeDtypeStruct((len(got) * depth, n), BF16) for n in (wide, width - wide)],
        me,
        *got,
    )


def rotate(x, cos, sin):
    return x * cos + pltpu.roll(x, HEAD_DIMENSION // 2, 1) * sin


def head_slice(i):
    return slice(i * HEAD_DIMENSION, (i + 1) * HEAD_DIMENSION)


def normed_rotated(raw, gain, cos, sin):
    return rotate(raw * norm_factor(raw) * gain, cos, sin).astype(BF16)


def probabilities(keys, queries, first_query, earliest):
    scores = dot(keys, queries, 1, 1)
    key_index = lax.broadcasted_iota(jnp.int32, scores.shape, 0)
    query_index = lax.broadcasted_iota(jnp.int32, scores.shape, 1) + first_query
    allowed = (key_index <= query_index) & (key_index >= earliest)
    masked = jnp.where(allowed, scores, -1e30)
    shifted = jnp.exp2((masked - jnp.max(masked, axis=0, keepdims=True)) * (score_scaling * 1.4426950408889634))
    return shifted * (1.0 / jnp.sum(shifted, axis=0, keepdims=True))


def forward_kernel(block, qkv_ref, gain_ref, cos_ref, sin_ref, early_ref, out_ref):
    length = qkv_ref.shape[0]
    gains = gain_ref[...]
    cos, sin = cos_ref[...], sin_ref[...]
    keys = normed_rotated(qkv_ref[:, head_slice(GROUP)], gains[1:2], cos, sin)
    values_t = qkv_ref[:, head_slice(GROUP + 1)].T.astype(BF16)
    for i in range(length // block):
        rows = slice(i * block, (i + 1) * block)
        seen = (i + 1) * block
        for g in range(GROUP):
            queries = normed_rotated(qkv_ref[rows, head_slice(g)], gains[0:1], cos[rows], sin[rows])
            probs = probabilities(keys[:seen], queries, i * block, early_ref[0:1, rows]).astype(BF16)
            mixed = dot(values_t[:, :seen], probs)
            out_ref[rows, head_slice(g)] = mixed.T.astype(BF16)


def backward_kernel(
    block, qkv_ref, dout_ref, gain_ref, cos_ref, sin_ref, early_ref, dqkv_ref, dgain_ref, dkey_ref, dvalue_ref
):
    length = qkv_ref.shape[0]
    gains = gain_ref[...]
    cos, sin = cos_ref[...], sin_ref[...]
    key_raw = qkv_ref[:, head_slice(GROUP)]
    keys = normed_rotated(key_raw, gains[1:2], cos, sin)
    keys_t = keys.astype(F32).T.astype(BF16)
    values = qkv_ref[:, head_slice(GROUP + 1)].astype(BF16)
    dkey_ref[...] = jnp.zeros_like(dkey_ref)
    dvalue_ref[...] = jnp.zeros_like(dvalue_ref)
    query_gain_sum = jnp.zeros((1, HEAD_DIMENSION), F32)
    for i in range(length // block):
        rows = slice(i * block, (i + 1) * block)
        seen = (i + 1) * block
        for g in range(GROUP):
            query_raw = qkv_ref[rows, head_slice(g)]
            queries = normed_rotated(query_raw, gains[0:1], cos[rows], sin[rows])
            dout = dout_ref[rows, head_slice(g)]
            probs = probabilities(keys[:seen], queries, i * block, early_ref[0:1, rows])
            dprobs = dot(values[:seen], dout, 1, 1)
            delta = jnp.sum(probs * dprobs, axis=0, keepdims=True)
            dscores = (probs * (dprobs - delta)).astype(BF16)
            dkey_ref[:seen] += dot(dscores, queries)
            dvalue_ref[:seen] += dot(probs.astype(BF16), dout)
            dquery = dot(keys_t[:, :seen], dscores).T * score_scaling
            dquery = rotate(dquery, cos[rows], -sin[rows])
            factor = norm_factor(query_raw)
            query_gain_sum += jnp.sum(query_raw * factor * dquery, axis=0, keepdims=True)
            dqkv_ref[rows, head_slice(g)] = norm_back(query_raw, factor, dquery * gains[0:1]).astype(BF16)
    dkey = rotate(dkey_ref[...] * score_scaling, cos, -sin)
    factor = norm_factor(key_raw)
    dgain_ref[0, 0:1, :] = query_gain_sum
    dgain_ref[0, 1:2, :] = jnp.sum(key_raw * factor * dkey, axis=0, keepdims=True)
    dgain_ref[0, 2:, :] = jnp.zeros((6, HEAD_DIMENSION), F32)
    dqkv_ref[:, head_slice(GROUP)] = norm_back(key_raw, factor, dkey * gains[1:2]).astype(BF16)
    dqkv_ref[:, head_slice(GROUP + 1)] = dvalue_ref[...].astype(BF16)


def per_head_specs(length):
    whole = lambda shape: pl.BlockSpec(shape, lambda n: (0,) * len(shape))
    return [
        whole((2, HEAD_DIMENSION)),
        whole((length, HEAD_DIMENSION)),
        whole((length, HEAD_DIMENSION)),
        whole((8, length)),
    ]


def columns_spec(length, width):
    return pl.BlockSpec((length, width), lambda n: (0, n))


def attention_forward(qkv, gains, cos, sin, earliest):
    length, width = qkv.shape
    heads = width // HEAD_SET
    return pl.pallas_call(
        functools.partial(forward_kernel, 256),
        grid=(heads,),
        in_specs=[columns_spec(length, HEAD_SET)] + per_head_specs(length),
        out_specs=columns_spec(length, GROUP * HEAD_DIMENSION),
        out_shape=jax.ShapeDtypeStruct((length, heads * GROUP * HEAD_DIMENSION), BF16),
        compiler_params=pltpu.CompilerParams(vmem_limit_bytes=48 << 20),
        cost_estimate=CHEAP,
    )(qkv, gains, cos, sin, earliest)


def attention_backward(qkv, dout, gains, cos, sin, earliest):
    length, width = qkv.shape
    heads = width // HEAD_SET
    return pl.pallas_call(
        functools.partial(backward_kernel, 256),
        grid=(heads,),
        in_specs=[columns_spec(length, HEAD_SET), columns_spec(length, GROUP * HEAD_DIMENSION)]
        + per_head_specs(length),
        out_specs=[
            columns_spec(length, HEAD_SET),
            pl.BlockSpec((1, 8, HEAD_DIMENSION), lambda n: (n, 0, 0)),
        ],
        out_shape=[
            jax.ShapeDtypeStruct((length, width), BF16),
            jax.ShapeDtypeStruct((heads, 8, HEAD_DIMENSION), F32),
        ],
        scratch_shapes=[pltpu.VMEM((length, HEAD_DIMENSION), F32)] * 2,
        compiler_params=pltpu.CompilerParams(vmem_limit_bytes=48 << 20),
        cost_estimate=CHEAP,
    )(qkv, dout, gains, cos, sin, earliest)


def hidden_kernel(pre_ref, grad_ref, down_ref, hidden_ref, dpre_ref):
    tile = hidden_ref.shape[1]
    grad_hidden = stacked_dot(grad_ref, down_ref)
    step = 128
    for start in range(0, hidden_ref.shape[0], step):
        rows = slice(start, start + step)
        gate, up, grad = pre_ref[rows, :tile], pre_ref[rows, tile:], grad_hidden[rows]
        sig = 1.0 / (1.0 + jnp.exp(-gate))
        act = gate * sig
        hidden_ref[rows] = (act * up).astype(BF16)
        dpre_ref[rows, :tile] = (grad * up * sig * (1.0 + gate * (1.0 - sig))).astype(BF16)
        dpre_ref[rows, tile:] = (grad * act).astype(BF16)


def hidden_layer(pre, grad, down, tiles):
    rows, width = grad.shape
    tile = down.shape[3] // tiles
    step = min(rows, 1024)
    return pl.pallas_call(
        hidden_kernel,
        grid=(tiles, rows // step),
        in_specs=[
            pl.BlockSpec((step, 2 * tile), lambda j, i: (i, j)),
            pl.BlockSpec((step, width), lambda j, i: (i, 0)),
            pl.BlockSpec(down.shape[:3] + (tile,), lambda j, i: (0, 0, 0, j)),
        ],
        out_specs=[
            pl.BlockSpec((step, tile), lambda j, i: (i, j)),
            pl.BlockSpec((step, 2 * tile), lambda j, i: (i, j)),
        ],
        out_shape=[
            jax.ShapeDtypeStruct((rows, tile * tiles), BF16),
            jax.ShapeDtypeStruct((rows, 2 * tile * tiles), BF16),
        ],
        compiler_params=pltpu.CompilerParams(vmem_limit_bytes=56 << 20),
        cost_estimate=CHEAP,
    )(pre, grad, down)


def tie(*items):
    return lax.optimization_barrier(items)


def swap(x, axis, bit):
    return lax.ppermute(x, axis, [(i, i ^ bit) for i in range(lax.axis_size(axis))])


def own_and_other(blocks):
    half = lax.axis_index("h")
    return [lax.dynamic_index_in_dim(blocks, k, 0, keepdims=True) for k in (half, 1 - half)]


def sequence_steps(own, give, together):
    half, part, parts = lax.axis_index("h"), lax.axis_index("t"), lax.axis_size("t")
    block = own.shape[1]
    got = swap(give, "h", 1)
    if not together:
        own_first, got = tie(swap(own, "t", parts // 2), got)
    got = yield got
    if together:
        starts = [(jnp.concatenate([own, got], axis=0), [0, parts])]
    else:
        starts = [(own, [0]), (got, [parts])]
    placed = []
    for first, keys in starts:
        held = [first]
        bit = parts // 2
        while bit:
            if together:
                for piece in list(held):
                    got = yield swap(piece, "t", bit)
                    held.append(got)
            else:
                if first is own and len(held) == 1:
                    got = yield own_first
                else:
                    got = yield swap(jnp.concatenate(held, axis=0) if len(held) > 1 else first, "t", bit)
                held.append(got)
            keys = keys + [k | bit for k in keys]
            bit //= 2
        flat = [piece[i] for piece in held for i in range(piece.shape[0])]
        placed += [(b, ((half * parts + part) ^ k) * block) for b, k in zip(flat, keys)]
    return placed


def run_steps(steps, ties):
    number, arrived = 0, next(steps)
    while True:
        try:
            arrived = steps.send(ties[number](arrived) if number in ties else arrived)
        except StopIteration as end:
            return end.value
        number += 1


def assemble(placed, columns=slice(None), out=None):
    rows = sum(part.shape[0] for part, _ in placed)
    if out is None:
        out = blank((rows, placed[0][0][:, columns].shape[1]), placed[0][0].dtype)
    for part, start in placed:
        out = lax.dynamic_update_slice_in_dim(out, part[:, columns], start, 0)
    return out


def to_blocks(partial, late=(), on_first=None, on_last=None):
    half, part, parts = lax.axis_index("h"), lax.axis_index("t"), lax.axis_size("t")
    both = partial.reshape(2, parts, -1, partial.shape[1])
    held = [lax.dynamic_index_in_dim(both, part ^ key, 1, keepdims=False) for key in range(parts)]

    def pick(x, h):
        return lax.dynamic_index_in_dim(x, h, 0, keepdims=False)

    bit = 1
    while 2 * bit < parts:
        keys = [key for key in range(parts) if held[key] is not None and key & bit]
        got = swap(jnp.stack([held[key].astype(BF16) for key in keys]), "t", bit)
        for n, key in enumerate(keys):
            held[key ^ bit] = held[key ^ bit].astype(F32) + got[n].astype(F32)
            held[key] = None
        bit *= 2
    first = swap(pick(held[bit], 1 - half).astype(BF16), "t", bit)
    if on_first is not None:
        first = on_first(first)
    far = pick(held[0], 1 - half).astype(F32) + first.astype(F32)
    far, near = tie(far.astype(BF16), pick(held[bit], half).astype(BF16))
    got = swap(far, "h", 1)
    second = swap(near, "t", bit)
    if on_last is not None:
        got, second = on_last(got, second)
    own = pick(held[0], half).astype(F32) + second.astype(F32)
    got, own, late = tie(got.astype(F32), own, list(late))
    return jnp.where(half == 0, jnp.stack([own, got]), jnp.stack([got, own])), late


def swaps(pieces, axis="dp"):
    return [pieces[0]] + list(reversed([swap(pieces[s], axis, s) for s in reversed(range(1, len(pieces)))]))


def gather_h(x):
    return [x, swap(x, "h", 1)]


def block_places():
    dp, half, count = lax.axis_index("dp"), lax.axis_index("h"), lax.axis_size("dp")
    return jnp.stack([(dp ^ s) * 2 + (half ^ k) for k in (0, 1) for s in range(count)]).astype(jnp.int32)


def blank(shape, dtype):
    return pl.pallas_call(
        lambda out_ref: None,
        out_specs=pl.BlockSpec(memory_space=pl.ANY),
        out_shape=jax.ShapeDtypeStruct(shape, dtype),
    )()


def place_rows(blocks, places):
    rows, width = blocks[0].shape
    out = blank((len(blocks) * rows, width), blocks[0].dtype)
    for k, part in enumerate(blocks):
        out = lax.dynamic_update_slice_in_dim(out, part, places[k] * rows, 0)
    return out


def sum_h(got):
    half = lax.axis_index("h")
    total = sum(g.astype(F32) for g in got)
    total = total.reshape(2, total.shape[0] // 2, -1)
    give = lax.dynamic_index_in_dim(total, 1 - half, 0, keepdims=False).astype(BF16)
    return lax.dynamic_index_in_dim(total, half, 0, keepdims=False), give


def total_over(x, axis):
    bit = 1
    while bit < lax.axis_size(axis):
        x = x + swap(x, axis, bit)
        bit *= 2
    return x


def per_device(
    tokens,
    positions,
    attn_norm,
    query_proj,
    key_projected,
    value_projected,
    head_norms,
    out_proj,
    mlp_norm,
    gate_proj,
    up_proj,
    down_proj,
    out_grad,
):
    block, seqs, width = tokens.shape
    rows = block * seqs
    dp = lax.axis_size("dp")
    parts = lax.axis_size("t")
    ctx = 2 * parts
    length = block * ctx
    depth = query_proj.shape[0]
    part = lax.axis_index("t")
    attn_gain = attn_norm.astype(F32)[:, None]
    mlp_gain = mlp_norm.astype(F32)[:, None]

    inputs = jnp.transpose(tokens, (1, 0, 2)).astype(F32)
    factor_one = norm_factor(inputs)
    digits = jnp.stack([positions.T // 16, positions.T % 16], axis=2).astype(BF16)
    digits = jnp.pad(digits, ((0, 0), (0, 0), (0, HEAD_DIMENSION - 2)))
    own_one = jnp.concatenate([(inputs * factor_one).astype(BF16), digits], axis=2)
    own_one, query_proj, gate_proj = tie(own_and_other(own_one), query_proj, gate_proj)

    heads = KEY_VALUE_HEADS // parts
    pair = GROUP * HEAD_DIMENSION
    qkv_width, mix_width = heads * HEAD_SET, heads * pair
    attn_width = qkv_width + mix_width

    dp_index = lax.axis_index("dp")
    attn_set = whole(
        functools.partial(attn_split_kernel, heads),
        [jax.ShapeDtypeStruct((depth, attn_width), BF16)] * parts,
        part,
        attn_gain,
        query_proj,
        key_projected,
        value_projected,
        out_proj,
    )
    attn_set, gate_proj = tie(attn_set, gate_proj)

    hidden = gate_proj.shape[1] // dp
    tiles = 3
    ffn_set = whole(
        functools.partial(ffn_split_kernel, tiles),
        [jax.ShapeDtypeStruct((depth, 3 * hidden), BF16)] * dp,
        dp_index,
        mlp_gain,
        gate_proj,
        up_proj,
        down_proj,
    )

    def swap_h(x):
        return swap(x, "h", 1)

    def swap_dp(x, keys):
        return [swap(x[k] if isinstance(x, (list, tuple)) else x, "dp", k) for k in keys]

    near, far = range(1, dp - 1), range(dp - 1, dp)
    bits = parts.bit_length() - 1
    hold = {}

    def first_step(x):
        x, got, ffn_near = tie(x, swaps(attn_set, "t"), swap_dp(ffn_set, near))
        qkv_rows, out_rows = rows_join(got, qkv_width, part)
        hold.update(qkv=qkv_rows, out=out_rows, ffn_near=ffn_near)
        return x

    def second_step(x):
        x, qkv_h, ffn_far, qkv_got, out_h = tie(
            x,
            swap_h(hold["qkv"]),
            swap_dp(ffn_set, far),
            swap_dp(hold["qkv"], range(1, dp)),
            swap_h(hold["out"]),
        )
        hold.update(qkv_h=qkv_h, ffn_far=ffn_far, qkv_got=qkv_got, out_h=out_h)
        return x

    def third_step(x):
        x, hold["qkv_h_got"] = tie(x, swap_dp(hold["qkv_h"], range(1, dp)))
        return x

    placed = run_steps(sequence_steps(*own_one, True), {0: first_step, 1: second_step, parts - 1: third_step})
    normed_one = assemble(placed, slice(0, width))
    places = assemble(placed, slice(width, width + HEAD_DIMENSION))[:, :2].astype(jnp.int32)
    places = places[:, 0] * 16 + places[:, 1]
    normed_one, out_rows = tie(normed_one, hold["out"])
    qkv_blocks = [hold["qkv"], *hold["qkv_got"], hold["qkv_h"], *hold["qkv_h_got"]]
    block_at = block_places()
    ffn_got = [ffn_set[0], *hold["ffn_near"], *hold["ffn_far"]]
    pre_rows, down_rows = rows_join(ffn_got, 2 * hidden, dp_index)

    def ffn_gather(x):
        return lax.all_gather(x, ("h", "t"), axis=0, tiled=False).reshape(ctx, dp, depth, -1)

    pre_weight = ffn_gather(pre_rows)

    def ffn_scatter(term):
        return lax.psum_scatter(term, ("h", "t"), scatter_dimension=0, tiled=True).reshape(dp, depth, -1)

    gains = head_norms.astype(F32)
    half_width = HEAD_DIMENSION // 2
    frequency = theta_base ** (-(jnp.arange(half_width, dtype=F32) * 2.0 / HEAD_DIMENSION))
    angles = places.astype(F32)[:, None] * frequency
    cos, sin = jnp.cos(angles), jnp.sin(angles)
    cos = jnp.concatenate([cos, cos], axis=1)
    sin = jnp.concatenate([-sin, sin], axis=1)
    earliest = jnp.broadcast_to((jnp.arange(length, dtype=jnp.int32) - places)[None, :], (8, length))
    out_pair = jnp.concatenate([out_rows, hold["out_h"]], axis=0)
    qkv = blocks_product(normed_one, qkv_blocks, block_at, 256)
    qkv, qkv_blocks, out_near, out_grad = tie(qkv, qkv_blocks, swap_dp(out_pair, near), out_grad)
    grad_own = jnp.transpose(out_grad, (1, 0, 2)).reshape(rows, width)
    mixed = attention_forward(qkv, gains, cos, sin, earliest)
    mixed, out_far = tie(mixed, swap_dp(out_pair, far))
    out_pairs = [out_pair, *out_near, *out_far]
    out_blocks = [p[: parts * depth] for p in out_pairs] + [p[parts * depth :] for p in out_pairs]
    mixed_part = blocks_back(mixed, out_blocks, block_at, 2)
    mixed_part, out_blocks, qkv_blocks, early = tie(
        mixed_part, out_blocks, qkv_blocks, swap_dp(grad_own, range(1, 2))
    )
    def weights_step(first):
        first, qkv_parts, out_parts = tie(first, qkv_blocks, out_blocks)
        hold["qkv_weight"] = place_rows(qkv_parts, block_at)
        hold["out_weight"] = place_rows(out_parts, block_at)
        return first

    def weights_done(got, second):
        got, hold["qkv_weight"], hold["out_weight"] = tie(got, hold["qkv_weight"], hold["out_weight"])
        return got, second

    mixed_sum, (late, pre_weight, down_rows) = to_blocks(
        mixed_part, [swap_dp(grad_own, range(2, dp)), pre_weight, down_rows], weights_step, weights_done
    )
    qkv_weight, out_weight = hold["qkv_weight"], hold["out_weight"]
    middle = (inputs + mixed_sum).reshape(rows, width)
    down_weight = ffn_gather(down_rows)

    factor_two = norm_factor(middle)
    own_two = (middle * factor_two).astype(BF16)
    normed_two = swaps([own_two] * dp)
    grad_rows = jnp.concatenate([grad_own, *early, *late], axis=0)
    normed_two = jnp.concatenate(normed_two, axis=0)
    pre = stacked_product(normed_two, pre_weight, hidden // 2)
    hidden_low, grad_pre = hidden_layer(pre, grad_rows, down_weight, tiles)
    down_term = term_product(grad_rows, hidden_low, dp, ctx)
    down_term, grad_pre = tie(down_term, grad_pre)
    down_sum = ffn_scatter(down_term)
    two_part = stacked_back(grad_pre, pre_weight, dp)
    grad_pre, two_part = tie(grad_pre, two_part)
    two_got = swaps(two_part)
    pre_term = term_product(normed_two, grad_pre, dp, ctx)
    branch_part = stacked_back(hidden_low, down_weight, dp)
    pre_term, branch_part, two_got = tie(pre_term, branch_part, two_got)
    grad_two = sum(g.astype(F32) for g in two_got)
    grad_middle = grad_own.astype(F32) + norm_back(middle, factor_two, grad_two)
    grad_mid_own = grad_middle.astype(BF16).reshape(seqs, block, width)
    grad_mid_own, grad_two = tie(grad_mid_own, grad_two)
    mlp_norm_sum = jnp.sum(middle * factor_two * grad_two, axis=0)

    def to_dp(x):
        return [lax.dynamic_index_in_dim(x, dp_index ^ k, 0, keepdims=False) for k in range(dp)]

    def near_step(x):
        x, hold["branch_near"] = tie(x, swap_dp(branch_part, near))
        return x

    def last_step(x):
        x, hold["mlp_sum"] = tie(x, mlp_norm_sum)
        return x

    placed = run_steps(
        sequence_steps(*own_and_other(grad_mid_own), False), {bits + 1: near_step, 2 * bits: last_step}
    )
    mlp_norm_sum = hold["mlp_sum"]
    grad_mid = assemble(placed, slice(None), normed_two)
    if PRE_LATE:
        grad_mid, pre_term = tie(grad_mid, pre_term)
    pre_sum = ffn_scatter(pre_term)
    grad_mixed = rows_product(grad_mid, out_weight, 0, 256, BF16)
    out_pieces = term_pieces(grad_mid, mixed, dp_index, dp)
    grad_mixed, out_pieces = tie(grad_mixed, out_pieces)
    grad_qkv, gain_terms = attention_backward(qkv, grad_mixed, gains, cos, sin, earliest)
    grad_qkv, hold["branch_far"] = tie(grad_qkv, swap_dp(branch_part, far))
    hops = [
        (axis, 1 << k) for axis in ("dp", "t", "h") for k in range(lax.axis_size(axis).bit_length() - 1)
    ]
    hold["head"] = jnp.sum(gain_terms, axis=0)[:2]

    def hop():
        axis, bit = hops.pop(0)
        return swap(hold["head"], axis, bit)

    grad_one_part, norm_sums = input_product(grad_qkv, qkv_weight, normed_one, mlp_norm_sum[None], 512)
    grad_qkv, grad_one_part, out_got, down_give, head = tie(
        grad_qkv, grad_one_part, swap_dp(out_pieces, range(1, dp)), to_dp(down_sum), hop()
    )
    hold["head"] += head
    out_keep, out_give = sum_h([out_pieces[0], *out_got])

    qkv_pieces = term_pieces(normed_one, grad_qkv, dp_index, dp, norm_sums)
    qkv_pieces, grad_one_part, down_got, head = tie(qkv_pieces, grad_one_part, swaps(down_give), hop())
    hold["head"] += head
    qkv_got = swaps(qkv_pieces)
    branch_got = [branch_part[0], *hold["branch_near"], *hold["branch_far"]]
    seen = []

    def gradients_step(first):
        arrived = first
        got, first, out_h, head, hold["branch"] = tie(qkv_got, first, swap_h(out_give), hop(), branch_got)
        hold["head"] += head
        seen.append(first)
        hold["out_h_got"] = out_h
        hold["qkv_keep"], hold["qkv_give"] = sum_h(got)
        return arrived

    def last_swap_step(got, second):
        got, head, second, pre_give = tie(got, hop(), second, to_dp(pre_sum))
        qkv_h_got, pre_near = tie(swap_h(hold["qkv_give"]), swap_dp(pre_give, near))
        hold["head"] += head
        attn_sum = hold["qkv_keep"] + qkv_h_got.astype(F32)
        out_sum = out_keep + hold["out_h_got"].astype(F32)
        attn_sum = jnp.concatenate([attn_sum, out_sum], axis=1).astype(BF16)
        attn_got = swaps(
            [lax.dynamic_slice_in_dim(attn_sum, (part ^ k) * depth, depth, 0) for k in range(parts)], "t"
        )
        while len(hops) > 1:
            hold["head"] += hop()
        hold["pre_got"] = [pre_give[0], *pre_near, *swap_dp(pre_give, far)]
        got, hold["attn_got"], head = tie(got, attn_got, hop())
        hold["head"] += head
        return got, second

    grad_one, _ = to_blocks(grad_one_part, [], gradients_step, last_swap_step)
    attn_grad, pre_grad = hold["attn_got"], hold["pre_got"]
    head_norm_grad = hold["head"]
    layer_out = (middle + sum(g.astype(F32) for g in hold["branch"])).astype(BF16)
    input_grad = grad_middle.reshape(seqs, block, width) + norm_back(inputs, factor_one, grad_one)
    layer_out = jnp.transpose(layer_out.reshape(seqs, block, width), (1, 0, 2))
    input_grad = jnp.transpose(input_grad, (1, 0, 2))
    pre_grad, input_grad, layer_out = tie(pre_grad, input_grad, layer_out)
    gate_grad, up_grad, down_grad = whole(
        functools.partial(ffn_join_kernel, tiles),
        [jax.ShapeDtypeStruct(gate_proj.shape, F32)] * 3,
        dp_index,
        mlp_gain,
        *pre_grad,
        *down_got,
    )
    query_grad, key_grad, value_grad, out_proj_grad, norm_grads = whole(
        functools.partial(attn_join_kernel, heads),
        [
            jax.ShapeDtypeStruct(x.shape, F32)
            for x in (query_proj, key_projected, value_projected, out_proj, jnp.zeros((depth, HEAD_DIMENSION)))
        ],
        part,
        attn_gain,
        *attn_grad,
        seen=seen,
    )
    attn_norm_grad = norm_grads[:, 0] / attn_gain[:, 0]
    mlp_norm_grad = norm_grads[:, 1] / mlp_gain[:, 0]

    return (
        layer_out,
        input_grad,
        attn_norm_grad,
        query_grad,
        key_grad,
        value_grad,
        head_norm_grad,
        out_proj_grad,
        mlp_norm_grad,
        gate_grad,
        up_grad,
        down_grad,
    )


def solution(mesh):
    dp, ctx = mesh.shape["dp"], mesh.shape["ctx"]
    fine = Mesh(mesh.devices.reshape(dp, 2, ctx // 2), ("dp", "h", "t"))
    acts = P(("h", "t"), "dp", None)
    rows = P(("dp", "h", "t"), None)
    gain = P(("dp", "h", "t"))
    in_specs = (
        acts,
        P(("h", "t"), "dp"),
        gain,
        rows,
        rows,
        rows,
        P(),
        rows,
        gain,
        rows,
        rows,
        rows,
        acts,
    )
    out_specs = (acts, acts, gain, rows, rows, rows, P(), rows, gain, rows, rows, rows)
    return jax.shard_map(per_device, mesh=fine, in_specs=in_specs, out_specs=out_specs, check_vma=False)
```
